128 devices in a mesh: row: 16 (over z_hi, y, core), col: 8 (over z_lo, x).
Axes of the slice: x: 4, y: 4, z: 4 (z_hi: 2, z_lo: 2; z = z_hi * 2 + z_lo), core: 2. Of those that a mesh axis runs over, the one named last changes fastest.
Arguments:
- pair_rep: bfloat16 [320, 320, 128], P('row', 'col'), may hold values from -6 to 6
- proj_weight: bfloat16 [2, 128, 512], replicated, may hold values from -0.5 to 0.5
- gate_weight: bfloat16 [2, 128, 128], replicated, may hold values from -0.5 to 0.5
- out_weight: bfloat16 [2, 128, 128], replicated, may hold values from -0.5 to 0.5
- pair_cot: bfloat16 [320, 320, 128], P('row', 'col'), may hold values from -6 to 6
Outputs:
- pair_out: bfloat16 [320, 320, 128], P('row', 'col')
- pair_grad: float32 [320, 320, 128], P('row', 'col')
- proj_grad: float32 [2, 128, 512], replicated
- gate_grad: float32 [2, 128, 128], replicated
- out_grad: float32 [2, 128, 128], replicated
The draws below stay inside these ranges and needn't reach their ends.
All inputs are finite; a program needn't handle non-finite values.
Results may differ from the reference program's by a relative error of at most 0.034.
Values may be sent and summed in bfloat16 or wider, within the bound.
No kernel may reach another device: no remote copies, remote signals or barrier semaphores. Data moves between devices by JAX's collectives and lax.ppermute only.
A program may use at most 128 MiB of HBM per device.

```python
import jax
import jax.numpy as jnp
from jax import lax

C = 128
H = 128
N = 320


def steps_of(key, dims, shards, smallest, largest):
    factor_of, own = 1.0, jax.random.fold_in(key, 6)
    for position, parts in shards:
        heights = jnp.exp(jax.random.uniform(jax.random.fold_in(own, position), (parts,), jnp.float32, smallest / len(shards), largest / len(shards)))
        factor_of = factor_of * jnp.repeat(heights, dims[position] // parts).reshape([-1 if axis == position else 1 for axis in range(len(dims))])
    return factor_of


def bell_draw(rng, dims, deviation, reach, shards=(), kind=jnp.bfloat16):
    values = deviation * jax.random.normal(rng, dims, jnp.float32)
    if shards:
        values = values * steps_of(rng, dims, shards, -0.22, 0.18)
    return jnp.clip(values, -reach, reach).astype(kind)


def setup_inputs(seed: int = 0) -> dict:
    streams_of = jax.random.split(jax.random.key(seed), 6)
    return {
        "pair_rep": bell_draw(streams_of[0], (N, N, C), 1.0, 6.0, ((0, 16), (1, 8))),
        "proj_weight": bell_draw(streams_of[1], (2, C, 4 * H), C ** -0.5, 0.5),
        "gate_weight": bell_draw(streams_of[2], (2, C, C), C ** -0.5, 0.5),
        "out_weight": bell_draw(streams_of[3], (2, H, C), H ** -0.5, 0.5),
        "pair_cot": bell_draw(streams_of[4], (N, N, C), 1.0, 6.0, ((0, 16), (1, 8))),
    }


EPSILON = 1e-05

def layer_norm(values):
    centered = values - lax.optimization_barrier(jnp.mean(values, axis=-1, keepdims=True))
    inverse = lax.rsqrt(lax.optimization_barrier(jnp.mean(centered * centered, axis=-1, keepdims=True)) + EPSILON)
    return centered * inverse

def norm_back(values, upstream):
    centered = values - lax.optimization_barrier(jnp.mean(values, axis=-1, keepdims=True))
    inverse = lax.rsqrt(lax.optimization_barrier(jnp.mean(centered * centered, axis=-1, keepdims=True)) + EPSILON)
    normed = centered * inverse
    mean_up = lax.optimization_barrier(jnp.mean(upstream, axis=-1, keepdims=True))
    mean_cross = lax.optimization_barrier(jnp.mean(upstream * normed, axis=-1, keepdims=True))
    return inverse * (upstream - mean_up - normed * mean_cross)

def as_float(tensor):
    return tensor.astype(jnp.float32)

def contract(pattern, first_op, second_op):
    return jnp.einsum(pattern, as_float(first_op), as_float(second_op))

def project(pair_rep, proj_mat, gate_mat):
    pair_full = pair_rep.astype(jnp.float32)
    normed = layer_norm(pair_full).astype(jnp.bfloat16)
    projected = contract('ijc,ch->ijh', normed, proj_mat)
    hidden = proj_mat.shape[1] // 4
    left_side = (jax.nn.sigmoid(projected[..., :hidden]) * projected[..., hidden:2 * hidden]).astype(jnp.bfloat16)
    right_side = (jax.nn.sigmoid(projected[..., 2 * hidden:3 * hidden]) * projected[..., 3 * hidden:]).astype(jnp.bfloat16)
    gating = jax.nn.sigmoid(contract('ijc,cd->ijd', normed, gate_mat))
    return (pair_full, normed, projected, left_side, right_side, gating)

def finish(pair_full, mix_value, out_mat, gating):
    normed_mix = layer_norm(mix_value).astype(jnp.bfloat16)
    product = contract('ijh,hc->ijc', normed_mix, out_mat)
    return ((pair_full + gating * product).astype(jnp.bfloat16), normed_mix, product)

def back_head(upstream, gating, product, normed_mix, mix_value, out_mat):
    through = (upstream * gating).astype(jnp.bfloat16)
    gate_pre = upstream * product * gating * (1.0 - gating)
    mix_up = contract('ijc,hc->ijh', through, out_mat)
    out_part = contract('ijh,ijc->hc', normed_mix, through)
    mix_grad = norm_back(mix_value, mix_up).astype(jnp.bfloat16)
    return (mix_grad, out_part, gate_pre)

def back_tail(upstream, pair_full, normed, projected, left_grad, right_grad, gate_pre, proj_mat, gate_mat):
    hidden = proj_mat.shape[1] // 4
    left_gate = jax.nn.sigmoid(projected[..., :hidden])
    left_value = projected[..., hidden:2 * hidden]
    right_gate = jax.nn.sigmoid(projected[..., 2 * hidden:3 * hidden])
    right_value = projected[..., 3 * hidden:]
    proj_up = jnp.concatenate([left_grad * left_value * left_gate * (1.0 - left_gate), left_grad * left_gate, right_grad * right_value * right_gate * (1.0 - right_gate), right_grad * right_gate], axis=-1).astype(jnp.bfloat16)
    gate_up = gate_pre.astype(jnp.bfloat16)
    normed_up = contract('ijh,ch->ijc', proj_up, proj_mat) + contract('ijd,cd->ijc', gate_up, gate_mat)
    proj_part = contract('ijc,ijh->ch', normed, proj_up)
    gate_part = contract('ijc,ijd->cd', normed, gate_up)
    return (upstream + norm_back(pair_full, normed_up), proj_part, gate_part)

def reference(pair_rep, proj_weight, gate_weight, out_weight, pair_cot):
    pair_full, normed, projected, left_side, right_side, gating = project(pair_rep, proj_weight[0], gate_weight[0])
    mix_out = contract('ikc,jkc->ijc', left_side, right_side)
    after_out, normed_mix, product = finish(pair_full, mix_out, out_weight[0], gating)
    pair_mid, normed_in, proj_in, left_in, right_in, gating_in = project(after_out, proj_weight[1], gate_weight[1])
    mix_in = contract('kic,kjc->ijc', left_in, right_in)
    pair_out, normed_mix_in, product_in = finish(pair_mid, mix_in, out_weight[1], gating_in)
    upstream = pair_cot.astype(jnp.float32)
    grad_in, out_part_in, gate_pre_in = back_head(upstream, gating_in, product_in, normed_mix_in, mix_in, out_weight[1])
    right_grad_in = contract('kic,ijc->kjc', left_in, grad_in)
    left_grad_in = contract('kjc,ijc->kic', right_in, grad_in)
    upstream_mid, proj_part_in, gate_part_in = back_tail(upstream, pair_mid, normed_in, proj_in, left_grad_in, right_grad_in, gate_pre_in, proj_weight[1], gate_weight[1])
    grad_out, out_part_out, gate_pre_out = back_head(upstream_mid, gating, product, normed_mix, mix_out, out_weight[0])
    left_grad_out = contract('ijc,jkc->ikc', grad_out, right_side)
    right_grad_out = contract('ijc,ikc->jkc', grad_out, left_side)
    pair_grad, proj_part_out, gate_part_out = back_tail(upstream_mid, pair_full, normed, projected, left_grad_out, right_grad_out, gate_pre_out, proj_weight[0], gate_weight[0])
    inverse_size = 1.0 / N
    proj_grad = jnp.stack([proj_part_out, proj_part_in]) * inverse_size
    gate_grad = jnp.stack([gate_part_out, gate_part_in]) * inverse_size
    out_grad = jnp.stack([out_part_out, out_part_in]) * inverse_size
    return (pair_out, pair_grad, proj_grad, gate_grad, out_grad)
```

```python
import functools

import jax
import jax.numpy as jnp
from jax import lax
from jax.experimental import pallas as pl
from jax.experimental.pallas import tpu as pltpu
from jax.sharding import PartitionSpec as P

EPSILON = 1e-05
F32 = jnp.float32
BF16 = jnp.bfloat16
AXES = ("row", "col")

PARTS_R, PARTS_C = 16, 8
ROWS, COLS, CHANNELS = 20, 40, 128
PER = 3
TILES = 7
SUBS = 8
LANES = 128
SIZE = 320
WIDE = 384


def dot(first_op, second_op, first_dim, second_dim):
    return lax.dot_general(
        first_op,
        second_op,
        (((first_dim,), (second_dim,)), ((), ())),
        preferred_element_type=F32,
    )


def mean0(values):
    return jnp.sum(values, axis=0, keepdims=True) * (1.0 / CHANNELS)


def norm_parts(values):
    centered = values - mean0(values)
    inverse = lax.rsqrt(mean0(centered * centered) + EPSILON)
    return centered * inverse, inverse


def norm_back(normed, inverse, upstream):
    return inverse * (upstream - mean0(upstream) - normed * mean0(upstream * normed))


def block_in(ref):
    values = ref[...].astype(F32)
    tiles = []
    for s in range(TILES):
        low = s * PER * COLS
        high = min(low + PER * COLS, ROWS * COLS)
        piece = values[low:high]
        piece = jnp.concatenate([piece, jnp.zeros((LANES - (high - low), CHANNELS), F32)], axis=0)
        tiles.append(piece.T)
    return jnp.concatenate(tiles, axis=1)


def block_out(values):
    pieces = []
    for s in range(TILES):
        count = min(PER * COLS, ROWS * COLS - s * PER * COLS)
        pieces.append(values[:, s * LANES : (s + 1) * LANES].T[:count])
    return jnp.concatenate(pieces, axis=0)


def pack(parts, out_ref, wide):
    stride = SUBS * len(parts)
    for a, part in enumerate(parts):
        for s in range(TILES):
            wide[pl.ds(a * SUBS + s, CHANNELS, stride=stride), :] = part[:, s * LANES : (s + 1) * LANES]
        wide[pl.ds(a * SUBS + TILES, CHANNELS, stride=stride), :] = jnp.zeros((CHANNELS, LANES), F32)
    out_ref[...] = wide[...].astype(BF16)


def unpack(ref, wide, count):
    wide[...] = ref[...].astype(F32)
    stride = SUBS * count
    return [
        jnp.concatenate(
            [wide[pl.ds(a * SUBS + s, CHANNELS, stride=stride), :] for s in range(TILES)], axis=1
        )
        for a in range(count)
    ]


def lanes_of(shape):
    return lax.broadcasted_iota(jnp.int32, shape, 1)


def matrix_in(ref, a):
    lane = lanes_of((LANES, LANES))
    pieces = [
        ref[:, c].astype(F32)[:, a * SUBS : (a + 1) * SUBS].reshape(LANES, LANES)
        for c in range(PARTS_C)
    ]
    rows = []
    for t in range(PER):
        turned = [
            pltpu.roll(pieces[c], ((c - t) * COLS) % LANES, 1) if (c - t) * COLS % LANES else pieces[c]
            for c in range(PARTS_C)
        ]
        tiles = []
        for q in range(WIDE // LANES):
            tile = jnp.zeros((LANES, LANES), F32)
            for c in range(PARTS_C):
                low, high = c * COLS - q * LANES, (c + 1) * COLS - q * LANES
                if high <= 0 or low >= LANES:
                    continue
                tile = jnp.where((lane >= low) & (lane < high), turned[c], tile)
            tiles.append(tile)
        rows.append(jnp.concatenate(tiles, axis=1))
    return jnp.concatenate(rows, axis=0).astype(BF16)


def matrix_out(values, a, wide):
    lane = lanes_of((LANES, LANES))
    for c in range(PARTS_C):
        low = c * COLS
        first, last = low // LANES, (low + COLS - 1) // LANES
        piece = jnp.zeros((LANES, LANES), F32)
        for t in range(PER):
            band = values[t * LANES : (t + 1) * LANES]
            source = band[:, first * LANES : (first + 1) * LANES]
            if last != first:
                source = jnp.where(lane >= low % LANES, source, band[:, last * LANES : (last + 1) * LANES])
            shift = ((t - c) * COLS) % LANES
            if shift:
                source = pltpu.roll(source, shift, 1)
            piece = jnp.where((lane >= t * COLS) & (lane < (t + 1) * COLS), source, piece)
        wide[:, c, a * SUBS : (a + 1) * SUBS, :] = piece.reshape(PARTS_R, SUBS, LANES)


def residue_of(index):
    part, s, t = (index % LANES) // SUBS, index % SUBS, index // LANES
    inner = PER * s + t
    return jnp.where(inner < ROWS, part * ROWS + inner, -1)


def first_to_second():
    first = lax.broadcasted_iota(jnp.int32, (WIDE, WIDE), 1)
    second = lax.broadcasted_iota(jnp.int32, (WIDE, WIDE), 0)
    return jnp.where(residue_of(first) == second, 1.0, 0.0).astype(BF16)


def second_to_first():
    first = lax.broadcasted_iota(jnp.int32, (WIDE, WIDE), 0)
    second = lax.broadcasted_iota(jnp.int32, (WIDE, WIDE), 1)
    return jnp.where(residue_of(first) == second, 1.0, 0.0).astype(BF16)


def project(normed, proj_mat):
    projected = dot(proj_mat, normed, 0, 0)
    return [projected[q * CHANNELS : (q + 1) * CHANNELS] for q in range(4)]


def edges(normed, proj_mat):
    p1, p2, p3, p4 = project(normed, proj_mat)
    return jax.nn.sigmoid(p1) * p2, jax.nn.sigmoid(p3) * p4


def gate_of(normed, gate_mat):
    return jax.nn.sigmoid(dot(gate_mat, normed, 0, 0))


def back_head(upstream, gating, product, normed_mix, mix_normed, mix_inverse, out_mat):
    through = (upstream * gating).astype(BF16)
    gate_up = (upstream * product * gating * (1.0 - gating)).astype(BF16)
    mix_up = dot(out_mat, through, 1, 0)
    out_part = dot(normed_mix, through, 1, 1)
    return norm_back(mix_normed, mix_inverse, mix_up), out_part, gate_up


def back_tail(upstream, pair_full, normed, left_grad, right_grad, gate_up, proj_mat, gate_mat):
    p1, p2, p3, p4 = project(normed, proj_mat)
    s1, s3 = jax.nn.sigmoid(p1), jax.nn.sigmoid(p3)
    proj_up = jnp.concatenate(
        [
            left_grad * p2 * s1 * (1.0 - s1),
            left_grad * s1,
            right_grad * p4 * s3 * (1.0 - s3),
            right_grad * s3,
        ],
        axis=0,
    ).astype(BF16)
    normed_up = dot(proj_mat, proj_up, 1, 0) + dot(gate_mat, gate_up, 1, 0)
    proj_part = dot(normed, proj_up, 1, 1)
    gate_part = dot(normed, gate_up, 1, 1)
    pair_normed, pair_inverse = norm_parts(pair_full)
    return upstream + norm_back(pair_normed, pair_inverse, normed_up), proj_part, gate_part


def start_kernel(pair_ref, proj_ref, gate_ref, message_ref, normed_ref, gating_ref, wide):
    normed = norm_parts(block_in(pair_ref))[0].astype(BF16)
    normed_ref[...] = normed
    pack(edges(normed, proj_ref[0]), message_ref, wide)
    gating_ref[...] = gate_of(normed, gate_ref[0])


def middle_kernel(
    mix_ref, pair_ref, gating0_ref, proj_ref, gate_ref, out_ref, message_ref, normed_ref, gating_ref, after_ref,
    narrow, wide,
):
    (mix,) = unpack(mix_ref, narrow, 1)
    normed_mix = norm_parts(mix)[0].astype(BF16)
    product = dot(out_ref[0], normed_mix, 0, 0)
    after = (block_in(pair_ref) + gating0_ref[...] * product).astype(BF16)
    after_ref[...] = after
    normed = norm_parts(after.astype(F32))[0].astype(BF16)
    normed_ref[...] = normed
    pack(edges(normed, proj_ref[1]), message_ref, wide)
    gating_ref[...] = gate_of(normed, gate_ref[1])


def turn_kernel(
    mix_ref, after_ref, gating_ref, cot_ref, out_ref, pair_out_ref, message_ref, gate_up_ref, out_part_ref, narrow
):
    (mix,) = unpack(mix_ref, narrow, 1)
    mix_normed, mix_inverse = norm_parts(mix)
    normed_mix = mix_normed.astype(BF16)
    product = dot(out_ref[1], normed_mix, 0, 0)
    gating = gating_ref[...]
    pair_out_ref[...] = block_out(after_ref[...].astype(F32) + gating * product).astype(BF16)
    mix_grad, out_part, gate_up = back_head(
        block_in(cot_ref), gating, product, normed_mix, mix_normed, mix_inverse, out_ref[1]
    )
    out_part_ref[...] = out_part
    gate_up_ref[...] = gate_up
    pack([mix_grad], message_ref, narrow)


def back_kernel(
    grads_ref, cot_ref, after_ref, normed1_ref, gate_up1_ref, mix_ref, gating0_ref, proj_ref, gate_ref, out_ref,
    message_ref, upstream_ref, gate_up_ref, proj_part_ref, gate_part_ref, out_part_ref, narrow, wide,
):
    left_grad, right_grad = unpack(grads_ref, wide, 2)
    upstream, proj_part, gate_part = back_tail(
        block_in(cot_ref), after_ref[...].astype(F32), normed1_ref[...], left_grad, right_grad, gate_up1_ref[...],
        proj_ref[1], gate_ref[1],
    )
    proj_part_ref[...] = proj_part
    gate_part_ref[...] = gate_part
    upstream_ref[...] = upstream
    (mix,) = unpack(mix_ref, narrow, 1)
    mix_normed, mix_inverse = norm_parts(mix)
    normed_mix = mix_normed.astype(BF16)
    product = dot(out_ref[0], normed_mix, 0, 0)
    mix_grad, out_part, gate_up = back_head(
        upstream, gating0_ref[...], product, normed_mix, mix_normed, mix_inverse, out_ref[0]
    )
    out_part_ref[...] = out_part
    gate_up_ref[...] = gate_up
    pack([mix_grad], message_ref, narrow)


def last_kernel(
    grads_ref, upstream_ref, pair_ref, normed_ref, gate_up_ref, proj_ref, gate_ref, proj1_ref, gate1_ref, out1_ref,
    out0_ref, pair_grad_ref, message_ref, wide,
):
    left_grad, right_grad = unpack(grads_ref, wide, 2)
    pair_grad, proj_part, gate_part = back_tail(
        upstream_ref[...], block_in(pair_ref), normed_ref[...], left_grad, right_grad, gate_up_ref[...],
        proj_ref[0], gate_ref[0],
    )
    pair_grad_ref[...] = block_out(pair_grad)
    parts = [proj_part[:, q * LANES : (q + 1) * LANES] for q in range(4)]
    parts += [proj1_ref[:, q * LANES : (q + 1) * LANES] for q in range(4)]
    parts += [gate_part, gate1_ref[...], out0_ref[...], out1_ref[...]]
    for q in range(2 * SUBS):
        wide[pl.ds(q, CHANNELS, stride=2 * SUBS), :] = parts[q] if q < len(parts) else jnp.zeros((CHANNELS, LANES), F32)
    message_ref[...] = wide[...].astype(BF16)


def sum_kernel(parts_ref, total_ref):
    total = jnp.sum(parts_ref[...].astype(F32), axis=0, keepdims=True) * (1.0 / SIZE)
    total_ref[...] = jnp.broadcast_to(total, total_ref.shape).astype(BF16)


def spread_kernel(sums_ref, proj_ref, gate_ref, out_ref, wide):
    wide[...] = sums_ref[...].astype(F32)
    rows = [wide[pl.ds(q, CHANNELS, stride=2 * SUBS), :] for q in range(12)]
    for l in range(2):
        proj_ref[l] = jnp.concatenate(rows[4 * l : 4 * l + 4], axis=1)
        gate_ref[l] = rows[8 + l]
        out_ref[l] = rows[10 + l]


def outgoing_kernel(edges_ref, mix_ref, left_ref, right_ref, wide):
    left, right = matrix_in(edges_ref, 0), matrix_in(edges_ref, 1)
    right = dot(first_to_second(), right, 1, 0).astype(BF16)
    left_ref[...], right_ref[...] = left, right
    matrix_out(dot(left, right, 1, 1), 0, wide)
    mix_ref[...] = wide[...].astype(BF16)


def incoming_kernel(edges_ref, mix_ref, left_ref, right_ref, wide):
    left, right = matrix_in(edges_ref, 0), matrix_in(edges_ref, 1)
    left_ref[...], right_ref[...] = left, right
    turned = dot(second_to_first(), left, 1, 1).astype(BF16)
    matrix_out(dot(turned, right, 1, 0), 0, wide)
    mix_ref[...] = wide[...].astype(BF16)


def incoming_back_kernel(grad_ref, left_ref, right_ref, grads_ref, wide):
    grad = dot(first_to_second(), matrix_in(grad_ref, 0), 1, 0).astype(BF16)
    matrix_out(dot(right_ref[...], grad, 1, 1), 0, wide)
    matrix_out(dot(left_ref[...], grad, 1, 0), 1, wide)
    grads_ref[...] = wide[...].astype(BF16)


def outgoing_back_kernel(grad_ref, left_ref, right_ref, grads_ref, wide):
    grad = matrix_in(grad_ref, 0)
    matrix_out(dot(grad, right_ref[...], 1, 0), 0, wide)
    turned = dot(second_to_first(), grad, 1, 1).astype(BF16)
    matrix_out(dot(turned, left_ref[...], 1, 0), 1, wide)
    grads_ref[...] = wide[...].astype(BF16)


def call(kernel, name, outs, scratch, *operands):
    return pl.pallas_call(
        kernel,
        out_shape=[jax.ShapeDtypeStruct(shape, kind) for shape, kind in outs],
        scratch_shapes=[pltpu.VMEM(shape, F32) for shape in scratch],
        compiler_params=pltpu.CompilerParams(vmem_limit_bytes=48 * 1024 * 1024),
        name=name,
    )(*operands)


def exchange(message):
    rows = message.size // (PARTS_R * PARTS_C * LANES)
    message = message.reshape(PARTS_R * PARTS_C, rows, LANES)
    return lax.all_to_all(message, AXES, 0, 0, tiled=True)


ONE = (CHANNELS * SUBS, LANES)
TWO = (CHANNELS * SUBS * 2, LANES)
MATRIX_ONE = (PARTS_R, PARTS_C, SUBS, LANES)
MATRIX_TWO = (PARTS_R, PARTS_C, SUBS * 2, LANES)
FLAT = (CHANNELS, TILES * LANES)
SQUARE = (WIDE, WIDE)


def local(pair_rep, proj_weight, gate_weight, out_weight, pair_cot):
    pair = pair_rep.reshape(ROWS * COLS, CHANNELS)
    cot = pair_cot.reshape(ROWS * COLS, CHANNELS)
    edges0, normed0, gating0 = call(
        start_kernel, "start", [(TWO, BF16), (FLAT, BF16), (FLAT, F32)], [TWO], pair, proj_weight, gate_weight
    )
    mix0, left0, right0 = call(
        outgoing_kernel, "outgoing", [(MATRIX_ONE, BF16), (SQUARE, BF16), (SQUARE, BF16)], [MATRIX_ONE],
        exchange(edges0).reshape(MATRIX_TWO),
    )
    mix0 = exchange(mix0).reshape(ONE)
    edges1, normed1, gating1, after = call(
        middle_kernel, "middle", [(TWO, BF16), (FLAT, BF16), (FLAT, F32), (FLAT, BF16)], [ONE, TWO],
        mix0, pair, gating0, proj_weight, gate_weight, out_weight,
    )
    mix1, left1, right1 = call(
        incoming_kernel, "incoming", [(MATRIX_ONE, BF16), (SQUARE, BF16), (SQUARE, BF16)], [MATRIX_ONE],
        exchange(edges1).reshape(MATRIX_TWO),
    )
    mix1 = exchange(mix1).reshape(ONE)
    pair_out, grad1, gate_up1, out_part1 = call(
        turn_kernel, "turn", [((ROWS * COLS, CHANNELS), BF16), (ONE, BF16), (FLAT, BF16), ((CHANNELS, CHANNELS), F32)],
        [ONE], mix1, after, gating1, cot, out_weight,
    )
    (grads1,) = call(
        incoming_back_kernel, "incoming_back", [(MATRIX_TWO, BF16)], [MATRIX_TWO],
        exchange(grad1).reshape(MATRIX_ONE), left1, right1,
    )
    grads1 = exchange(grads1).reshape(TWO)
    grad0, upstream, gate_up0, proj_part1, gate_part1, out_part0 = call(
        back_kernel, "back",
        [
            (ONE, BF16), (FLAT, F32), (FLAT, BF16), ((CHANNELS, 4 * CHANNELS), F32), ((CHANNELS, CHANNELS), F32),
            ((CHANNELS, CHANNELS), F32),
        ],
        [ONE, TWO], grads1, cot, after, normed1, gate_up1, mix0, gating0, proj_weight, gate_weight, out_weight,
    )
    (grads0,) = call(
        outgoing_back_kernel, "outgoing_back", [(MATRIX_TWO, BF16)], [MATRIX_TWO],
        exchange(grad0).reshape(MATRIX_ONE), left0, right0,
    )
    grads0 = exchange(grads0).reshape(TWO)
    pair_grad, parts = call(
        last_kernel, "last", [((ROWS * COLS, CHANNELS), F32), (TWO, BF16)], [TWO],
        grads0, upstream, pair, normed0, gate_up0, proj_weight, gate_weight, proj_part1, gate_part1, out_part1,
        out_part0,
    )
    (sums,) = call(sum_kernel, "sum", [((CHANNELS, 2 * SUBS, LANES), BF16)], [], exchange(parts))
    proj_grad, gate_grad, out_grad = call(
        spread_kernel, "spread",
        [((2, CHANNELS, 4 * CHANNELS), F32), ((2, CHANNELS, CHANNELS), F32), ((2, CHANNELS, CHANNELS), F32)],
        [TWO], exchange(sums).reshape(TWO),
    )
    return (
        pair_out.reshape(ROWS, COLS, CHANNELS),
        pair_grad.reshape(ROWS, COLS, CHANNELS),
        proj_grad,
        gate_grad,
        out_grad,
    )


def solution(mesh):
    in_specs = (P("row", "col", None), P(), P(), P(), P("row", "col", None))
    out_specs = (P("row", "col", None), P("row", "col", None), P(), P(), P())
    return jax.shard_map(local, mesh=mesh, in_specs=in_specs, out_specs=out_specs, check_vma=False)
```

```python
import jax
import jax.numpy as jnp
from jax import lax
from jax.experimental import pallas as pl
from jax.experimental.pallas import tpu as pltpu
from jax.sharding import PartitionSpec as P

EPSILON = 1e-05
F32 = jnp.float32
BF16 = jnp.bfloat16
AXES = ("row", "col")

PARTS_R, PARTS_C = 16, 8
DEVICES = PARTS_R * PARTS_C
ROWS, COLS, CHANNELS = 20, 40, 128
PER = 3
TILES = 7
SUBS = 8
LANES = 128
SIZE = 320
WIDE = 384
SINGLE, DOUBLE, WEIGHTS = 8, 14, 12


def dot(first_op, second_op, first_dim, second_dim):
    return lax.dot_general(
        first_op,
        second_op,
        (((first_dim,), (second_dim,)), ((), ())),
        preferred_element_type=F32,
    )


def mean0(values):
    return jnp.sum(values, axis=0, keepdims=True) * (1.0 / CHANNELS)


def norm_parts(values):
    centered = values - mean0(values)
    inverse = lax.rsqrt(mean0(centered * centered) + EPSILON)
    return centered * inverse, inverse


def norm_back(normed, inverse, upstream):
    return inverse * (upstream - mean0(upstream) - normed * mean0(upstream * normed))


def sigmoid(values):
    return 0.5 * jnp.tanh(0.5 * values) + 0.5


def block_in(ref):
    values = ref[...].astype(F32)
    tiles = []
    for s in range(TILES):
        low = s * PER * COLS
        high = min(low + PER * COLS, ROWS * COLS)
        piece = values[low:high]
        piece = jnp.concatenate([piece, jnp.zeros((LANES - (high - low), CHANNELS), F32)], axis=0)
        tiles.append(piece.T)
    return jnp.concatenate(tiles, axis=1)


def block_out(values):
    pieces = []
    for s in range(TILES):
        count = min(PER * COLS, ROWS * COLS - s * PER * COLS)
        pieces.append(values[:, s * LANES : (s + 1) * LANES].T[:count])
    return jnp.concatenate(pieces, axis=0)


def rows_of(parts):
    return SINGLE if parts == 1 else DOUBLE


def pitch_of(parts):
    return SINGLE + 1 if parts == 1 else DOUBLE


def pack(parts, out_ref, wide):
    pitch = pitch_of(len(parts))
    for a, part in enumerate(parts):
        for s in range(TILES):
            wide[pl.ds(a * TILES + s, CHANNELS, stride=pitch), :] = part[:, s * LANES : (s + 1) * LANES]
    if len(parts) == 1:
        wide[pl.ds(TILES, CHANNELS, stride=pitch), :] = jnp.zeros((CHANNELS, LANES), F32)
        for d in range(0, CHANNELS, 2):
            two = [wide[e * pitch : e * pitch + SINGLE, :] for e in (d, d + 1)]
            out_ref[d * SINGLE : (d + 2) * SINGLE, :] = jnp.concatenate(two, axis=0).astype(BF16)
    else:
        out_ref[...] = wide[...].astype(BF16)


def unpack(ref, wide, count):
    pitch = pitch_of(count)
    if count == 1:
        for d in range(0, CHANNELS, 2):
            two = ref[d * SINGLE : (d + 2) * SINGLE, :].astype(F32)
            for e in range(2):
                wide[(d + e) * pitch : (d + e) * pitch + SINGLE, :] = two[e * SINGLE : (e + 1) * SINGLE]
    else:
        wide[...] = ref[...].astype(F32)
    return [
        jnp.concatenate([wide[pl.ds(a * TILES + s, CHANNELS, stride=pitch), :] for s in range(TILES)], axis=1)
        for a in range(count)
    ]


def matrix_in(wide, a, count):
    lane = lax.broadcasted_iota(jnp.int32, (LANES, LANES), 1)
    real = lax.broadcasted_iota(jnp.int32, (LANES, LANES), 0) % SUBS < TILES
    stride = rows_of(count)
    pieces = []
    for c in range(PARTS_C):
        starts = [(r * PARTS_C + c) * stride + a * TILES for r in range(PARTS_R)]
        piece = jnp.concatenate([wide[start : start + SUBS, :] for start in starts], axis=0)
        pieces.append((piece if count == 1 else jnp.where(real, piece, 0.0)).astype(BF16))
    rows = []
    for t in range(PER):
        turned = [
            pltpu.roll(pieces[c], ((c - t) * COLS) % LANES, 1) if (c - t) * COLS % LANES else pieces[c]
            for c in range(PARTS_C)
        ]
        tiles = []
        for q in range(WIDE // LANES):
            low, high = q * LANES, (q + 1) * LANES
            inside = [c for c in range(PARTS_C) if c * COLS < high and (c + 1) * COLS > low]
            tile = turned[inside[0]]
            for c in inside[1:]:
                tile = jnp.where(lane >= c * COLS - low, turned[c], tile)
            if high > SIZE:
                tile = jnp.where(lane < SIZE - low, tile, jnp.zeros_like(tile))
            tiles.append(tile)
        rows.append(jnp.concatenate(tiles, axis=1))
    return jnp.concatenate(rows, axis=0)


def matrix_out(values, a, count, wide):
    lane = lax.broadcasted_iota(jnp.int32, (LANES, LANES), 1)
    stride = rows_of(count)
    height = SUBS if count == 1 else TILES
    for c in range(PARTS_C):
        low = c * COLS
        first, last = low // LANES, (low + COLS - 1) // LANES
        piece = None
        for t in range(PER):
            band = values[t * LANES : (t + 1) * LANES]
            source = band[:, first * LANES : (first + 1) * LANES]
            if last != first:
                source = jnp.where(lane >= low % LANES, source, band[:, last * LANES : (last + 1) * LANES])
            shift = ((t - c) * COLS) % LANES
            if shift:
                source = pltpu.roll(source, shift, 1)
            piece = source if piece is None else jnp.where(lane >= t * COLS, source, piece)
        piece = jnp.where(lane < PER * COLS, piece, 0.0)
        for r in range(PARTS_R):
            start = (r * PARTS_C + c) * stride + a * TILES
            wide[start : start + height, :] = piece[r * SUBS : r * SUBS + height]


def residue_of(index):
    part, s, t = (index % LANES) // SUBS, index % SUBS, index // LANES
    inner = PER * s + t
    return jnp.where((s < TILES) & (inner < ROWS), part * ROWS + inner, -1)


def first_to_second():
    first = lax.broadcasted_iota(jnp.int32, (WIDE, WIDE), 1)
    second = lax.broadcasted_iota(jnp.int32, (WIDE, WIDE), 0)
    return jnp.where(residue_of(first) == second, 1.0, 0.0).astype(BF16)


def second_to_first():
    first = lax.broadcasted_iota(jnp.int32, (WIDE, WIDE), 0)
    second = lax.broadcasted_iota(jnp.int32, (WIDE, WIDE), 1)
    return jnp.where(residue_of(first) == second, 1.0, 0.0).astype(BF16)


def edges(normed, proj_mat, kept_ref):
    projected = dot(proj_mat, normed, 0, 0)
    p1, p2, p3, p4 = [projected[q * CHANNELS : (q + 1) * CHANNELS] for q in range(4)]
    s1, s3 = sigmoid(p1), sigmoid(p3)
    left, right = s1 * p2, s3 * p4
    for q, value in enumerate((s1, left, s3, right)):
        kept_ref[q] = value
    return left, right


def back_head(upstream, gating, product, normed_mix, mix_normed, mix_inverse, out_mat):
    through = (upstream * gating).astype(BF16)
    gate_up = (upstream * product * gating * (1.0 - gating)).astype(BF16)
    mix_up = dot(out_mat, through, 1, 0)
    out_part = dot(normed_mix, through, 1, 1)
    return norm_back(mix_normed, mix_inverse, mix_up), out_part, gate_up


def back_tail(upstream, pair_normed, pair_inverse, kept_ref, left_grad, right_grad, gate_up, proj_mat, gate_mat):
    s1, left, s3, right = [kept_ref[q] for q in range(4)]
    proj_up = jnp.concatenate(
        [left_grad * left * (1.0 - s1), left_grad * s1, right_grad * right * (1.0 - s3), right_grad * s3], axis=0
    ).astype(BF16)
    normed_up = dot(proj_mat, proj_up, 1, 0) + dot(gate_mat, gate_up, 1, 0)
    return upstream + norm_back(pair_normed, pair_inverse, normed_up), proj_up


def start_kernel(pair_ref, proj_ref, message_ref, flat_ref, normed_ref, inverse_ref, kept_ref, wide):
    pair = block_in(pair_ref)
    flat_ref[...] = pair.astype(BF16)
    pair_normed, inverse = norm_parts(pair)
    normed_ref[...] = pair_normed
    inverse_ref[...] = inverse
    pack(edges(pair_normed.astype(BF16), proj_ref[0], kept_ref), message_ref, wide)


def middle_kernel(
    mix_ref, pair_ref, normed0_ref, proj_ref, gate_ref, out_ref,
    message_ref, mix_normed_ref, mix_inverse_ref, product_ref, gating0_ref, after_ref, normed_ref, inverse_ref, kept_ref,
    gating_ref, narrow, wide,
):
    (mix,) = unpack(mix_ref, narrow, 1)
    mix_normed, mix_inverse = norm_parts(mix)
    mix_normed_ref[...] = mix_normed
    mix_inverse_ref[...] = mix_inverse
    product = dot(out_ref[0], mix_normed.astype(BF16), 0, 0)
    product_ref[...] = product
    gating0 = sigmoid(dot(gate_ref[0], normed0_ref[...].astype(BF16), 0, 0))
    gating0_ref[...] = gating0
    after = (pair_ref[...].astype(F32) + gating0 * product).astype(BF16)
    after_ref[...] = after
    pair_normed, inverse = norm_parts(after.astype(F32))
    normed_ref[...] = pair_normed
    inverse_ref[...] = inverse
    normed = pair_normed.astype(BF16)
    pack(edges(normed, proj_ref[1], kept_ref), message_ref, wide)
    gating_ref[...] = sigmoid(dot(gate_ref[1], normed, 0, 0))


def turn_kernel(
    mix_ref, after_ref, gating_ref, cot_ref, out_ref, normed_ref,
    pair_out_hbm, message_ref, cot_out_ref, gate_up_ref, gate_part_ref, out_part_ref, narrow, pair_out, sem,
):
    (mix,) = unpack(mix_ref, narrow, 1)
    mix_normed, mix_inverse = norm_parts(mix)
    normed_mix = mix_normed.astype(BF16)
    product = dot(out_ref[1], normed_mix, 0, 0)
    gating = gating_ref[...]
    pair_out[...] = block_out(after_ref[...].astype(F32) + gating * product).astype(BF16)
    copy = pltpu.make_async_copy(pair_out, pair_out_hbm, sem)
    copy.start()
    cot = block_in(cot_ref)
    cot_out_ref[...] = cot.astype(BF16)
    mix_grad, out_part, gate_up = back_head(cot, gating, product, normed_mix, mix_normed, mix_inverse, out_ref[1])
    pack([mix_grad], message_ref, narrow)
    out_part_ref[...] = out_part
    gate_up_ref[...] = gate_up
    gate_part_ref[...] = dot(normed_ref[...].astype(BF16), gate_up, 1, 1)
    copy.wait()


def back_kernel(
    grads_ref, cot_ref, normed1_ref, inverse1_ref, kept1_ref, gate_up1_ref, mix_normed_ref, mix_inverse_ref,
    product_ref, gating0_ref, proj_ref, gate_ref, out_ref,
    message_ref, upstream_ref, gate_up_ref, proj_part_ref, out_part_ref, narrow, wide,
):
    left_grad, right_grad = unpack(grads_ref, wide, 2)
    pair_normed = normed1_ref[...]
    upstream, proj_up = back_tail(
        cot_ref[...].astype(F32), pair_normed, inverse1_ref[...], kept1_ref, left_grad, right_grad, gate_up1_ref[...],
        proj_ref[1], gate_ref[1],
    )
    upstream_ref[...] = upstream
    proj_part_ref[...] = dot(pair_normed.astype(BF16), proj_up, 1, 1)
    mix_normed = mix_normed_ref[...]
    mix_grad, out_part, gate_up = back_head(
        upstream, gating0_ref[...], product_ref[...], mix_normed.astype(BF16), mix_normed, mix_inverse_ref[...],
        out_ref[0],
    )
    pack([mix_grad], message_ref, narrow)
    out_part_ref[...] = out_part
    gate_up_ref[...] = gate_up


def last_kernel(
    grads_ref, upstream_ref, normed_ref, inverse_ref, kept_ref, gate_up_ref, proj_ref, gate_ref,
    proj1_ref, gate1_ref, out1_ref, out0_ref,
    pair_grad_hbm, message_ref, wide, weights, pair_grad, sem,
):
    left_grad, right_grad = unpack(grads_ref, wide, 2)
    pair_normed = normed_ref[...]
    gate_up = gate_up_ref[...]
    total, proj_up = back_tail(
        upstream_ref[...], pair_normed, inverse_ref[...], kept_ref, left_grad, right_grad, gate_up,
        proj_ref[0], gate_ref[0],
    )
    pair_grad[...] = block_out(total)
    copy = pltpu.make_async_copy(pair_grad, pair_grad_hbm, sem)
    copy.start()
    normed = pair_normed.astype(BF16)
    proj_part = dot(normed, proj_up, 1, 1)
    parts = [proj_part[:, q * LANES : (q + 1) * LANES] for q in range(4)]
    parts += [proj1_ref[:, q * LANES : (q + 1) * LANES] for q in range(4)]
    parts += [dot(normed, gate_up, 1, 1), gate1_ref[...], out0_ref[...], out1_ref[...]]
    for q, part in enumerate(parts):
        weights[pl.ds(q, CHANNELS, stride=WEIGHTS), :] = part
    message_ref[...] = weights[...].astype(BF16)
    copy.wait()


def sum_kernel(parts_ref, total_ref):
    pairs = parts_ref[...].astype(F32).reshape(DEVICES // 2, 2 * WEIGHTS, LANES)
    total = jnp.sum(pairs, axis=0)
    total = (total[:WEIGHTS] + total[WEIGHTS:]) * (1.0 / SIZE)
    total = jnp.concatenate([total, total], axis=0)[None]
    total_ref[...] = jnp.broadcast_to(total, pairs.shape).reshape(DEVICES * WEIGHTS, LANES).astype(BF16)


def spread_kernel(sums_ref, proj_hbm, gate_hbm, out_hbm, weights, proj, gate, out, sems):
    weights[...] = sums_ref[...].astype(F32)
    copies = []
    for l in range(2):
        proj[l] = jnp.concatenate(
            [weights[pl.ds(4 * l + q, CHANNELS, stride=WEIGHTS), :] for q in range(4)], axis=1
        )
        copies.append(pltpu.make_async_copy(proj.at[l], proj_hbm.at[l], sems.at[l]))
        copies[-1].start()
    for l in range(2):
        gate[l] = weights[pl.ds(8 + l, CHANNELS, stride=WEIGHTS), :]
        out[l] = weights[pl.ds(10 + l, CHANNELS, stride=WEIGHTS), :]
    copies.append(pltpu.make_async_copy(gate, gate_hbm, sems.at[2]))
    copies.append(pltpu.make_async_copy(out, out_hbm, sems.at[3]))
    for copy in copies[2:]:
        copy.start()
    for copy in copies:
        copy.wait()


def outgoing_kernel(edges_ref, mix_ref, left_ref, right_ref, double, single):
    double[: DEVICES * DOUBLE, :] = edges_ref[...].astype(F32)
    left, right = matrix_in(double, 0, 2), matrix_in(double, 1, 2)
    right = dot(first_to_second(), right, 1, 0).astype(BF16)
    left_ref[...], right_ref[...] = left, right
    matrix_out(dot(left, right, 1, 1), 0, 1, single)
    mix_ref[...] = single[...].astype(BF16)


def incoming_kernel(edges_ref, mix_ref, left_ref, right_ref, double, single):
    double[: DEVICES * DOUBLE, :] = edges_ref[...].astype(F32)
    left, right = matrix_in(double, 0, 2), matrix_in(double, 1, 2)
    left_ref[...], right_ref[...] = left, right
    turned = dot(second_to_first(), left, 1, 1).astype(BF16)
    matrix_out(dot(turned, right, 1, 0), 0, 1, single)
    mix_ref[...] = single[...].astype(BF16)


def incoming_back_kernel(grad_ref, left_ref, right_ref, grads_ref, double, single):
    single[...] = grad_ref[...].astype(F32)
    grad = dot(first_to_second(), matrix_in(single, 0, 1), 1, 0).astype(BF16)
    matrix_out(dot(right_ref[...], grad, 1, 1), 0, 2, double)
    matrix_out(dot(left_ref[...], grad, 1, 0), 1, 2, double)
    grads_ref[...] = double[: DEVICES * DOUBLE, :].astype(BF16)


def outgoing_back_kernel(grad_ref, left_ref, right_ref, grads_ref, double, single):
    single[...] = grad_ref[...].astype(F32)
    grad = matrix_in(single, 0, 1)
    matrix_out(dot(grad, right_ref[...], 1, 0), 0, 2, double)
    turned = dot(second_to_first(), grad, 1, 1).astype(BF16)
    matrix_out(dot(turned, left_ref[...], 1, 0), 1, 2, double)
    grads_ref[...] = double[: DEVICES * DOUBLE, :].astype(BF16)


SINGLE_SHAPE = (DEVICES * SINGLE, LANES)
DOUBLE_SHAPE = (DEVICES * DOUBLE, LANES)
WEIGHTS_SHAPE = (DEVICES * WEIGHTS, LANES)
BLOCK = (ROWS * COLS, CHANNELS)
FLAT = (CHANNELS, TILES * LANES)
KEPT = (4, CHANNELS, TILES * LANES)
LINE = (1, TILES * LANES)
SQUARE = (WIDE, WIDE)
WEIGHT = (CHANNELS, CHANNELS)
PROJ = (CHANNELS, 4 * CHANNELS)
DMA = pltpu.SemaphoreType.DMA


def call(kernel, name, outs, scratch, *operands, far_out=()):
    def spec(far):
        return pl.BlockSpec(memory_space=pl.ANY if far else pltpu.VMEM)

    return pl.pallas_call(
        kernel,
        out_shape=[jax.ShapeDtypeStruct(shape, kind) for shape, kind in outs],
        in_specs=[spec(False) for _ in operands],
        out_specs=[spec(position in far_out) for position in range(len(outs))],
        scratch_shapes=scratch,
        compiler_params=pltpu.CompilerParams(vmem_limit_bytes=24 * 1024 * 1024),
        name=name,
    )(*operands)


def exchange(message):
    rows = message.shape[0] // DEVICES
    shape = (DEVICES, rows, LANES)
    for low in (4, 2):
        if rows % 8 and rows % low == 0:
            shape = (DEVICES, rows // low, low, LANES)
            break
    return lax.all_to_all(message.reshape(shape), AXES, 0, 0, tiled=True).reshape(message.shape)


def local(pair_rep, proj_weight, gate_weight, out_weight, pair_cot):
    pair = pair_rep.reshape(BLOCK)
    cot = pair_cot.reshape(BLOCK)
    single, double, weights = [pltpu.VMEM(shape, F32) for shape in (SINGLE_SHAPE, DOUBLE_SHAPE, WEIGHTS_SHAPE)]
    spaced = pltpu.VMEM((DEVICES * (SINGLE + 1), LANES), F32)
    longer = pltpu.VMEM((DEVICES * DOUBLE + SUBS, LANES), F32)
    edges0, pair0, normed0, inverse0, kept0 = call(
        start_kernel, "start", [(DOUBLE_SHAPE, BF16), (FLAT, BF16), (FLAT, F32), (LINE, F32), (KEPT, F32)], [double],
        pair, proj_weight,
    )
    mix0, left0, right0 = call(
        outgoing_kernel, "outgoing", [(SINGLE_SHAPE, BF16), (SQUARE, BF16), (SQUARE, BF16)], [longer, single],
        exchange(edges0),
    )
    edges1, mix_normed0, mix_inverse0, product0, gating0, after, normed1, inverse1, kept1, gating1 = call(
        middle_kernel, "middle",
        [
            (DOUBLE_SHAPE, BF16), (FLAT, F32), (LINE, F32), (FLAT, F32), (FLAT, F32), (FLAT, BF16), (FLAT, F32),
            (LINE, F32), (KEPT, F32), (FLAT, F32),
        ],
        [spaced, double], exchange(mix0), pair0, normed0, proj_weight, gate_weight, out_weight,
    )
    mix1, left1, right1 = call(
        incoming_kernel, "incoming", [(SINGLE_SHAPE, BF16), (SQUARE, BF16), (SQUARE, BF16)], [longer, single],
        exchange(edges1),
    )
    pair_out, grad1, cot1, gate_up1, gate_part1, out_part1 = call(
        turn_kernel, "turn",
        [(BLOCK, BF16), (SINGLE_SHAPE, BF16), (FLAT, BF16), (FLAT, BF16), (WEIGHT, F32), (WEIGHT, F32)],
        [spaced, pltpu.VMEM(BLOCK, BF16), DMA],
        exchange(mix1), after, gating1, cot, out_weight, normed1, far_out=(0,),
    )
    (grads1,) = call(
        incoming_back_kernel, "incoming_back", [(DOUBLE_SHAPE, BF16)], [longer, single], exchange(grad1), left1, right1
    )
    grad0, upstream, gate_up0, proj_part1, out_part0 = call(
        back_kernel, "back",
        [(SINGLE_SHAPE, BF16), (FLAT, F32), (FLAT, BF16), (PROJ, F32), (WEIGHT, F32)],
        [spaced, double], exchange(grads1), cot1, normed1, inverse1, kept1, gate_up1, mix_normed0, mix_inverse0,
        product0, gating0, proj_weight, gate_weight, out_weight,
    )
    (grads0,) = call(
        outgoing_back_kernel, "outgoing_back", [(DOUBLE_SHAPE, BF16)], [longer, single], exchange(grad0), left0, right0
    )
    pair_grad, parts = call(
        last_kernel, "last", [(BLOCK, F32), (WEIGHTS_SHAPE, BF16)],
        [double, weights, pltpu.VMEM(BLOCK, F32), DMA],
        exchange(grads0), upstream, normed0, inverse0, kept0, gate_up0, proj_weight, gate_weight,
        proj_part1, gate_part1, out_part1, out_part0, far_out=(0,),
    )
    (sums,) = call(sum_kernel, "sum", [(WEIGHTS_SHAPE, BF16)], [], exchange(parts))
    proj_grad, gate_grad, out_grad = call(
        spread_kernel, "spread", [((2,) + PROJ, F32), ((2,) + WEIGHT, F32), ((2,) + WEIGHT, F32)],
        [weights, pltpu.VMEM((2,) + PROJ, F32), pltpu.VMEM((2,) + WEIGHT, F32), pltpu.VMEM((2,) + WEIGHT, F32), DMA((4,))],
        exchange(sums), far_out=(0, 1, 2),
    )
    return (
        pair_out.reshape(ROWS, COLS, CHANNELS),
        pair_grad.reshape(ROWS, COLS, CHANNELS),
        proj_grad,
        gate_grad,
        out_grad,
    )


def solution(mesh):
    in_specs = (P("row", "col", None), P(), P(), P(), P("row", "col", None))
    out_specs = (P("row", "col", None), P("row", "col", None), P(), P(), P())
    return jax.shard_map(local, mesh=mesh, in_specs=in_specs, out_specs=out_specs, check_vma=False)
```

```python
import jax
import jax.numpy as jnp
from jax import lax
from jax.experimental import pallas as pl
from jax.experimental.pallas import tpu as pltpu
from jax.sharding import PartitionSpec as P

EPSILON = 1e-05
F32 = jnp.float32
BF16 = jnp.bfloat16
AXES = ("row", "col")

PARTS_R, PARTS_C = 16, 8
DEVICES = PARTS_R * PARTS_C
ROWS, COLS, CHANNELS = 20, 40, 128
PER = 3
TILES = 7
SUBS = 8
LANES = 128
SIZE = 320
WIDE = 384
SINGLE, DOUBLE, WEIGHTS = 8, 14, 12


def dot(first_op, second_op, first_dim, second_dim):
    return lax.dot_general(
        first_op,
        second_op,
        (((first_dim,), (second_dim,)), ((), ())),
        preferred_element_type=F32,
    )


def mean0(values):
    return jnp.sum(values, axis=0, keepdims=True) * (1.0 / CHANNELS)


def norm_parts(values):
    centered = values - mean0(values)
    inverse = lax.rsqrt(mean0(centered * centered) + EPSILON)
    return centered * inverse, inverse


def norm_back(normed, inverse, upstream):
    return inverse * (upstream - mean0(upstream) - normed * mean0(upstream * normed))


def sigmoid(values):
    return 0.5 * jnp.tanh(0.5 * values) + 0.5


def identity():
    shape = (CHANNELS, CHANNELS)
    same = lax.broadcasted_iota(jnp.int32, shape, 0) == lax.broadcasted_iota(jnp.int32, shape, 1)
    return jnp.where(same, 1.0, 0.0).astype(BF16)


def block_in(ref):
    values = ref[...].astype(F32)
    pieces = []
    for s in range(TILES):
        low = s * PER * COLS
        high = min(low + PER * COLS, ROWS * COLS)
        pieces += [values[low:high], jnp.zeros((LANES - (high - low), CHANNELS), F32)]
    return dot(identity(), jnp.concatenate(pieces, axis=0).astype(BF16), 1, 1)


def block_out(values):
    pieces = []
    for s in range(TILES):
        count = min(PER * COLS, ROWS * COLS - s * PER * COLS)
        pieces.append(values[:, s * LANES : (s + 1) * LANES].T[:count])
    return jnp.concatenate(pieces, axis=0)


def block_out_exact(values):
    pieces = []
    for s in range(TILES):
        count = min(PER * COLS, ROWS * COLS - s * PER * COLS)
        pieces.append(dot(identity(), values[:, s * LANES : (s + 1) * LANES], 1, 1)[:count])
    return jnp.concatenate(pieces, axis=0).astype(BF16)


def rows_of(parts):
    return SINGLE if parts == 1 else DOUBLE


def pitch_of(parts):
    return SINGLE + 1 if parts == 1 else DOUBLE


def pack(parts, out_ref, wide):
    pitch = pitch_of(len(parts))
    for a, part in enumerate(parts):
        for s in range(TILES):
            wide[pl.ds(a * TILES + s, CHANNELS, stride=pitch), :] = part[:, s * LANES : (s + 1) * LANES]
    if len(parts) == 1:
        wide[pl.ds(TILES, CHANNELS, stride=pitch), :] = jnp.zeros((CHANNELS, LANES), F32)
        for d in range(0, CHANNELS, 2):
            two = [wide[e * pitch : e * pitch + SINGLE, :] for e in (d, d + 1)]
            out_ref[d * SINGLE : (d + 2) * SINGLE, :] = jnp.concatenate(two, axis=0).astype(BF16)
    else:
        out_ref[...] = wide[...].astype(BF16)


def unpack(ref, wide, count):
    pitch = pitch_of(count)
    if count == 1:
        for d in range(0, CHANNELS, 2):
            two = ref[d * SINGLE : (d + 2) * SINGLE, :].astype(F32)
            for e in range(2):
                wide[(d + e) * pitch : (d + e) * pitch + SINGLE, :] = two[e * SINGLE : (e + 1) * SINGLE]
    else:
        wide[...] = ref[...].astype(F32)
    return [
        jnp.concatenate([wide[pl.ds(a * TILES + s, CHANNELS, stride=pitch), :] for s in range(TILES)], axis=1)
        for a in range(count)
    ]


def pieces_in(ref, count):
    values = ref[...].astype(F32).reshape(PARTS_R, -1, SUBS, LANES)
    if count == 1:
        return [[values[:, c].reshape(LANES, LANES) for c in range(PARTS_C)]]
    sub = lax.broadcasted_iota(jnp.int32, (PARTS_R, SUBS, LANES), 1)
    parts = []
    for a in range(count):
        parts.append([])
        for c in range(PARTS_C):
            tile, shift = divmod(c * DOUBLE + a * TILES, SUBS)
            piece = values[:, tile]
            if shift + TILES > SUBS:
                piece = jnp.where(sub >= shift, piece, values[:, tile + 1])
            if shift:
                piece = pltpu.roll(piece, SUBS - shift, 1)
            parts[a].append(jnp.where(sub < TILES, piece, 0.0).reshape(LANES, LANES))
    return parts


def matrix_of(pieces):
    lane = lax.broadcasted_iota(jnp.int32, (LANES, LANES), 1)
    pieces = [piece.astype(BF16) for piece in pieces]
    rows = []
    for t in range(PER):
        turned = [
            pltpu.roll(pieces[c], ((c - t) * COLS) % LANES, 1) if (c - t) * COLS % LANES else pieces[c]
            for c in range(PARTS_C)
        ]
        tiles = []
        for q in range(WIDE // LANES):
            low, high = q * LANES, (q + 1) * LANES
            inside = [c for c in range(PARTS_C) if c * COLS < high and (c + 1) * COLS > low]
            tile = turned[inside[0]]
            for c in inside[1:]:
                tile = jnp.where(lane >= c * COLS - low, turned[c], tile)
            if high > SIZE:
                tile = jnp.where(lane < SIZE - low, tile, jnp.zeros_like(tile))
            tiles.append(tile)
        rows.append(jnp.concatenate(tiles, axis=1))
    return jnp.concatenate(rows, axis=0)


def pieces_of(values):
    lane = lax.broadcasted_iota(jnp.int32, (LANES, LANES), 1)
    pieces = []
    for c in range(PARTS_C):
        low = c * COLS
        first, last = low // LANES, (low + COLS - 1) // LANES
        piece = None
        for t in range(PER):
            band = values[t * LANES : (t + 1) * LANES]
            source = band[:, first * LANES : (first + 1) * LANES]
            if last != first:
                source = jnp.where(lane >= low % LANES, source, band[:, last * LANES : (last + 1) * LANES])
            shift = ((t - c) * COLS) % LANES
            if shift:
                source = pltpu.roll(source, shift, 1)
            piece = source if piece is None else jnp.where(lane >= t * COLS, source, piece)
        pieces.append(jnp.where(lane < PER * COLS, piece, 0.0))
    return pieces


def pieces_out(parts, ref):
    if len(parts) == 1:
        tiles = [piece.reshape(PARTS_R, SUBS, LANES) for piece in parts[0]]
    else:
        sub = lax.broadcasted_iota(jnp.int32, (PARTS_R, SUBS, LANES), 1)
        tiles = [None] * (PARTS_C * DOUBLE // SUBS)
        for c in range(PARTS_C):
            for a, pieces in enumerate(parts):
                tile, shift = divmod(c * DOUBLE + a * TILES, SUBS)
                piece = pieces[c].reshape(PARTS_R, SUBS, LANES)
                if shift:
                    piece = pltpu.roll(piece, shift, 1)
                tiles[tile] = piece if tiles[tile] is None else jnp.where(sub >= shift, piece, tiles[tile])
                if shift + TILES > SUBS:
                    tiles[tile + 1] = piece
    values = jnp.concatenate([tile[:, None] for tile in tiles], axis=1)
    ref[...] = values.reshape(-1, LANES).astype(BF16)


def first_to_second():
    index = lax.broadcasted_iota(jnp.int32, (1, WIDE), 1)
    part, s, t = (index % LANES) // SUBS, index % SUBS, index // LANES
    inner = PER * s + t
    residue = jnp.where((s < TILES) & (inner < ROWS), part * ROWS + inner, -1)
    second = lax.broadcasted_iota(jnp.int32, (WIDE, WIDE), 0)
    return jnp.where(second == residue, 1.0, 0.0).astype(BF16)


def second_to_first():
    index = lax.broadcasted_iota(jnp.int32, (WIDE, 1), 0)
    part, s, t = (index % LANES) // SUBS, index % SUBS, index // LANES
    inner = PER * s + t
    residue = jnp.where((s < TILES) & (inner < ROWS), part * ROWS + inner, -1)
    second = lax.broadcasted_iota(jnp.int32, (WIDE, WIDE), 1)
    return jnp.where(second == residue, 1.0, 0.0).astype(BF16)


def edges(normed, proj_mat, kept_ref):
    projected = dot(proj_mat, normed, 0, 0)
    p1, p2, p3, p4 = [projected[q * CHANNELS : (q + 1) * CHANNELS] for q in range(4)]
    s1, s3 = sigmoid(p1), sigmoid(p3)
    left, right = s1 * p2, s3 * p4
    for q, value in enumerate((s1, left, s3, right)):
        kept_ref[q] = value
    return left, right


def back_head(upstream, gating, product, normed_mix, mix_normed, mix_inverse, out_mat):
    through = (upstream * gating).astype(BF16)
    gate_up = (upstream * product * gating * (1.0 - gating)).astype(BF16)
    mix_up = dot(out_mat, through, 1, 0)
    out_part = dot(normed_mix, through, 1, 1)
    return norm_back(mix_normed, mix_inverse, mix_up), out_part, gate_up


def back_tail(upstream, pair_normed, pair_inverse, kept_ref, left_grad, right_grad, gate_up, proj_mat, gate_mat):
    s1, left, s3, right = [kept_ref[q] for q in range(4)]
    proj_up = jnp.concatenate(
        [left_grad * left * (1.0 - s1), left_grad * s1, right_grad * right * (1.0 - s3), right_grad * s3], axis=0
    ).astype(BF16)
    normed_up = dot(proj_mat, proj_up, 1, 0) + dot(gate_mat, gate_up, 1, 0)
    return upstream + norm_back(pair_normed, pair_inverse, normed_up), proj_up


def start_kernel(pair_ref, proj_ref, message_ref, flat_ref, normed_ref, inverse_ref, kept_ref, wide):
    pair = block_in(pair_ref)
    flat_ref[...] = pair.astype(BF16)
    pair_normed, inverse = norm_parts(pair)
    normed_ref[...] = pair_normed
    inverse_ref[...] = inverse
    pack(edges(pair_normed.astype(BF16), proj_ref[0], kept_ref), message_ref, wide)


def middle_kernel(
    mix_ref, pair_ref, normed0_ref, proj_ref, gate_ref, out_ref,
    message_ref, mix_normed_ref, mix_inverse_ref, product_ref, gating0_ref, after_ref, normed_ref, inverse_ref, kept_ref,
    gating_ref, narrow, wide,
):
    (mix,) = unpack(mix_ref, narrow, 1)
    mix_normed, mix_inverse = norm_parts(mix)
    mix_normed_ref[...] = mix_normed
    mix_inverse_ref[...] = mix_inverse
    product = dot(out_ref[0], mix_normed.astype(BF16), 0, 0)
    product_ref[...] = product
    gating0 = sigmoid(dot(gate_ref[0], normed0_ref[...].astype(BF16), 0, 0))
    gating0_ref[...] = gating0
    after = (pair_ref[...].astype(F32) + gating0 * product).astype(BF16)
    after_ref[...] = after
    pair_normed, inverse = norm_parts(after.astype(F32))
    normed_ref[...] = pair_normed
    inverse_ref[...] = inverse
    normed = pair_normed.astype(BF16)
    pack(edges(normed, proj_ref[1], kept_ref), message_ref, wide)
    gating_ref[...] = sigmoid(dot(gate_ref[1], normed, 0, 0))


def turn_kernel(
    mix_ref, after_ref, gating_ref, cot_ref, out_ref, normed_ref,
    pair_out_hbm, message_ref, cot_out_ref, gate_up_ref, gate_part_ref, out_part_ref, narrow, pair_out, sem,
):
    (mix,) = unpack(mix_ref, narrow, 1)
    mix_normed, mix_inverse = norm_parts(mix)
    normed_mix = mix_normed.astype(BF16)
    product = dot(out_ref[1], normed_mix, 0, 0)
    gating = gating_ref[...]
    pair_out[...] = block_out_exact((after_ref[...].astype(F32) + gating * product).astype(BF16))
    copy = pltpu.make_async_copy(pair_out, pair_out_hbm, sem)
    copy.start()
    cot = block_in(cot_ref)
    cot_out_ref[...] = cot.astype(BF16)
    mix_grad, out_part, gate_up = back_head(cot, gating, product, normed_mix, mix_normed, mix_inverse, out_ref[1])
    pack([mix_grad], message_ref, narrow)
    out_part_ref[...] = out_part
    gate_up_ref[...] = gate_up
    gate_part_ref[...] = dot(normed_ref[...].astype(BF16), gate_up, 1, 1)
    copy.wait()


def back_kernel(
    grads_ref, cot_ref, normed1_ref, inverse1_ref, kept1_ref, gate_up1_ref, mix_normed_ref, mix_inverse_ref,
    product_ref, gating0_ref, proj_ref, gate_ref, out_ref,
    message_ref, upstream_ref, gate_up_ref, proj_part_ref, out_part_ref, narrow, wide,
):
    left_grad, right_grad = unpack(grads_ref, wide, 2)
    pair_normed = normed1_ref[...]
    upstream, proj_up = back_tail(
        cot_ref[...].astype(F32), pair_normed, inverse1_ref[...], kept1_ref, left_grad, right_grad, gate_up1_ref[...],
        proj_ref[1], gate_ref[1],
    )
    upstream_ref[...] = upstream
    proj_part_ref[...] = dot(pair_normed.astype(BF16), proj_up, 1, 1)
    mix_normed = mix_normed_ref[...]
    mix_grad, out_part, gate_up = back_head(
        upstream, gating0_ref[...], product_ref[...], mix_normed.astype(BF16), mix_normed, mix_inverse_ref[...],
        out_ref[0],
    )
    pack([mix_grad], message_ref, narrow)
    out_part_ref[...] = out_part
    gate_up_ref[...] = gate_up


def last_kernel(
    grads_ref, upstream_ref, normed_ref, inverse_ref, kept_ref, gate_up_ref, proj_ref, gate_ref,
    proj1_ref, gate1_ref, out1_ref, out0_ref,
    pair_grad_hbm, message_ref, wide, pair_grad, sem,
):
    left_grad, right_grad = unpack(grads_ref, wide, 2)
    pair_normed = normed_ref[...]
    gate_up = gate_up_ref[...]
    total, proj_up = back_tail(
        upstream_ref[...], pair_normed, inverse_ref[...], kept_ref, left_grad, right_grad, gate_up,
        proj_ref[0], gate_ref[0],
    )
    pair_grad[...] = block_out(total)
    copy = pltpu.make_async_copy(pair_grad, pair_grad_hbm, sem)
    copy.start()
    normed = pair_normed.astype(BF16)
    proj_part = dot(normed, proj_up, 1, 1)
    parts = [proj_part[:, q * LANES : (q + 1) * LANES] for q in range(4)]
    parts += [proj1_ref[:, q * LANES : (q + 1) * LANES] for q in range(4)]
    parts += [dot(normed, gate_up, 1, 1), gate1_ref[...], out0_ref[...], out1_ref[...]]
    for q, part in enumerate(parts):
        message_ref[q * CHANNELS : (q + 1) * CHANNELS, :] = part.astype(BF16)
    copy.wait()


def sum_kernel(parts_ref, total_ref):
    pairs = parts_ref[...].astype(F32).reshape(DEVICES // 2, 2 * WEIGHTS, LANES)
    total = jnp.sum(pairs, axis=0)
    total = (total[:WEIGHTS] + total[WEIGHTS:]) * (1.0 / SIZE)
    total = jnp.concatenate([total, total], axis=0)[None]
    total_ref[...] = jnp.broadcast_to(total, pairs.shape).reshape(DEVICES * WEIGHTS, LANES).astype(BF16)


def spread_kernel(sums_ref, proj_hbm, gate_hbm, out_hbm, proj, gate, out, sems):
    parts = [sums_ref[q * CHANNELS : (q + 1) * CHANNELS, :].astype(F32) for q in range(WEIGHTS)]
    copies = []
    for l in range(2):
        proj[l] = jnp.concatenate(parts[4 * l : 4 * l + 4], axis=1)
        copies.append(pltpu.make_async_copy(proj.at[l], proj_hbm.at[l], sems.at[l]))
        copies[-1].start()
    for l in range(2):
        gate[l], out[l] = parts[8 + l], parts[10 + l]
    copies.append(pltpu.make_async_copy(gate, gate_hbm, sems.at[2]))
    copies.append(pltpu.make_async_copy(out, out_hbm, sems.at[3]))
    for copy in copies[2:]:
        copy.start()
    for copy in copies:
        copy.wait()


def outgoing_kernel(edges_ref, mix_ref, left_ref, right_ref, forth_ref):
    forth = first_to_second()
    forth_ref[...] = forth
    left, right = [matrix_of(pieces) for pieces in pieces_in(edges_ref, 2)]
    right = dot(forth, right, 1, 0).astype(BF16)
    left_ref[...], right_ref[...] = left, right
    pieces_out([pieces_of(dot(left, right, 1, 1))], mix_ref)


def incoming_kernel(edges_ref, mix_ref, left_ref, right_ref, back_ref):
    back = second_to_first()
    back_ref[...] = back
    left, right = [matrix_of(pieces) for pieces in pieces_in(edges_ref, 2)]
    left_ref[...], right_ref[...] = left, right
    turned = dot(back, left, 1, 1).astype(BF16)
    pieces_out([pieces_of(dot(turned, right, 1, 0))], mix_ref)


def incoming_back_kernel(grad_ref, forth_ref, left_ref, right_ref, grads_ref):
    grad = dot(forth_ref[...], matrix_of(pieces_in(grad_ref, 1)[0]), 1, 0).astype(BF16)
    pieces_out([pieces_of(dot(right_ref[...], grad, 1, 1)), pieces_of(dot(left_ref[...], grad, 1, 0))], grads_ref)


def outgoing_back_kernel(grad_ref, back_ref, left_ref, right_ref, grads_ref):
    grad = matrix_of(pieces_in(grad_ref, 1)[0])
    turned = dot(back_ref[...], grad, 1, 1).astype(BF16)
    pieces_out([pieces_of(dot(grad, right_ref[...], 1, 0)), pieces_of(dot(turned, left_ref[...], 1, 0))], grads_ref)


SINGLE_SHAPE = (DEVICES * SINGLE, LANES)
DOUBLE_SHAPE = (DEVICES * DOUBLE, LANES)
WEIGHTS_SHAPE = (DEVICES * WEIGHTS, LANES)
BLOCK = (ROWS * COLS, CHANNELS)
FLAT = (CHANNELS, TILES * LANES)
KEPT = (4, CHANNELS, TILES * LANES)
LINE = (1, TILES * LANES)
SQUARE = (WIDE, WIDE)
WEIGHT = (CHANNELS, CHANNELS)
PROJ = (CHANNELS, 4 * CHANNELS)
DMA = pltpu.SemaphoreType.DMA


def call(kernel, name, outs, scratch, *operands, far_out=()):
    def spec(far):
        return pl.BlockSpec(memory_space=pl.ANY if far else pltpu.VMEM)

    return pl.pallas_call(
        kernel,
        out_shape=[jax.ShapeDtypeStruct(shape, kind) for shape, kind in outs],
        in_specs=[spec(False) for _ in operands],
        out_specs=[spec(position in far_out) for position in range(len(outs))],
        scratch_shapes=scratch,
        compiler_params=pltpu.CompilerParams(vmem_limit_bytes=24 * 1024 * 1024),
        name=name,
    )(*operands)


def exchange(message):
    rows = message.shape[0] // DEVICES
    shape = (DEVICES, rows, LANES)
    for low in (4, 2):
        if rows % 8 and rows % low == 0:
            shape = (DEVICES, rows // low, low, LANES)
            break
    return lax.all_to_all(message.reshape(shape), AXES, 0, 0, tiled=True).reshape(message.shape)


def local(pair_rep, proj_weight, gate_weight, out_weight, pair_cot):
    pair = pair_rep.reshape(BLOCK)
    cot = pair_cot.reshape(BLOCK)
    double = pltpu.VMEM(DOUBLE_SHAPE, F32)
    spaced = pltpu.VMEM((DEVICES * (SINGLE + 1), LANES), F32)
    edges0, pair0, normed0, inverse0, kept0 = call(
        start_kernel, "start", [(DOUBLE_SHAPE, BF16), (FLAT, BF16), (FLAT, F32), (LINE, F32), (KEPT, F32)], [double],
        pair, proj_weight,
    )
    mix0, left0, right0, forth = call(
        outgoing_kernel, "outgoing", [(SINGLE_SHAPE, BF16), (SQUARE, BF16), (SQUARE, BF16), (SQUARE, BF16)], [],
        exchange(edges0),
    )
    edges1, mix_normed0, mix_inverse0, product0, gating0, after, normed1, inverse1, kept1, gating1 = call(
        middle_kernel, "middle",
        [
            (DOUBLE_SHAPE, BF16), (FLAT, F32), (LINE, F32), (FLAT, F32), (FLAT, F32), (FLAT, BF16), (FLAT, F32),
            (LINE, F32), (KEPT, F32), (FLAT, F32),
        ],
        [spaced, double], exchange(mix0), pair0, normed0, proj_weight, gate_weight, out_weight,
    )
    mix1, left1, right1, back = call(
        incoming_kernel, "incoming", [(SINGLE_SHAPE, BF16), (SQUARE, BF16), (SQUARE, BF16), (SQUARE, BF16)], [],
        exchange(edges1),
    )
    pair_out, grad1, cot1, gate_up1, gate_part1, out_part1 = call(
        turn_kernel, "turn",
        [(BLOCK, BF16), (SINGLE_SHAPE, BF16), (FLAT, BF16), (FLAT, BF16), (WEIGHT, F32), (WEIGHT, F32)],
        [spaced, pltpu.VMEM(BLOCK, BF16), DMA],
        exchange(mix1), after, gating1, cot, out_weight, normed1, far_out=(0,),
    )
    (grads1,) = call(
        incoming_back_kernel, "incoming_back", [(DOUBLE_SHAPE, BF16)], [], exchange(grad1), forth, left1, right1
    )
    grad0, upstream, gate_up0, proj_part1, out_part0 = call(
        back_kernel, "back",
        [(SINGLE_SHAPE, BF16), (FLAT, F32), (FLAT, BF16), (PROJ, F32), (WEIGHT, F32)],
        [spaced, double], exchange(grads1), cot1, normed1, inverse1, kept1, gate_up1, mix_normed0, mix_inverse0,
        product0, gating0, proj_weight, gate_weight, out_weight,
    )
    (grads0,) = call(
        outgoing_back_kernel, "outgoing_back", [(DOUBLE_SHAPE, BF16)], [], exchange(grad0), back, left0, right0
    )
    pair_grad, parts = call(
        last_kernel, "last", [(BLOCK, F32), (WEIGHTS_SHAPE, BF16)],
        [double, pltpu.VMEM(BLOCK, F32), DMA],
        exchange(grads0), upstream, normed0, inverse0, kept0, gate_up0, proj_weight, gate_weight,
        proj_part1, gate_part1, out_part1, out_part0, far_out=(0,),
    )
    (sums,) = call(sum_kernel, "sum", [(WEIGHTS_SHAPE, BF16)], [], exchange(parts))
    proj_grad, gate_grad, out_grad = call(
        spread_kernel, "spread", [((2,) + PROJ, F32), ((2,) + WEIGHT, F32), ((2,) + WEIGHT, F32)],
        [pltpu.VMEM((2,) + PROJ, F32), pltpu.VMEM((2,) + WEIGHT, F32), pltpu.VMEM((2,) + WEIGHT, F32), DMA((4,))],
        exchange(sums), far_out=(0, 1, 2),
    )
    return (
        pair_out.reshape(ROWS, COLS, CHANNELS),
        pair_grad.reshape(ROWS, COLS, CHANNELS),
        proj_grad,
        gate_grad,
        out_grad,
    )


def solution(mesh):
    in_specs = (P("row", "col", None), P(), P(), P(), P("row", "col", None))
    out_specs = (P("row", "col", None), P("row", "col", None), P(), P(), P())
    return jax.shard_map(local, mesh=mesh, in_specs=in_specs, out_specs=out_specs, check_vma=False)
```

```python
import jax
import jax.numpy as jnp
from jax import lax
from jax.experimental import pallas as pl
from jax.experimental.pallas import tpu as pltpu
from jax.sharding import PartitionSpec as P

EPSILON = 1e-05
F32 = jnp.float32
BF16 = jnp.bfloat16
AXES = ("row", "col")

PARTS_R, PARTS_C = 16, 8
DEVICES = PARTS_R * PARTS_C
ROWS, COLS, CHANNELS = 20, 40, 128
PER = 3
TILES = 7
SUBS = 8
LANES = 128
SIZE = 320
WIDE = 384
SINGLE, DOUBLE, WEIGHTS = 8, 14, 12


def dot(first_op, second_op, first_dim, second_dim):
    return lax.dot_general(
        first_op,
        second_op,
        (((first_dim,), (second_dim,)), ((), ())),
        preferred_element_type=F32,
    )


def mean0(values):
    return jnp.sum(values, axis=0, keepdims=True) * (1.0 / CHANNELS)


def norm_parts(values):
    centered = values - mean0(values)
    inverse = lax.rsqrt(mean0(centered * centered) + EPSILON)
    return centered * inverse, inverse


def norm_back(normed, inverse, upstream):
    return inverse * (upstream - mean0(upstream) - normed * mean0(upstream * normed))


def sigmoid(values):
    return 0.5 * jnp.tanh(0.5 * values) + 0.5


def identity():
    shape = (CHANNELS, CHANNELS)
    same = lax.broadcasted_iota(jnp.int32, shape, 0) == lax.broadcasted_iota(jnp.int32, shape, 1)
    return jnp.where(same, 1.0, 0.0).astype(BF16)


def block_in(ref):
    values = ref[...].astype(F32)
    pieces = []
    for s in range(TILES):
        low = s * PER * COLS
        high = min(low + PER * COLS, ROWS * COLS)
        pieces += [values[low:high], jnp.zeros((LANES - (high - low), CHANNELS), F32)]
    return dot(identity(), jnp.concatenate(pieces, axis=0).astype(BF16), 1, 1)


def block_out_exact(values):
    pieces = []
    for s in range(TILES):
        count = min(PER * COLS, ROWS * COLS - s * PER * COLS)
        pieces.append(dot(identity(), values[:, s * LANES : (s + 1) * LANES], 1, 1)[:count])
    return jnp.concatenate(pieces, axis=0).astype(BF16)


def rows_of(parts):
    return SINGLE if parts == 1 else DOUBLE


def pitch_of(parts):
    return SINGLE + 1 if parts == 1 else DOUBLE


def pack(parts, out_ref, wide):
    pitch = pitch_of(len(parts))
    for a, part in enumerate(parts):
        for s in range(TILES):
            wide[pl.ds(a * TILES + s, CHANNELS, stride=pitch), :] = part[:, s * LANES : (s + 1) * LANES]
    if len(parts) == 1:
        wide[pl.ds(TILES, CHANNELS, stride=pitch), :] = jnp.zeros((CHANNELS, LANES), F32)
        for d in range(0, CHANNELS, 2):
            two = [wide[e * pitch : e * pitch + SINGLE, :] for e in (d, d + 1)]
            out_ref[d * SINGLE : (d + 2) * SINGLE, :] = jnp.concatenate(two, axis=0).astype(BF16)
    else:
        out_ref[...] = wide[...].astype(BF16)


def unpack(ref, wide, count):
    pitch = pitch_of(count)
    if count == 1:
        for d in range(0, CHANNELS, 2):
            two = ref[d * SINGLE : (d + 2) * SINGLE, :].astype(F32)
            for e in range(2):
                wide[(d + e) * pitch : (d + e) * pitch + SINGLE, :] = two[e * SINGLE : (e + 1) * SINGLE]
    else:
        wide[...] = ref[...].astype(F32)
    return [
        jnp.concatenate([wide[pl.ds(a * TILES + s, CHANNELS, stride=pitch), :] for s in range(TILES)], axis=1)
        for a in range(count)
    ]


def pieces_in(ref, count):
    values = ref[...].astype(F32).reshape(PARTS_R, -1, SUBS, LANES)
    if count == 1:
        return [[values[:, c].reshape(LANES, LANES) for c in range(PARTS_C)]]
    sub = lax.broadcasted_iota(jnp.int32, (PARTS_R, SUBS, LANES), 1)
    parts = []
    for a in range(count):
        parts.append([])
        for c in range(PARTS_C):
            tile, shift = divmod(c * DOUBLE + a * TILES, SUBS)
            piece = values[:, tile]
            if shift + TILES > SUBS:
                piece = jnp.where(sub >= shift, piece, values[:, tile + 1])
            if shift:
                piece = pltpu.roll(piece, SUBS - shift, 1)
            parts[a].append(jnp.where(sub < TILES, piece, 0.0).reshape(LANES, LANES))
    return parts


def matrix_of(pieces):
    lane = lax.broadcasted_iota(jnp.int32, (LANES, LANES), 1)
    pieces = [piece.astype(BF16) for piece in pieces]
    rows = []
    for t in range(PER):
        turned = [
            pltpu.roll(pieces[c], ((c - t) * COLS) % LANES, 1) if (c - t) * COLS % LANES else pieces[c]
            for c in range(PARTS_C)
        ]
        tiles = []
        for q in range(WIDE // LANES):
            low, high = q * LANES, (q + 1) * LANES
            inside = [c for c in range(PARTS_C) if c * COLS < high and (c + 1) * COLS > low]
            tile = turned[inside[0]]
            for c in inside[1:]:
                tile = jnp.where(lane >= c * COLS - low, turned[c], tile)
            if high > SIZE:
                tile = jnp.where(lane < SIZE - low, tile, jnp.zeros_like(tile))
            tiles.append(tile)
        rows.append(jnp.concatenate(tiles, axis=1))
    return jnp.concatenate(rows, axis=0)


def pieces_of(values):
    values = values.astype(BF16)
    lane = lax.broadcasted_iota(jnp.int32, (LANES, LANES), 1)
    pieces = []
    for c in range(PARTS_C):
        low = c * COLS
        first, last = low // LANES, (low + COLS - 1) // LANES
        piece = None
        for t in range(PER):
            band = values[t * LANES : (t + 1) * LANES]
            source = band[:, first * LANES : (first + 1) * LANES]
            if last != first:
                source = jnp.where(lane >= low % LANES, source, band[:, last * LANES : (last + 1) * LANES])
            shift = ((t - c) * COLS) % LANES
            if shift:
                source = pltpu.roll(source, shift, 1)
            piece = source if piece is None else jnp.where(lane >= t * COLS, source, piece)
        pieces.append(jnp.where(lane < PER * COLS, piece, jnp.zeros_like(piece)).astype(F32))
    return pieces


def pieces_out(parts, ref):
    if len(parts) == 1:
        tiles = [piece.reshape(PARTS_R, SUBS, LANES) for piece in parts[0]]
    else:
        sub = lax.broadcasted_iota(jnp.int32, (PARTS_R, SUBS, LANES), 1)
        tiles = [None] * (PARTS_C * DOUBLE // SUBS)
        for c in range(PARTS_C):
            for a, pieces in enumerate(parts):
                tile, shift = divmod(c * DOUBLE + a * TILES, SUBS)
                piece = pieces[c].reshape(PARTS_R, SUBS, LANES)
                if shift:
                    piece = pltpu.roll(piece, shift, 1)
                tiles[tile] = piece if tiles[tile] is None else jnp.where(sub >= shift, piece, tiles[tile])
                if shift + TILES > SUBS:
                    tiles[tile + 1] = piece
    values = jnp.concatenate([tile[:, None] for tile in tiles], axis=1)
    ref[...] = values.reshape(-1, LANES).astype(BF16)


def first_to_second():
    index = lax.broadcasted_iota(jnp.int32, (1, WIDE), 1)
    part, s, t = (index % LANES) // SUBS, index % SUBS, index // LANES
    inner = PER * s + t
    residue = jnp.where((s < TILES) & (inner < ROWS), part * ROWS + inner, -1)
    second = lax.broadcasted_iota(jnp.int32, (WIDE, WIDE), 0)
    return jnp.where(second == residue, 1.0, 0.0).astype(BF16)


def second_to_first():
    index = lax.broadcasted_iota(jnp.int32, (WIDE, 1), 0)
    part, s, t = (index % LANES) // SUBS, index % SUBS, index // LANES
    inner = PER * s + t
    residue = jnp.where((s < TILES) & (inner < ROWS), part * ROWS + inner, -1)
    second = lax.broadcasted_iota(jnp.int32, (WIDE, WIDE), 1)
    return jnp.where(second == residue, 1.0, 0.0).astype(BF16)


def edges(normed, proj_mat, kept_ref):
    projected = dot(proj_mat, normed, 0, 0)
    p1, p2, p3, p4 = [projected[q * CHANNELS : (q + 1) * CHANNELS] for q in range(4)]
    s1, s3 = sigmoid(p1), sigmoid(p3)
    left, right = s1 * p2, s3 * p4
    for q, value in enumerate((s1, left, s3, right)):
        kept_ref[q] = value
    return left, right


def back_head(upstream, gating, product, normed_mix, mix_normed, mix_inverse, out_mat):
    through = (upstream * gating).astype(BF16)
    gate_up = (upstream * product * gating * (1.0 - gating)).astype(BF16)
    mix_up = dot(out_mat, through, 1, 0)
    out_part = dot(normed_mix, through, 1, 1)
    return norm_back(mix_normed, mix_inverse, mix_up), out_part, gate_up


def back_tail(upstream, pair_normed, pair_inverse, kept_ref, left_grad, right_grad, gate_up, proj_mat, gate_mat):
    s1, left, s3, right = [kept_ref[q] for q in range(4)]
    proj_up = jnp.concatenate(
        [left_grad * left * (1.0 - s1), left_grad * s1, right_grad * right * (1.0 - s3), right_grad * s3], axis=0
    ).astype(BF16)
    normed_up = dot(proj_mat, proj_up, 1, 0) + dot(gate_mat, gate_up, 1, 0)
    return upstream + norm_back(pair_normed, pair_inverse, normed_up), proj_up


def start_kernel(pair_ref, proj_ref, _, message_ref, flat_ref, normed_ref, inverse_ref, kept_ref, wide):
    pair = block_in(pair_ref)
    flat_ref[...] = pair.astype(BF16)
    pair_normed, inverse = norm_parts(pair)
    normed_ref[...] = pair_normed
    inverse_ref[...] = inverse
    pack(edges(pair_normed.astype(BF16), proj_ref[0], kept_ref), message_ref, wide)


def middle_kernel(
    mix_ref, pair_ref, normed0_ref, proj_ref, gate_ref, out_ref,
    message_ref, mix_normed_ref, mix_inverse_ref, product_ref, gating0_ref, after_ref, normed_ref, inverse_ref, kept_ref,
    gating_ref, narrow, wide,
):
    (mix,) = unpack(mix_ref, narrow, 1)
    mix_normed, mix_inverse = norm_parts(mix)
    mix_normed_ref[...] = mix_normed
    mix_inverse_ref[...] = mix_inverse
    product = dot(out_ref[0], mix_normed.astype(BF16), 0, 0)
    product_ref[...] = product
    gating0 = sigmoid(dot(gate_ref[0], normed0_ref[...].astype(BF16), 0, 0))
    gating0_ref[...] = gating0
    after = (pair_ref[...].astype(F32) + gating0 * product).astype(BF16)
    after_ref[...] = after
    pair_normed, inverse = norm_parts(after.astype(F32))
    normed_ref[...] = pair_normed
    inverse_ref[...] = inverse
    normed = pair_normed.astype(BF16)
    pack(edges(normed, proj_ref[1], kept_ref), message_ref, wide)
    gating_ref[...] = sigmoid(dot(gate_ref[1], normed, 0, 0))


def turn_kernel(
    mix_ref, after_ref, gating_ref, cot_ref, out_ref, normed_ref,
    pair_out_ref, message_ref, cot_out_ref, gate_up_ref, gate_part_ref, out_part_ref, narrow,
):
    (mix,) = unpack(mix_ref, narrow, 1)
    mix_normed, mix_inverse = norm_parts(mix)
    normed_mix = mix_normed.astype(BF16)
    product = dot(out_ref[1], normed_mix, 0, 0)
    gating = gating_ref[...]
    pair_out_ref[...] = (after_ref[...].astype(F32) + gating * product).astype(BF16)
    cot = block_in(cot_ref)
    cot_out_ref[...] = cot.astype(BF16)
    mix_grad, out_part, gate_up = back_head(cot, gating, product, normed_mix, mix_normed, mix_inverse, out_ref[1])
    pack([mix_grad], message_ref, narrow)
    out_part_ref[...] = out_part
    gate_up_ref[...] = gate_up
    gate_part_ref[...] = dot(normed_ref[...].astype(BF16), gate_up, 1, 1)


def back_kernel(
    grads_ref, cot_ref, normed1_ref, inverse1_ref, kept1_ref, gate_up1_ref, mix_normed_ref, mix_inverse_ref,
    product_ref, gating0_ref, proj_ref, gate_ref, out_ref,
    message_ref, upstream_ref, gate_up_ref, proj_part_ref, out_part_ref, narrow, wide,
):
    left_grad, right_grad = unpack(grads_ref, wide, 2)
    pair_normed = normed1_ref[...]
    upstream, proj_up = back_tail(
        cot_ref[...].astype(F32), pair_normed, inverse1_ref[...], kept1_ref, left_grad, right_grad, gate_up1_ref[...],
        proj_ref[1], gate_ref[1],
    )
    upstream_ref[...] = upstream
    proj_part_ref[...] = dot(pair_normed.astype(BF16), proj_up, 1, 1)
    mix_normed = mix_normed_ref[...]
    mix_grad, out_part, gate_up = back_head(
        upstream, gating0_ref[...], product_ref[...], mix_normed.astype(BF16), mix_normed, mix_inverse_ref[...],
        out_ref[0],
    )
    pack([mix_grad], message_ref, narrow)
    out_part_ref[...] = out_part
    gate_up_ref[...] = gate_up


def last_kernel(
    grads_ref, upstream_ref, normed_ref, inverse_ref, kept_ref, gate_up_ref, proj_ref, gate_ref,
    proj1_ref, gate1_ref, out1_ref, out0_ref,
    pair_grad_ref, message_ref, wide,
):
    left_grad, right_grad = unpack(grads_ref, wide, 2)
    pair_normed = normed_ref[...]
    gate_up = gate_up_ref[...]
    total, proj_up = back_tail(
        upstream_ref[...], pair_normed, inverse_ref[...], kept_ref, left_grad, right_grad, gate_up,
        proj_ref[0], gate_ref[0],
    )
    pair_grad_ref[...] = total
    normed = pair_normed.astype(BF16)
    proj_part = dot(normed, proj_up, 1, 1)
    parts = [proj_part[:, q * LANES : (q + 1) * LANES] for q in range(4)]
    parts += [proj1_ref[:, q * LANES : (q + 1) * LANES] for q in range(4)]
    parts += [dot(normed, gate_up, 1, 1), gate1_ref[...], out0_ref[...], out1_ref[...]]
    for q, part in enumerate(parts):
        message_ref[q * CHANNELS : (q + 1) * CHANNELS, :] = part.astype(BF16)


def sum_kernel(parts_ref, total_ref):
    pairs = parts_ref[...].astype(F32).reshape(DEVICES // 2, 2 * WEIGHTS, LANES)
    total = jnp.sum(pairs, axis=0)
    total = (total[:WEIGHTS] + total[WEIGHTS:]) * (1.0 / SIZE)
    total = jnp.concatenate([total, total], axis=0)[None]
    total_ref[...] = jnp.broadcast_to(total, pairs.shape).reshape(DEVICES * WEIGHTS, LANES).astype(BF16)


def spread_kernel(
    sums_ref, pair_out_ref, pair_grad_ref, proj_hbm, gate_hbm, out_hbm, pair_out_hbm, pair_grad_hbm,
    proj, gate, out, pair_out, pair_grad, sems,
):
    copies = []

    def send(source, target):
        copies.append(pltpu.make_async_copy(source, target, sems.at[len(copies)]))
        copies[-1].start()

    parts = [sums_ref[q * CHANNELS : (q + 1) * CHANNELS, :].astype(F32) for q in range(WEIGHTS)]
    for l in range(2):
        proj[l] = jnp.concatenate(parts[4 * l : 4 * l + 4], axis=1)
        send(proj.at[l], proj_hbm.at[l])
    for l in range(2):
        gate[l], out[l] = parts[8 + l], parts[10 + l]
    send(gate, gate_hbm)
    send(out, out_hbm)
    for s in range(TILES):
        low = s * PER * COLS
        count = min(PER * COLS, ROWS * COLS - low)
        pair_grad[low : low + count, :] = pair_grad_ref[:, s * LANES : (s + 1) * LANES].T[:count]
        send(pair_grad.at[pl.ds(low, count)], pair_grad_hbm.at[pl.ds(low, count)])
    pair_out[...] = block_out_exact(pair_out_ref[...])
    send(pair_out, pair_out_hbm)
    for copy in copies:
        copy.wait()


def orders_kernel(forth_ref, back_ref):
    forth_ref[...] = first_to_second()
    back_ref[...] = second_to_first()


def outgoing_kernel(edges_ref, forth_ref, mix_ref, left_ref, right_ref):
    left, right = [matrix_of(pieces) for pieces in pieces_in(edges_ref, 2)]
    right = dot(forth_ref[...], right, 1, 0).astype(BF16)
    left_ref[...], right_ref[...] = left, right
    pieces_out([pieces_of(dot(left, right, 1, 1))], mix_ref)


def incoming_kernel(edges_ref, back_ref, mix_ref, left_ref, right_ref):
    left, right = [matrix_of(pieces) for pieces in pieces_in(edges_ref, 2)]
    left_ref[...], right_ref[...] = left, right
    turned = dot(back_ref[...], left, 1, 1).astype(BF16)
    pieces_out([pieces_of(dot(turned, right, 1, 0))], mix_ref)


def incoming_back_kernel(grad_ref, forth_ref, left_ref, right_ref, grads_ref):
    grad = dot(forth_ref[...], matrix_of(pieces_in(grad_ref, 1)[0]), 1, 0).astype(BF16)
    pieces_out([pieces_of(dot(right_ref[...], grad, 1, 1)), pieces_of(dot(left_ref[...], grad, 1, 0))], grads_ref)


def outgoing_back_kernel(grad_ref, back_ref, left_ref, right_ref, grads_ref):
    grad = matrix_of(pieces_in(grad_ref, 1)[0])
    turned = dot(back_ref[...], grad, 1, 1).astype(BF16)
    pieces_out([pieces_of(dot(grad, right_ref[...], 1, 0)), pieces_of(dot(turned, left_ref[...], 1, 0))], grads_ref)


SINGLE_SHAPE = (DEVICES * SINGLE, LANES)
DOUBLE_SHAPE = (DEVICES * DOUBLE, LANES)
WEIGHTS_SHAPE = (DEVICES * WEIGHTS, LANES)
BLOCK = (ROWS * COLS, CHANNELS)
FLAT = (CHANNELS, TILES * LANES)
KEPT = (4, CHANNELS, TILES * LANES)
LINE = (1, TILES * LANES)
SQUARE = (WIDE, WIDE)
WEIGHT = (CHANNELS, CHANNELS)
PROJ = (CHANNELS, 4 * CHANNELS)
DMA = pltpu.SemaphoreType.DMA


def call(kernel, name, outs, scratch, *operands, far_out=(), flops=None):
    def spec(far):
        return pl.BlockSpec(memory_space=pl.ANY if far else pltpu.VMEM)

    return pl.pallas_call(
        kernel,
        out_shape=[jax.ShapeDtypeStruct(shape, kind) for shape, kind in outs],
        in_specs=[spec(False) for _ in operands],
        out_specs=[spec(position in far_out) for position in range(len(outs))],
        scratch_shapes=scratch,
        cost_estimate=flops and pl.CostEstimate(flops=flops, bytes_accessed=0, transcendentals=0),
        compiler_params=pltpu.CompilerParams(vmem_limit_bytes=24 * 1024 * 1024),
        name=name,
    )(*operands)


def exchange(message):
    rows = message.shape[0] // DEVICES
    shape = (DEVICES, rows, LANES)
    for low in (4, 2):
        if rows % 8 and rows % low == 0:
            shape = (DEVICES, rows // low, low, LANES)
            break
    return lax.all_to_all(message.reshape(shape), AXES, 0, 0, tiled=True).reshape(message.shape)


def local(pair_rep, proj_weight, gate_weight, out_weight, pair_cot):
    pair = pair_rep.reshape(BLOCK)
    cot = pair_cot.reshape(BLOCK)
    double = pltpu.VMEM(DOUBLE_SHAPE, F32)
    spaced = pltpu.VMEM((DEVICES * (SINGLE + 1), LANES), F32)
    forth, back = call(orders_kernel, "orders", [(SQUARE, BF16), (SQUARE, BF16)], [], flops=4 * 1024**3)
    edges0, pair0, normed0, inverse0, kept0 = call(
        start_kernel, "start", [(DOUBLE_SHAPE, BF16), (FLAT, BF16), (FLAT, F32), (LINE, F32), (KEPT, F32)], [double],
        pair, proj_weight, forth,
    )
    mix0, left0, right0 = call(
        outgoing_kernel, "outgoing", [(SINGLE_SHAPE, BF16), (SQUARE, BF16), (SQUARE, BF16)], [],
        exchange(edges0), forth,
    )
    edges1, mix_normed0, mix_inverse0, product0, gating0, after, normed1, inverse1, kept1, gating1 = call(
        middle_kernel, "middle",
        [
            (DOUBLE_SHAPE, BF16), (FLAT, F32), (LINE, F32), (FLAT, F32), (FLAT, F32), (FLAT, BF16), (FLAT, F32),
            (LINE, F32), (KEPT, F32), (FLAT, F32),
        ],
        [spaced, double], exchange(mix0), pair0, normed0, proj_weight, gate_weight, out_weight,
    )
    mix1, left1, right1 = call(
        incoming_kernel, "incoming", [(SINGLE_SHAPE, BF16), (SQUARE, BF16), (SQUARE, BF16)], [],
        exchange(edges1), back,
    )
    pair_out, grad1, cot1, gate_up1, gate_part1, out_part1 = call(
        turn_kernel, "turn",
        [(FLAT, BF16), (SINGLE_SHAPE, BF16), (FLAT, BF16), (FLAT, BF16), (WEIGHT, F32), (WEIGHT, F32)],
        [spaced], exchange(mix1), after, gating1, cot, out_weight, normed1,
    )
    (grads1,) = call(
        incoming_back_kernel, "incoming_back", [(DOUBLE_SHAPE, BF16)], [], exchange(grad1), forth, left1, right1
    )
    grad0, upstream, gate_up0, proj_part1, out_part0 = call(
        back_kernel, "back",
        [(SINGLE_SHAPE, BF16), (FLAT, F32), (FLAT, BF16), (PROJ, F32), (WEIGHT, F32)],
        [spaced, double], exchange(grads1), cot1, normed1, inverse1, kept1, gate_up1, mix_normed0, mix_inverse0,
        product0, gating0, proj_weight, gate_weight, out_weight,
    )
    (grads0,) = call(
        outgoing_back_kernel, "outgoing_back", [(DOUBLE_SHAPE, BF16)], [], exchange(grad0), back, left0, right0
    )
    pair_grad, parts = call(
        last_kernel, "last", [(FLAT, F32), (WEIGHTS_SHAPE, BF16)], [double],
        exchange(grads0), upstream, normed0, inverse0, kept0, gate_up0, proj_weight, gate_weight,
        proj_part1, gate_part1, out_part1, out_part0,
    )
    (sums,) = call(sum_kernel, "sum", [(WEIGHTS_SHAPE, BF16)], [], exchange(parts))
    outs = [((2,) + PROJ, F32), ((2,) + WEIGHT, F32), ((2,) + WEIGHT, F32), (BLOCK, BF16), (BLOCK, F32)]
    proj_grad, gate_grad, out_grad, pair_out, pair_grad = call(
        spread_kernel, "spread", outs, [pltpu.VMEM(shape, kind) for shape, kind in outs] + [DMA((5 + TILES,))],
        exchange(sums), pair_out, pair_grad, far_out=range(5),
    )
    return (
        pair_out.reshape(ROWS, COLS, CHANNELS),
        pair_grad.reshape(ROWS, COLS, CHANNELS),
        proj_grad,
        gate_grad,
        out_grad,
    )


def solution(mesh):
    in_specs = (P("row", "col", None), P(), P(), P(), P("row", "col", None))
    out_specs = (P("row", "col", None), P("row", "col", None), P(), P(), P())
    return jax.shard_map(local, mesh=mesh, in_specs=in_specs, out_specs=out_specs, check_vma=False)
```

```python
import jax
import jax.numpy as jnp
from jax import lax
from jax.experimental import pallas as pl
from jax.experimental.pallas import tpu as pltpu
from jax.sharding import PartitionSpec as P

EPSILON = 1e-05
F32 = jnp.float32
BF16 = jnp.bfloat16
AXES = ("row", "col")

PARTS_R, PARTS_C = 16, 8
DEVICES = PARTS_R * PARTS_C
ROWS, COLS, CHANNELS = 20, 40, 128
PER = 3
TILES = 7
SUBS = 8
LANES = 128
SIZE = 320
WIDE = 384
SINGLE, DOUBLE, WEIGHTS = 8, 14, 12


def dot(first_op, second_op, first_dim, second_dim):
    return lax.dot_general(
        first_op,
        second_op,
        (((first_dim,), (second_dim,)), ((), ())),
        preferred_element_type=F32,
    )


def mean0(values):
    return jnp.sum(values, axis=0, keepdims=True) * (1.0 / CHANNELS)


def norm_parts(values):
    centered = values - mean0(values)
    inverse = lax.rsqrt(mean0(centered * centered) + EPSILON)
    return centered * inverse, inverse


def norm_back(normed, inverse, upstream):
    return inverse * (upstream - mean0(upstream) - normed * mean0(upstream * normed))


def sigmoid(values):
    return 0.5 * jnp.tanh(0.5 * values) + 0.5


def identity():
    shape = (CHANNELS, CHANNELS)
    same = lax.broadcasted_iota(jnp.int32, shape, 0) == lax.broadcasted_iota(jnp.int32, shape, 1)
    return jnp.where(same, 1.0, 0.0).astype(BF16)


def block_in(ref):
    values = ref[...].astype(F32)
    pieces = []
    for s in range(TILES):
        low = s * PER * COLS
        high = min(low + PER * COLS, ROWS * COLS)
        pieces += [values[low:high], jnp.zeros((LANES - (high - low), CHANNELS), F32)]
    return dot(identity(), jnp.concatenate(pieces, axis=0).astype(BF16), 1, 1)


def block_out_exact(values):
    pieces = []
    for s in range(TILES):
        count = min(PER * COLS, ROWS * COLS - s * PER * COLS)
        pieces.append(dot(identity(), values[:, s * LANES : (s + 1) * LANES], 1, 1)[:count])
    return jnp.concatenate(pieces, axis=0).astype(BF16)


def rows_of(parts):
    return SINGLE if parts == 1 else DOUBLE


def pitch_of(parts):
    return SINGLE + 1 if parts == 1 else DOUBLE


def pack(parts, out_ref, wide):
    pitch = pitch_of(len(parts))
    for a, part in enumerate(parts):
        for s in range(TILES):
            wide[pl.ds(a * TILES + s, CHANNELS, stride=pitch), :] = part[:, s * LANES : (s + 1) * LANES]
    if len(parts) == 1:
        wide[pl.ds(TILES, CHANNELS, stride=pitch), :] = jnp.zeros((CHANNELS, LANES), F32)
        for d in range(0, CHANNELS, 2):
            two = [wide[e * pitch : e * pitch + SINGLE, :] for e in (d, d + 1)]
            out_ref[d * SINGLE : (d + 2) * SINGLE, :] = jnp.concatenate(two, axis=0).astype(BF16)
    else:
        out_ref[...] = wide[...].astype(BF16)


def unpack(ref, wide, count):
    pitch = pitch_of(count)
    if count == 1:
        for d in range(0, CHANNELS, 2):
            two = ref[d * SINGLE : (d + 2) * SINGLE, :].astype(F32)
            for e in range(2):
                wide[(d + e) * pitch : (d + e) * pitch + SINGLE, :] = two[e * SINGLE : (e + 1) * SINGLE]
    else:
        wide[...] = ref[...].astype(F32)
    return [
        jnp.concatenate([wide[pl.ds(a * TILES + s, CHANNELS, stride=pitch), :] for s in range(TILES)], axis=1)
        for a in range(count)
    ]


def pieces_in(ref, count, clean=()):
    values = ref[...].astype(F32).reshape(PARTS_R, -1, SUBS, LANES)
    if count == 1:
        return [[values[:, c].reshape(LANES, LANES) for c in range(PARTS_C)]]
    sub = lax.broadcasted_iota(jnp.int32, (PARTS_R, SUBS, LANES), 1)
    parts = []
    for a in range(count):
        parts.append([])
        for c in range(PARTS_C):
            tile, shift = divmod(c * DOUBLE + a * TILES, SUBS)
            piece = values[:, tile]
            if shift + TILES > SUBS:
                piece = jnp.where(sub >= shift, piece, values[:, tile + 1])
            if shift:
                piece = pltpu.roll(piece, SUBS - shift, 1)
            if a in clean:
                piece = jnp.where(sub < TILES, piece, 0.0)
            parts[a].append(piece.reshape(LANES, LANES))
    return parts


def matrix_of(pieces):
    lane = lax.broadcasted_iota(jnp.int32, (LANES, LANES), 1)
    pieces = [piece.astype(BF16) for piece in pieces]
    rows = []
    for t in range(PER):
        turned = [
            pltpu.roll(pieces[c], ((c - t) * COLS) % LANES, 1) if (c - t) * COLS % LANES else pieces[c]
            for c in range(PARTS_C)
        ]
        tiles = []
        for q in range(WIDE // LANES):
            low, high = q * LANES, (q + 1) * LANES
            inside = [c for c in range(PARTS_C) if c * COLS < high and (c + 1) * COLS > low]
            tile = turned[inside[0]]
            for c in inside[1:]:
                tile = jnp.where(lane >= c * COLS - low, turned[c], tile)
            if high > SIZE:
                tile = jnp.where(lane < SIZE - low, tile, jnp.zeros_like(tile))
            tiles.append(tile)
        rows.append(jnp.concatenate(tiles, axis=1))
    return jnp.concatenate(rows, axis=0)


def pieces_of(values):
    values = values.astype(BF16)
    lane = lax.broadcasted_iota(jnp.int32, (LANES, LANES), 1)
    pieces = []
    for c in range(PARTS_C):
        low = c * COLS
        first, last = low // LANES, (low + COLS - 1) // LANES
        piece = None
        for t in range(PER):
            band = values[t * LANES : (t + 1) * LANES]
            source = band[:, first * LANES : (first + 1) * LANES]
            if last != first:
                source = jnp.where(lane >= low % LANES, source, band[:, last * LANES : (last + 1) * LANES])
            shift = ((t - c) * COLS) % LANES
            if shift:
                source = pltpu.roll(source, shift, 1)
            piece = source if piece is None else jnp.where(lane >= t * COLS, source, piece)
        pieces.append(jnp.where(lane < PER * COLS, piece, jnp.zeros_like(piece)).astype(F32))
    return pieces


def pieces_out(parts, ref):
    if len(parts) == 1:
        tiles = [piece.reshape(PARTS_R, SUBS, LANES) for piece in parts[0]]
    else:
        sub = lax.broadcasted_iota(jnp.int32, (PARTS_R, SUBS, LANES), 1)
        tiles = [None] * (PARTS_C * DOUBLE // SUBS)
        for c in range(PARTS_C):
            for a, pieces in enumerate(parts):
                tile, shift = divmod(c * DOUBLE + a * TILES, SUBS)
                piece = pieces[c].reshape(PARTS_R, SUBS, LANES)
                if shift:
                    piece = pltpu.roll(piece, shift, 1)
                tiles[tile] = piece if tiles[tile] is None else jnp.where(sub >= shift, piece, tiles[tile])
                if shift + TILES > SUBS:
                    tiles[tile + 1] = piece
    values = jnp.concatenate([tile[:, None] for tile in tiles], axis=1)
    ref[...] = values.reshape(-1, LANES).astype(BF16)


def first_to_second():
    index = lax.broadcasted_iota(jnp.int32, (1, WIDE), 1)
    part, s, t = (index % LANES) // SUBS, index % SUBS, index // LANES
    inner = PER * s + t
    residue = jnp.where((s < TILES) & (inner < ROWS), part * ROWS + inner, -1)
    second = lax.broadcasted_iota(jnp.int32, (WIDE, WIDE), 0)
    return jnp.where(second == residue, 1.0, 0.0).astype(BF16)


def second_to_first():
    index = lax.broadcasted_iota(jnp.int32, (WIDE, 1), 0)
    part, s, t = (index % LANES) // SUBS, index % SUBS, index // LANES
    inner = PER * s + t
    residue = jnp.where((s < TILES) & (inner < ROWS), part * ROWS + inner, -1)
    second = lax.broadcasted_iota(jnp.int32, (WIDE, WIDE), 1)
    return jnp.where(second == residue, 1.0, 0.0).astype(BF16)


def edges(normed, proj_mat, kept_ref):
    projected = dot(proj_mat, normed, 0, 0)
    p1, p2, p3, p4 = [projected[q * CHANNELS : (q + 1) * CHANNELS] for q in range(4)]
    s1, s3 = sigmoid(p1), sigmoid(p3)
    left, right = s1 * p2, s3 * p4
    for q, value in enumerate((s1, left, s3, right)):
        kept_ref[q] = value
    return left, right


def back_head(upstream, gating, product, normed_mix, mix_normed, mix_inverse, out_mat):
    through = (upstream * gating).astype(BF16)
    gate_up = (upstream * product * gating * (1.0 - gating)).astype(BF16)
    mix_up = dot(out_mat, through, 1, 0)
    out_part = dot(normed_mix, through, 1, 1)
    return norm_back(mix_normed, mix_inverse, mix_up), out_part, gate_up


def back_tail(upstream, pair_normed, pair_inverse, kept_ref, left_grad, right_grad, gate_up, proj_mat, gate_mat):
    s1, left, s3, right = [kept_ref[q] for q in range(4)]
    proj_up = jnp.concatenate(
        [left_grad * left * (1.0 - s1), left_grad * s1, right_grad * right * (1.0 - s3), right_grad * s3], axis=0
    ).astype(BF16)
    normed_up = dot(proj_mat, proj_up, 1, 0) + dot(gate_mat, gate_up, 1, 0)
    return upstream + norm_back(pair_normed, pair_inverse, normed_up), proj_up


def start_kernel(pair_ref, proj_ref, _, message_ref, flat_ref, normed_ref, inverse_ref, kept_ref, wide):
    pair = block_in(pair_ref)
    flat_ref[...] = pair.astype(BF16)
    pair_normed, inverse = norm_parts(pair)
    normed_ref[...] = pair_normed
    inverse_ref[...] = inverse
    pack(edges(pair_normed.astype(BF16), proj_ref[0], kept_ref), message_ref, wide)


def middle_kernel(
    mix_ref, pair_ref, normed0_ref, proj_ref, gate_ref, out_ref,
    message_ref, mix_normed_ref, mix_inverse_ref, product_ref, gating0_ref, after_ref, normed_ref, inverse_ref, kept_ref,
    gating_ref, narrow, wide,
):
    (mix,) = unpack(mix_ref, narrow, 1)
    mix_normed, mix_inverse = norm_parts(mix)
    mix_normed_ref[...] = mix_normed
    mix_inverse_ref[...] = mix_inverse
    product = dot(out_ref[0], mix_normed.astype(BF16), 0, 0)
    product_ref[...] = product
    gating0 = sigmoid(dot(gate_ref[0], normed0_ref[...].astype(BF16), 0, 0))
    gating0_ref[...] = gating0
    after = (pair_ref[...].astype(F32) + gating0 * product).astype(BF16)
    after_ref[...] = after
    pair_normed, inverse = norm_parts(after.astype(F32))
    normed_ref[...] = pair_normed
    inverse_ref[...] = inverse
    normed = pair_normed.astype(BF16)
    pack(edges(normed, proj_ref[1], kept_ref), message_ref, wide)
    gating_ref[...] = sigmoid(dot(gate_ref[1], normed, 0, 0))


def turn_kernel(
    mix_ref, after_ref, gating_ref, cot_ref, out_ref, normed_ref,
    pair_out_ref, message_ref, cot_out_ref, gate_up_ref, gate_part_ref, out_part_ref, narrow,
):
    (mix,) = unpack(mix_ref, narrow, 1)
    mix_normed, mix_inverse = norm_parts(mix)
    normed_mix = mix_normed.astype(BF16)
    product = dot(out_ref[1], normed_mix, 0, 0)
    gating = gating_ref[...]
    pair_out_ref[...] = (after_ref[...].astype(F32) + gating * product).astype(BF16)
    cot = block_in(cot_ref)
    cot_out_ref[...] = cot.astype(BF16)
    mix_grad, out_part, gate_up = back_head(cot, gating, product, normed_mix, mix_normed, mix_inverse, out_ref[1])
    pack([mix_grad], message_ref, narrow)
    out_part_ref[...] = out_part
    gate_up_ref[...] = gate_up
    gate_part_ref[...] = dot(normed_ref[...].astype(BF16), gate_up, 1, 1)


def back_kernel(
    grads_ref, cot_ref, normed1_ref, inverse1_ref, kept1_ref, gate_up1_ref, mix_normed_ref, mix_inverse_ref,
    product_ref, gating0_ref, proj_ref, gate_ref, out_ref, pair_out_ref,
    pair_out_hbm, message_ref, upstream_ref, gate_up_ref, proj_part_ref, out_part_ref, narrow, wide, pair_out, sem,
):
    pair_out[...] = block_out_exact(pair_out_ref[...])
    copy = pltpu.make_async_copy(pair_out, pair_out_hbm, sem)
    copy.start()
    left_grad, right_grad = unpack(grads_ref, wide, 2)
    pair_normed = normed1_ref[...]
    upstream, proj_up = back_tail(
        cot_ref[...].astype(F32), pair_normed, inverse1_ref[...], kept1_ref, left_grad, right_grad, gate_up1_ref[...],
        proj_ref[1], gate_ref[1],
    )
    upstream_ref[...] = upstream
    proj_part_ref[...] = dot(pair_normed.astype(BF16), proj_up, 1, 1)
    mix_normed = mix_normed_ref[...]
    mix_grad, out_part, gate_up = back_head(
        upstream, gating0_ref[...], product_ref[...], mix_normed.astype(BF16), mix_normed, mix_inverse_ref[...],
        out_ref[0],
    )
    pack([mix_grad], message_ref, narrow)
    out_part_ref[...] = out_part
    gate_up_ref[...] = gate_up
    copy.wait()


def last_kernel(
    grads_ref, upstream_ref, normed_ref, inverse_ref, kept_ref, gate_up_ref, proj_ref, gate_ref,
    proj1_ref, gate1_ref, out1_ref, out0_ref,
    pair_grad_ref, message_ref, wide,
):
    left_grad, right_grad = unpack(grads_ref, wide, 2)
    pair_normed = normed_ref[...]
    gate_up = gate_up_ref[...]
    total, proj_up = back_tail(
        upstream_ref[...], pair_normed, inverse_ref[...], kept_ref, left_grad, right_grad, gate_up,
        proj_ref[0], gate_ref[0],
    )
    pair_grad_ref[...] = total
    normed = pair_normed.astype(BF16)
    proj_part = dot(normed, proj_up, 1, 1)
    parts = [proj_part[:, q * LANES : (q + 1) * LANES] for q in range(4)]
    parts += [proj1_ref[:, q * LANES : (q + 1) * LANES] for q in range(4)]
    parts += [dot(normed, gate_up, 1, 1), gate1_ref[...], out0_ref[...], out1_ref[...]]
    for q, part in enumerate(parts):
        message_ref[q * CHANNELS : (q + 1) * CHANNELS, :] = part.astype(BF16)


def sum_kernel(parts_ref, total_ref):
    pairs = parts_ref[...].astype(F32).reshape(DEVICES // 2, 2 * WEIGHTS, LANES)
    total = jnp.sum(pairs, axis=0)
    total = (total[:WEIGHTS] + total[WEIGHTS:]) * (1.0 / SIZE)
    total = jnp.concatenate([total, total], axis=0)[None]
    total_ref[...] = jnp.broadcast_to(total, pairs.shape).reshape(DEVICES * WEIGHTS, LANES).astype(BF16)


def spread_kernel(
    sums_ref, pair_grad_ref, proj_hbm, gate_hbm, out_hbm, pair_grad_hbm, proj, gate, out, pair_grad, sems,
):
    copies = []

    def send(source, target):
        copies.append(pltpu.make_async_copy(source, target, sems.at[len(copies)]))
        copies[-1].start()

    parts = [sums_ref[q * CHANNELS : (q + 1) * CHANNELS, :].astype(F32) for q in range(WEIGHTS)]
    for l in range(2):
        proj[l] = jnp.concatenate(parts[4 * l : 4 * l + 4], axis=1)
        send(proj.at[l], proj_hbm.at[l])
    for l in range(2):
        gate[l], out[l] = parts[8 + l], parts[10 + l]
    send(gate, gate_hbm)
    send(out, out_hbm)
    for s in range(TILES):
        low = s * PER * COLS
        count = min(PER * COLS, ROWS * COLS - low)
        pair_grad[low : low + count, :] = pair_grad_ref[:, s * LANES : (s + 1) * LANES].T[:count]
        send(pair_grad.at[pl.ds(low, count)], pair_grad_hbm.at[pl.ds(low, count)])
    for copy in copies:
        copy.wait()


def orders_kernel(forth_ref, back_ref):
    forth_ref[...] = first_to_second()
    back_ref[...] = second_to_first()


def outgoing_kernel(edges_ref, forth_ref, mix_ref, left_ref, right_ref):
    left, right = [matrix_of(pieces) for pieces in pieces_in(edges_ref, 2)]
    right = dot(forth_ref[...], right, 1, 0).astype(BF16)
    left_ref[...], right_ref[...] = left, right
    pieces_out([pieces_of(dot(left, right, 1, 1))], mix_ref)


def incoming_kernel(edges_ref, back_ref, mix_ref, left_ref, right_ref):
    left, right = [matrix_of(pieces) for pieces in pieces_in(edges_ref, 2, (0,))]
    turned = dot(back_ref[...], left, 1, 1).astype(BF16)
    left_ref[...], right_ref[...] = turned, right
    pieces_out([pieces_of(dot(turned, right, 1, 0))], mix_ref)


def incoming_back_kernel(grad_ref, back_ref, left_ref, right_ref, grads_ref):
    grad = matrix_of(pieces_in(grad_ref, 1)[0])
    left_grad = dot(right_ref[...], grad, 1, 1).astype(BF16)
    right_grad = dot(left_ref[...], grad, 0, 0)
    pieces_out([pieces_of(dot(left_grad, back_ref[...], 1, 0)), pieces_of(right_grad)], grads_ref)


def outgoing_back_kernel(grad_ref, back_ref, left_ref, right_ref, grads_ref):
    grad = matrix_of(pieces_in(grad_ref, 1)[0])
    turned = dot(back_ref[...], grad, 1, 1).astype(BF16)
    pieces_out([pieces_of(dot(grad, right_ref[...], 1, 0)), pieces_of(dot(turned, left_ref[...], 1, 0))], grads_ref)


SINGLE_SHAPE = (DEVICES * SINGLE, LANES)
DOUBLE_SHAPE = (DEVICES * DOUBLE, LANES)
WEIGHTS_SHAPE = (DEVICES * WEIGHTS, LANES)
BLOCK = (ROWS * COLS, CHANNELS)
FLAT = (CHANNELS, TILES * LANES)
KEPT = (4, CHANNELS, TILES * LANES)
LINE = (1, TILES * LANES)
SQUARE = (WIDE, WIDE)
WEIGHT = (CHANNELS, CHANNELS)
PROJ = (CHANNELS, 4 * CHANNELS)
DMA = pltpu.SemaphoreType.DMA


def call(kernel, name, outs, scratch, *operands, far_out=(), flops=None):
    def spec(far):
        return pl.BlockSpec(memory_space=pl.ANY if far else pltpu.VMEM)

    return pl.pallas_call(
        kernel,
        out_shape=[jax.ShapeDtypeStruct(shape, kind) for shape, kind in outs],
        in_specs=[spec(False) for _ in operands],
        out_specs=[spec(position in far_out) for position in range(len(outs))],
        scratch_shapes=scratch,
        cost_estimate=flops and pl.CostEstimate(flops=flops, bytes_accessed=0, transcendentals=0),
        compiler_params=pltpu.CompilerParams(vmem_limit_bytes=24 * 1024 * 1024),
        name=name,
    )(*operands)


def exchange(message):
    rows = message.shape[0] // DEVICES
    shape = (DEVICES, rows, LANES)
    for low in (4, 2):
        if rows % 8 and rows % low == 0:
            shape = (DEVICES, rows // low, low, LANES)
            break
    return lax.all_to_all(message.reshape(shape), AXES, 0, 0, tiled=True).reshape(message.shape)


def local(pair_rep, proj_weight, gate_weight, out_weight, pair_cot):
    pair = pair_rep.reshape(BLOCK)
    cot = pair_cot.reshape(BLOCK)
    double = pltpu.VMEM(DOUBLE_SHAPE, F32)
    spaced = pltpu.VMEM((DEVICES * (SINGLE + 1), LANES), F32)
    forth, back = call(orders_kernel, "orders", [(SQUARE, BF16), (SQUARE, BF16)], [], flops=4 * 1024**3)
    edges0, pair0, normed0, inverse0, kept0 = call(
        start_kernel, "start", [(DOUBLE_SHAPE, BF16), (FLAT, BF16), (FLAT, F32), (LINE, F32), (KEPT, F32)], [double],
        pair, proj_weight, forth,
    )
    mix0, left0, right0 = call(
        outgoing_kernel, "outgoing", [(SINGLE_SHAPE, BF16), (SQUARE, BF16), (SQUARE, BF16)], [],
        exchange(edges0), forth,
    )
    edges1, mix_normed0, mix_inverse0, product0, gating0, after, normed1, inverse1, kept1, gating1 = call(
        middle_kernel, "middle",
        [
            (DOUBLE_SHAPE, BF16), (FLAT, F32), (LINE, F32), (FLAT, F32), (FLAT, F32), (FLAT, BF16), (FLAT, F32),
            (LINE, F32), (KEPT, F32), (FLAT, F32),
        ],
        [spaced, double], exchange(mix0), pair0, normed0, proj_weight, gate_weight, out_weight,
    )
    mix1, left1, right1 = call(
        incoming_kernel, "incoming", [(SINGLE_SHAPE, BF16), (SQUARE, BF16), (SQUARE, BF16)], [],
        exchange(edges1), back,
    )
    pair_out, grad1, cot1, gate_up1, gate_part1, out_part1 = call(
        turn_kernel, "turn",
        [(FLAT, BF16), (SINGLE_SHAPE, BF16), (FLAT, BF16), (FLAT, BF16), (WEIGHT, F32), (WEIGHT, F32)],
        [spaced], exchange(mix1), after, gating1, cot, out_weight, normed1,
    )
    (grads1,) = call(
        incoming_back_kernel, "incoming_back", [(DOUBLE_SHAPE, BF16)], [], exchange(grad1), back, left1, right1
    )
    pair_out, grad0, upstream, gate_up0, proj_part1, out_part0 = call(
        back_kernel, "back",
        [(BLOCK, BF16), (SINGLE_SHAPE, BF16), (FLAT, F32), (FLAT, BF16), (PROJ, F32), (WEIGHT, F32)],
        [spaced, double, pltpu.VMEM(BLOCK, BF16), DMA], exchange(grads1), cot1, normed1, inverse1, kept1, gate_up1, mix_normed0, mix_inverse0,
        product0, gating0, proj_weight, gate_weight, out_weight, pair_out, far_out=(0,),
    )
    (grads0,) = call(
        outgoing_back_kernel, "outgoing_back", [(DOUBLE_SHAPE, BF16)], [], exchange(grad0), back, left0, right0
    )
    pair_grad, parts = call(
        last_kernel, "last", [(FLAT, F32), (WEIGHTS_SHAPE, BF16)], [double],
        exchange(grads0), upstream, normed0, inverse0, kept0, gate_up0, proj_weight, gate_weight,
        proj_part1, gate_part1, out_part1, out_part0,
    )
    (sums,) = call(sum_kernel, "sum", [(WEIGHTS_SHAPE, BF16)], [], exchange(parts))
    outs = [((2,) + PROJ, F32), ((2,) + WEIGHT, F32), ((2,) + WEIGHT, F32), (BLOCK, F32)]
    proj_grad, gate_grad, out_grad, pair_grad = call(
        spread_kernel, "spread", outs, [pltpu.VMEM(shape, kind) for shape, kind in outs] + [DMA((4 + TILES,))],
        exchange(sums), pair_grad, far_out=range(4),
    )
    return (
        pair_out.reshape(ROWS, COLS, CHANNELS),
        pair_grad.reshape(ROWS, COLS, CHANNELS),
        proj_grad,
        gate_grad,
        out_grad,
    )


def solution(mesh):
    in_specs = (P("row", "col", None), P(), P(), P(), P("row", "col", None))
    out_specs = (P("row", "col", None), P("row", "col", None), P(), P(), P())
    return jax.shard_map(local, mesh=mesh, in_specs=in_specs, out_specs=out_specs, check_vma=False)
```

```python
import jax
import jax.numpy as jnp
from jax import lax
from jax.experimental import pallas as pl
from jax.experimental.pallas import tpu as pltpu
from jax.sharding import PartitionSpec as P

EPSILON = 1e-05
F32 = jnp.float32
BF16 = jnp.bfloat16
AXES = ("row", "col")

PARTS_R, PARTS_C = 16, 8
DEVICES = PARTS_R * PARTS_C
ROWS, COLS, CHANNELS = 20, 40, 128
PER = 3
TILES = 7
SUBS = 8
LANES = 128
SIZE = 320
WIDE = 384
SINGLE, DOUBLE, WEIGHTS = 8, 14, 12


def dot(first_op, second_op, first_dim, second_dim):
    return lax.dot_general(
        first_op,
        second_op,
        (((first_dim,), (second_dim,)), ((), ())),
        preferred_element_type=F32,
    )


def mean0(values):
    return jnp.sum(values, axis=0, keepdims=True) * (1.0 / CHANNELS)


def norm_parts(values):
    centered = values - mean0(values)
    inverse = lax.rsqrt(mean0(centered * centered) + EPSILON)
    return centered * inverse, inverse


def norm_back(normed, inverse, upstream):
    return inverse * (upstream - mean0(upstream) - normed * mean0(upstream * normed))


def sigmoid(values):
    return 0.5 * jnp.tanh(0.5 * values) + 0.5


def identity():
    shape = (CHANNELS, CHANNELS)
    same = lax.broadcasted_iota(jnp.int32, shape, 0) == lax.broadcasted_iota(jnp.int32, shape, 1)
    return jnp.where(same, 1.0, 0.0).astype(BF16)


def block_in(ref):
    values = ref[...].astype(F32)
    pieces = []
    for s in range(TILES):
        low = s * PER * COLS
        high = min(low + PER * COLS, ROWS * COLS)
        pieces += [values[low:high], jnp.zeros((LANES - (high - low), CHANNELS), F32)]
    return dot(identity(), jnp.concatenate(pieces, axis=0).astype(BF16), 1, 1)


def block_out_exact(values):
    pieces = []
    for s in range(TILES):
        count = min(PER * COLS, ROWS * COLS - s * PER * COLS)
        pieces.append(dot(identity(), values[:, s * LANES : (s + 1) * LANES], 1, 1)[:count])
    return jnp.concatenate(pieces, axis=0).astype(BF16)


def rows_of(parts):
    return SINGLE if parts == 1 else DOUBLE


def pitch_of(parts):
    return SINGLE + 1 if parts == 1 else DOUBLE


def pack(parts, out_ref, wide):
    pitch = pitch_of(len(parts))
    for a, part in enumerate(parts):
        for s in range(TILES):
            wide[pl.ds(a * TILES + s, CHANNELS, stride=pitch), :] = part[:, s * LANES : (s + 1) * LANES]
    if len(parts) == 1:
        wide[pl.ds(TILES, CHANNELS, stride=pitch), :] = jnp.zeros((CHANNELS, LANES), F32)
        for d in range(0, CHANNELS, 2):
            two = [wide[e * pitch : e * pitch + SINGLE, :] for e in (d, d + 1)]
            out_ref[d * SINGLE : (d + 2) * SINGLE, :] = jnp.concatenate(two, axis=0).astype(BF16)
    else:
        out_ref[...] = wide[: DEVICES * DOUBLE, :].astype(BF16)


def unpack(ref, wide, count):
    pitch = pitch_of(count)
    if count == 1:
        for d in range(0, CHANNELS, 2):
            two = ref[d * SINGLE : (d + 2) * SINGLE, :].astype(F32)
            for e in range(2):
                wide[(d + e) * pitch : (d + e) * pitch + SINGLE, :] = two[e * SINGLE : (e + 1) * SINGLE]
    else:
        wide[: DEVICES * DOUBLE, :] = ref[...].astype(F32)
    return [
        jnp.concatenate([wide[pl.ds(a * TILES + s, CHANNELS, stride=pitch), :] for s in range(TILES)], axis=1)
        for a in range(count)
    ]


def pieces_in(ref, count, clean=()):
    values = ref[...].astype(F32).reshape(PARTS_R, -1, SUBS, LANES)
    if count == 1:
        return [[values[:, c].reshape(LANES, LANES) for c in range(PARTS_C)]]
    sub = lax.broadcasted_iota(jnp.int32, (PARTS_R, SUBS, LANES), 1)
    parts = []
    for a in range(count):
        parts.append([])
        for c in range(PARTS_C):
            tile, shift = divmod(c * DOUBLE + a * TILES, SUBS)
            piece = values[:, tile]
            if shift + TILES > SUBS:
                piece = jnp.where(sub >= shift, piece, values[:, tile + 1])
            if shift:
                piece = pltpu.roll(piece, SUBS - shift, 1)
            if a in clean:
                piece = jnp.where(sub < TILES, piece, 0.0)
            parts[a].append(piece.reshape(LANES, LANES))
    return parts


def matrix_of(pieces):
    lane = lax.broadcasted_iota(jnp.int32, (LANES, LANES), 1)
    pieces = [piece.astype(BF16) for piece in pieces]
    rows = []
    for t in range(PER):
        turned = [
            pltpu.roll(pieces[c], ((c - t) * COLS) % LANES, 1) if (c - t) * COLS % LANES else pieces[c]
            for c in range(PARTS_C)
        ]
        tiles = []
        for q in range(WIDE // LANES):
            low, high = q * LANES, (q + 1) * LANES
            inside = [c for c in range(PARTS_C) if c * COLS < high and (c + 1) * COLS > low]
            tile = turned[inside[0]]
            for c in inside[1:]:
                tile = jnp.where(lane >= c * COLS - low, turned[c], tile)
            if high > SIZE:
                tile = jnp.where(lane < SIZE - low, tile, jnp.zeros_like(tile))
            tiles.append(tile)
        rows.append(jnp.concatenate(tiles, axis=1))
    return jnp.concatenate(rows, axis=0)


def pieces_of(values):
    values = values.astype(BF16)
    lane = lax.broadcasted_iota(jnp.int32, (LANES, LANES), 1)
    pieces = []
    for c in range(PARTS_C):
        low = c * COLS
        first, last = low // LANES, (low + COLS - 1) // LANES
        piece = None
        for t in range(PER):
            band = values[t * LANES : (t + 1) * LANES]
            source = band[:, first * LANES : (first + 1) * LANES]
            if last != first:
                source = jnp.where(lane >= low % LANES, source, band[:, last * LANES : (last + 1) * LANES])
            shift = ((t - c) * COLS) % LANES
            if shift:
                source = pltpu.roll(source, shift, 1)
            piece = source if piece is None else jnp.where(lane >= t * COLS, source, piece)
        pieces.append(jnp.where(lane < PER * COLS, piece, jnp.zeros_like(piece)).astype(F32))
    return pieces


def pieces_out(parts, ref):
    if len(parts) == 1:
        tiles = [piece.reshape(PARTS_R, SUBS, LANES) for piece in parts[0]]
    else:
        sub = lax.broadcasted_iota(jnp.int32, (PARTS_R, SUBS, LANES), 1)
        tiles = [None] * (PARTS_C * DOUBLE // SUBS)
        for c in range(PARTS_C):
            for a, pieces in enumerate(parts):
                tile, shift = divmod(c * DOUBLE + a * TILES, SUBS)
                piece = pieces[c].reshape(PARTS_R, SUBS, LANES)
                if shift:
                    piece = pltpu.roll(piece, shift, 1)
                tiles[tile] = piece if tiles[tile] is None else jnp.where(sub >= shift, piece, tiles[tile])
                if shift + TILES > SUBS:
                    tiles[tile + 1] = piece
    values = jnp.concatenate([tile[:, None] for tile in tiles], axis=1)
    ref[...] = values.reshape(-1, LANES).astype(BF16)


def first_to_second():
    index = lax.broadcasted_iota(jnp.int32, (1, WIDE), 1)
    part, s, t = (index % LANES) // SUBS, index % SUBS, index // LANES
    inner = PER * s + t
    residue = jnp.where((s < TILES) & (inner < ROWS), part * ROWS + inner, -1)
    second = lax.broadcasted_iota(jnp.int32, (WIDE, WIDE), 0)
    return jnp.where(second == residue, 1.0, 0.0).astype(BF16)


def second_to_first():
    index = lax.broadcasted_iota(jnp.int32, (WIDE, 1), 0)
    part, s, t = (index % LANES) // SUBS, index % SUBS, index // LANES
    inner = PER * s + t
    residue = jnp.where((s < TILES) & (inner < ROWS), part * ROWS + inner, -1)
    second = lax.broadcasted_iota(jnp.int32, (WIDE, WIDE), 1)
    return jnp.where(second == residue, 1.0, 0.0).astype(BF16)


def edges(normed, proj_mat, kept_ref):
    projected = dot(proj_mat, normed, 0, 0)
    p1, p2, p3, p4 = [projected[q * CHANNELS : (q + 1) * CHANNELS] for q in range(4)]
    s1, s3 = sigmoid(p1), sigmoid(p3)
    left, right = s1 * p2, s3 * p4
    for q, value in enumerate((s1, left, s3, right)):
        kept_ref[q] = value
    return left, right


def back_head(upstream, gating, product, normed_mix, mix_normed, mix_inverse, out_mat):
    through = (upstream * gating).astype(BF16)
    gate_up = (upstream * product * gating * (1.0 - gating)).astype(BF16)
    mix_up = dot(out_mat, through, 1, 0)
    out_part = dot(normed_mix, through, 1, 1)
    return norm_back(mix_normed, mix_inverse, mix_up), out_part, gate_up


def back_tail(upstream, pair_normed, pair_inverse, kept_ref, left_grad, right_grad, gate_up, proj_mat, gate_mat):
    s1, left, s3, right = [kept_ref[q] for q in range(4)]
    proj_up = jnp.concatenate(
        [left_grad * left * (1.0 - s1), left_grad * s1, right_grad * right * (1.0 - s3), right_grad * s3], axis=0
    ).astype(BF16)
    normed_up = dot(proj_mat, proj_up, 1, 0) + dot(gate_mat, gate_up, 1, 0)
    return upstream + norm_back(pair_normed, pair_inverse, normed_up), proj_up


def start_kernel(pair_ref, proj_ref, _, message_ref, flat_ref, normed_ref, inverse_ref, kept_ref, wide):
    pair = block_in(pair_ref)
    flat_ref[...] = pair.astype(BF16)
    pair_normed, inverse = norm_parts(pair)
    normed_ref[...] = pair_normed
    inverse_ref[...] = inverse
    pack(edges(pair_normed.astype(BF16), proj_ref[0], kept_ref), message_ref, wide)


def middle_kernel(
    mix_ref, pair_ref, normed0_ref, proj_ref, gate_ref, out_ref,
    message_ref, mix_normed_ref, mix_inverse_ref, product_ref, gating0_ref, after_ref, normed_ref, inverse_ref, kept_ref,
    gating_ref, narrow, wide,
):
    (mix,) = unpack(mix_ref, narrow, 1)
    mix_normed, mix_inverse = norm_parts(mix)
    mix_normed_ref[...] = mix_normed
    mix_inverse_ref[...] = mix_inverse
    product = dot(out_ref[0], mix_normed.astype(BF16), 0, 0)
    product_ref[...] = product
    gating0 = sigmoid(dot(gate_ref[0], normed0_ref[...].astype(BF16), 0, 0))
    gating0_ref[...] = gating0
    after = (pair_ref[...].astype(F32) + gating0 * product).astype(BF16)
    after_ref[...] = after
    pair_normed, inverse = norm_parts(after.astype(F32))
    normed_ref[...] = pair_normed
    inverse_ref[...] = inverse
    normed = pair_normed.astype(BF16)
    pack(edges(normed, proj_ref[1], kept_ref), message_ref, wide)
    gating_ref[...] = sigmoid(dot(gate_ref[1], normed, 0, 0))


def turn_kernel(
    mix_ref, after_ref, gating_ref, cot_ref, out_ref, normed_ref,
    pair_out_ref, message_ref, cot_out_ref, gate_up_ref, gate_part_ref, out_part_ref, narrow,
):
    (mix,) = unpack(mix_ref, narrow, 1)
    mix_normed, mix_inverse = norm_parts(mix)
    normed_mix = mix_normed.astype(BF16)
    product = dot(out_ref[1], normed_mix, 0, 0)
    gating = gating_ref[...]
    pair_out_ref[...] = (after_ref[...].astype(F32) + gating * product).astype(BF16)
    cot = block_in(cot_ref)
    cot_out_ref[...] = cot.astype(BF16)
    mix_grad, out_part, gate_up = back_head(cot, gating, product, normed_mix, mix_normed, mix_inverse, out_ref[1])
    pack([mix_grad], message_ref, narrow)
    out_part_ref[...] = out_part
    gate_up_ref[...] = gate_up
    gate_part_ref[...] = dot(normed_ref[...].astype(BF16), gate_up, 1, 1)


def back_kernel(
    grads_ref, cot_ref, normed1_ref, inverse1_ref, kept1_ref, gate_up1_ref, mix_normed_ref, mix_inverse_ref,
    product_ref, gating0_ref, proj_ref, gate_ref, out_ref, pair_out_ref,
    pair_out_hbm, message_ref, upstream_ref, gate_up_ref, proj_part_ref, out_part_ref, narrow, wide, pair_out, sem,
):
    pair_out[...] = block_out_exact(pair_out_ref[...])
    copy = pltpu.make_async_copy(pair_out, pair_out_hbm, sem)
    copy.start()
    left_grad, right_grad = unpack(grads_ref, wide, 2)
    pair_normed = normed1_ref[...]
    upstream, proj_up = back_tail(
        cot_ref[...].astype(F32), pair_normed, inverse1_ref[...], kept1_ref, left_grad, right_grad, gate_up1_ref[...],
        proj_ref[1], gate_ref[1],
    )
    upstream_ref[...] = upstream
    proj_part_ref[...] = dot(pair_normed.astype(BF16), proj_up, 1, 1)
    mix_normed = mix_normed_ref[...]
    mix_grad, out_part, gate_up = back_head(
        upstream, gating0_ref[...], product_ref[...], mix_normed.astype(BF16), mix_normed, mix_inverse_ref[...],
        out_ref[0],
    )
    pack([mix_grad], message_ref, narrow)
    out_part_ref[...] = out_part
    gate_up_ref[...] = gate_up
    copy.wait()


def last_kernel(
    grads_ref, upstream_ref, normed_ref, inverse_ref, kept_ref, gate_up_ref, proj_ref, gate_ref,
    proj1_ref, gate1_ref, out1_ref, out0_ref,
    pair_grad_ref, message_ref, wide,
):
    left_grad, right_grad = unpack(grads_ref, wide, 2)
    pair_normed = normed_ref[...]
    gate_up = gate_up_ref[...]
    total, proj_up = back_tail(
        upstream_ref[...], pair_normed, inverse_ref[...], kept_ref, left_grad, right_grad, gate_up,
        proj_ref[0], gate_ref[0],
    )
    pair_grad_ref[...] = total
    normed = pair_normed.astype(BF16)
    proj_part = dot(normed, proj_up, 1, 1)
    parts = [proj_part[:, q * LANES : (q + 1) * LANES] for q in range(4)]
    parts += [proj1_ref[:, q * LANES : (q + 1) * LANES] for q in range(4)]
    parts += [dot(normed, gate_up, 1, 1), gate1_ref[...], out0_ref[...], out1_ref[...]]
    for q, part in enumerate(parts):
        message_ref[q * CHANNELS : (q + 1) * CHANNELS, :] = part.astype(BF16)


def sum_kernel(parts_ref, total_ref):
    pairs = parts_ref[...].astype(F32).reshape(DEVICES // 2, 2 * WEIGHTS, LANES)
    total = jnp.sum(pairs, axis=0)
    total = (total[:WEIGHTS] + total[WEIGHTS:]) * (1.0 / SIZE)
    total = jnp.concatenate([total, total], axis=0)[None]
    total_ref[...] = jnp.broadcast_to(total, pairs.shape).reshape(DEVICES * WEIGHTS, LANES).astype(BF16)


def spread_kernel(
    sums_ref, pair_grad_ref, proj_hbm, gate_hbm, out_hbm, pair_grad_hbm, proj, gate, out, pair_grad, sems,
):
    copies = []

    def send(source, target):
        copies.append(pltpu.make_async_copy(source, target, sems.at[len(copies)]))
        copies[-1].start()

    parts = [sums_ref[q * CHANNELS : (q + 1) * CHANNELS, :].astype(F32) for q in range(WEIGHTS)]
    for l in range(2):
        proj[l] = jnp.concatenate(parts[4 * l : 4 * l + 4], axis=1)
        send(proj.at[l], proj_hbm.at[l])
    for l in range(2):
        gate[l], out[l] = parts[8 + l], parts[10 + l]
    send(gate, gate_hbm)
    send(out, out_hbm)
    for s in range(TILES):
        low = s * PER * COLS
        count = min(PER * COLS, ROWS * COLS - low)
        pair_grad[low : low + count, :] = pair_grad_ref[:, s * LANES : (s + 1) * LANES].T[:count]
        send(pair_grad.at[pl.ds(low, count)], pair_grad_hbm.at[pl.ds(low, count)])
    for copy in copies:
        copy.wait()


def orders_kernel(forth_ref, back_ref):
    forth_ref[...] = first_to_second()
    back_ref[...] = second_to_first()


def outgoing_kernel(edges_ref, forth_ref, mix_ref, left_ref, right_ref):
    left, right = [matrix_of(pieces) for pieces in pieces_in(edges_ref, 2)]
    right = dot(forth_ref[...], right, 1, 0).astype(BF16)
    left_ref[...], right_ref[...] = left, right
    pieces_out([pieces_of(dot(left, right, 1, 1))], mix_ref)


def incoming_kernel(edges_ref, back_ref, mix_ref, left_ref, right_ref):
    left, right = [matrix_of(pieces) for pieces in pieces_in(edges_ref, 2, (0,))]
    turned = dot(back_ref[...], left, 1, 1).astype(BF16)
    left_ref[...], right_ref[...] = turned, right
    pieces_out([pieces_of(dot(turned, right, 1, 0))], mix_ref)


def incoming_back_kernel(grad_ref, back_ref, left_ref, right_ref, grads_ref):
    grad = matrix_of(pieces_in(grad_ref, 1)[0])
    left_grad = dot(right_ref[...], grad, 1, 1).astype(BF16)
    right_grad = dot(left_ref[...], grad, 0, 0)
    pieces_out([pieces_of(dot(left_grad, back_ref[...], 1, 0)), pieces_of(right_grad)], grads_ref)


def outgoing_back_kernel(grad_ref, back_ref, left_ref, right_ref, grads_ref):
    grad = matrix_of(pieces_in(grad_ref, 1)[0])
    turned = dot(back_ref[...], grad, 1, 1).astype(BF16)
    pieces_out([pieces_of(dot(grad, right_ref[...], 1, 0)), pieces_of(dot(turned, left_ref[...], 1, 0))], grads_ref)


SINGLE_SHAPE = (DEVICES * SINGLE, LANES)
DOUBLE_SHAPE = (DEVICES * DOUBLE, LANES)
WEIGHTS_SHAPE = (DEVICES * WEIGHTS, LANES)
BLOCK = (ROWS * COLS, CHANNELS)
FLAT = (CHANNELS, TILES * LANES)
KEPT = (4, CHANNELS, TILES * LANES)
LINE = (1, TILES * LANES)
SQUARE = (WIDE, WIDE)
WEIGHT = (CHANNELS, CHANNELS)
PROJ = (CHANNELS, 4 * CHANNELS)
DMA = pltpu.SemaphoreType.DMA


def call(kernel, name, outs, scratch, *operands, far_out=(), flops=None):
    def spec(far):
        return pl.BlockSpec(memory_space=pl.ANY if far else pltpu.VMEM)

    return pl.pallas_call(
        kernel,
        out_shape=[jax.ShapeDtypeStruct(shape, kind) for shape, kind in outs],
        in_specs=[spec(False) for _ in operands],
        out_specs=[spec(position in far_out) for position in range(len(outs))],
        scratch_shapes=scratch,
        cost_estimate=flops and pl.CostEstimate(flops=flops, bytes_accessed=0, transcendentals=0),
        compiler_params=pltpu.CompilerParams(vmem_limit_bytes=24 * 1024 * 1024),
        name=name,
    )(*operands)


def exchange(message):
    rows = message.shape[0] // DEVICES
    shape = (DEVICES, rows, LANES)
    for low in (4, 2):
        if rows % 8 and rows % low == 0:
            shape = (DEVICES, rows // low, low, LANES)
            break
    return lax.all_to_all(message.reshape(shape), AXES, 0, 0, tiled=True).reshape(message.shape)


def local(pair_rep, proj_weight, gate_weight, out_weight, pair_cot):
    pair = pair_rep.reshape(BLOCK)
    cot = pair_cot.reshape(BLOCK)
    double = pltpu.VMEM((DEVICES * DOUBLE + 16, LANES), F32)
    spaced = pltpu.VMEM((DEVICES * (SINGLE + 1) + 16, LANES), F32)
    forth, back = call(orders_kernel, "orders", [(SQUARE, BF16), (SQUARE, BF16)], [], flops=4 * 1024**3)
    edges0, pair0, normed0, inverse0, kept0 = call(
        start_kernel, "start", [(DOUBLE_SHAPE, BF16), (FLAT, BF16), (FLAT, F32), (LINE, F32), (KEPT, F32)], [double],
        pair, proj_weight, forth,
    )
    mix0, left0, right0 = call(
        outgoing_kernel, "outgoing", [(SINGLE_SHAPE, BF16), (SQUARE, BF16), (SQUARE, BF16)], [],
        exchange(edges0), forth,
    )
    edges1, mix_normed0, mix_inverse0, product0, gating0, after, normed1, inverse1, kept1, gating1 = call(
        middle_kernel, "middle",
        [
            (DOUBLE_SHAPE, BF16), (FLAT, F32), (LINE, F32), (FLAT, F32), (FLAT, F32), (FLAT, BF16), (FLAT, F32),
            (LINE, F32), (KEPT, F32), (FLAT, F32),
        ],
        [spaced, double], exchange(mix0), pair0, normed0, proj_weight, gate_weight, out_weight,
    )
    mix1, left1, right1 = call(
        incoming_kernel, "incoming", [(SINGLE_SHAPE, BF16), (SQUARE, BF16), (SQUARE, BF16)], [],
        exchange(edges1), back,
    )
    pair_out, grad1, cot1, gate_up1, gate_part1, out_part1 = call(
        turn_kernel, "turn",
        [(FLAT, BF16), (SINGLE_SHAPE, BF16), (FLAT, BF16), (FLAT, BF16), (WEIGHT, F32), (WEIGHT, F32)],
        [spaced], exchange(mix1), after, gating1, cot, out_weight, normed1,
    )
    (grads1,) = call(
        incoming_back_kernel, "incoming_back", [(DOUBLE_SHAPE, BF16)], [], exchange(grad1), back, left1, right1
    )
    pair_out, grad0, upstream, gate_up0, proj_part1, out_part0 = call(
        back_kernel, "back",
        [(BLOCK, BF16), (SINGLE_SHAPE, BF16), (FLAT, F32), (FLAT, BF16), (PROJ, F32), (WEIGHT, F32)],
        [spaced, double, pltpu.VMEM(BLOCK, BF16), DMA], exchange(grads1), cot1, normed1, inverse1, kept1, gate_up1, mix_normed0, mix_inverse0,
        product0, gating0, proj_weight, gate_weight, out_weight, pair_out, far_out=(0,),
    )
    (grads0,) = call(
        outgoing_back_kernel, "outgoing_back", [(DOUBLE_SHAPE, BF16)], [], exchange(grad0), back, left0, right0
    )
    pair_grad, parts = call(
        last_kernel, "last", [(FLAT, F32), (WEIGHTS_SHAPE, BF16)], [double],
        exchange(grads0), upstream, normed0, inverse0, kept0, gate_up0, proj_weight, gate_weight,
        proj_part1, gate_part1, out_part1, out_part0,
    )
    (sums,) = call(sum_kernel, "sum", [(WEIGHTS_SHAPE, BF16)], [], exchange(parts))
    outs = [((2,) + PROJ, F32), ((2,) + WEIGHT, F32), ((2,) + WEIGHT, F32), (BLOCK, F32)]
    proj_grad, gate_grad, out_grad, pair_grad = call(
        spread_kernel, "spread", outs, [pltpu.VMEM(shape, kind) for shape, kind in outs] + [DMA((4 + TILES,))],
        exchange(sums), pair_grad, far_out=range(4),
    )
    return (
        pair_out.reshape(ROWS, COLS, CHANNELS),
        pair_grad.reshape(ROWS, COLS, CHANNELS),
        proj_grad,
        gate_grad,
        out_grad,
    )


def solution(mesh):
    in_specs = (P("row", "col", None), P(), P(), P(), P("row", "col", None))
    out_specs = (P("row", "col", None), P("row", "col", None), P(), P(), P())
    return jax.shard_map(local, mesh=mesh, in_specs=in_specs, out_specs=out_specs, check_vma=False)
```

```python
import jax
import jax.numpy as jnp
from jax import lax
from jax.experimental import pallas as pl
from jax.experimental.pallas import tpu as pltpu
from jax.sharding import PartitionSpec as P

EPSILON = 1e-05
F32 = jnp.float32
BF16 = jnp.bfloat16
AXES = ("row", "col")

PARTS_R, PARTS_C = 16, 8
DEVICES = PARTS_R * PARTS_C
ROWS, COLS, CHANNELS = 20, 40, 128
PER = 3
TILES = 7
SUBS = 8
LANES = 128
SIZE = 320
WIDE = 384
SINGLE, DOUBLE, WEIGHTS = 8, 14, 12


def dot(first_op, second_op, first_dim, second_dim):
    return lax.dot_general(
        first_op,
        second_op,
        (((first_dim,), (second_dim,)), ((), ())),
        preferred_element_type=F32,
    )


def mean0(values):
    return jnp.sum(values, axis=0, keepdims=True) * (1.0 / CHANNELS)


def norm_parts(values):
    centered = values - mean0(values)
    inverse = lax.rsqrt(mean0(centered * centered) + EPSILON)
    return centered * inverse, inverse


def norm_back(normed, inverse, upstream):
    return inverse * (upstream - mean0(upstream) - normed * mean0(upstream * normed))


def sigmoid(values):
    return 0.5 * jnp.tanh(0.5 * values) + 0.5


def identity():
    shape = (CHANNELS, CHANNELS)
    same = lax.broadcasted_iota(jnp.int32, shape, 0) == lax.broadcasted_iota(jnp.int32, shape, 1)
    return jnp.where(same, 1.0, 0.0).astype(BF16)


def block_in(ref):
    values = ref[...].astype(F32)
    pieces = []
    for s in range(TILES):
        low = s * PER * COLS
        high = min(low + PER * COLS, ROWS * COLS)
        pieces += [values[low:high], jnp.zeros((LANES - (high - low), CHANNELS), F32)]
    return dot(identity(), jnp.concatenate(pieces, axis=0).astype(BF16), 1, 1)


def block_out_exact(values):
    pieces = []
    for s in range(TILES):
        count = min(PER * COLS, ROWS * COLS - s * PER * COLS)
        pieces.append(dot(identity(), values[:, s * LANES : (s + 1) * LANES], 1, 1)[:count])
    return jnp.concatenate(pieces, axis=0).astype(BF16)


def rows_of(parts):
    return SINGLE if parts == 1 else DOUBLE


def pitch_of(parts):
    return SINGLE + 1 if parts == 1 else DOUBLE


def pack(parts, out_ref, wide):
    pitch = pitch_of(len(parts))
    for a, part in enumerate(parts):
        for s in range(TILES):
            wide[pl.ds(a * TILES + s, CHANNELS, stride=pitch), :] = part[:, s * LANES : (s + 1) * LANES]
    if len(parts) == 1:
        wide[pl.ds(TILES, CHANNELS, stride=pitch), :] = jnp.zeros((CHANNELS, LANES), F32)
        for d in range(0, CHANNELS, 2):
            two = [wide[e * pitch : e * pitch + SINGLE, :] for e in (d, d + 1)]
            out_ref[d * SINGLE : (d + 2) * SINGLE, :] = jnp.concatenate(two, axis=0).astype(BF16)
    else:
        out_ref[...] = wide[: DEVICES * DOUBLE, :].astype(BF16)


def unpack(ref, wide, count):
    pitch = pitch_of(count)
    if count == 1:
        for d in range(0, CHANNELS, 2):
            two = ref[d * SINGLE : (d + 2) * SINGLE, :].astype(F32)
            for e in range(2):
                wide[(d + e) * pitch : (d + e) * pitch + SINGLE, :] = two[e * SINGLE : (e + 1) * SINGLE]
    else:
        wide[: DEVICES * DOUBLE, :] = ref[...].astype(F32)
    return [
        jnp.concatenate([wide[pl.ds(a * TILES + s, CHANNELS, stride=pitch), :] for s in range(TILES)], axis=1)
        for a in range(count)
    ]


def pieces_in(ref, count, clean=()):
    values = ref[...].astype(F32).reshape(PARTS_R, -1, SUBS, LANES)
    if count == 1:
        return [[values[:, c].reshape(LANES, LANES) for c in range(PARTS_C)]]
    sub = lax.broadcasted_iota(jnp.int32, (PARTS_R, SUBS, LANES), 1)
    parts = []
    for a in range(count):
        parts.append([])
        for c in range(PARTS_C):
            tile, shift = divmod(c * DOUBLE + a * TILES, SUBS)
            piece = values[:, tile]
            if shift + TILES > SUBS:
                piece = jnp.where(sub >= shift, piece, values[:, tile + 1])
            if shift:
                piece = pltpu.roll(piece, SUBS - shift, 1)
            if a in clean:
                piece = jnp.where(sub < TILES, piece, 0.0)
            parts[a].append(piece.reshape(LANES, LANES))
    return parts


def matrix_of(pieces):
    lane = lax.broadcasted_iota(jnp.int32, (LANES, LANES), 1)
    pieces = [piece.astype(BF16) for piece in pieces]
    rows = []
    for t in range(PER):
        turned = [
            pltpu.roll(pieces[c], ((c - t) * COLS) % LANES, 1) if (c - t) * COLS % LANES else pieces[c]
            for c in range(PARTS_C)
        ]
        tiles = []
        for q in range(WIDE // LANES):
            low, high = q * LANES, (q + 1) * LANES
            inside = [c for c in range(PARTS_C) if c * COLS < high and (c + 1) * COLS > low]
            tile = turned[inside[0]]
            for c in inside[1:]:
                tile = jnp.where(lane >= c * COLS - low, turned[c], tile)
            if high > SIZE:
                tile = jnp.where(lane < SIZE - low, tile, jnp.zeros_like(tile))
            tiles.append(tile)
        rows.append(jnp.concatenate(tiles, axis=1))
    return jnp.concatenate(rows, axis=0)


def pieces_of(values):
    values = values.astype(BF16)
    lane = lax.broadcasted_iota(jnp.int32, (LANES, LANES), 1)
    pieces = []
    for c in range(PARTS_C):
        low = c * COLS
        first, last = low // LANES, (low + COLS - 1) // LANES
        piece = None
        for t in range(PER):
            band = values[t * LANES : (t + 1) * LANES]
            source = band[:, first * LANES : (first + 1) * LANES]
            if last != first:
                source = jnp.where(lane >= low % LANES, source, band[:, last * LANES : (last + 1) * LANES])
            shift = ((t - c) * COLS) % LANES
            if shift:
                source = pltpu.roll(source, shift, 1)
            piece = source if piece is None else jnp.where(lane >= t * COLS, source, piece)
        pieces.append(jnp.where(lane < PER * COLS, piece, jnp.zeros_like(piece)).astype(F32))
    return pieces


def pieces_out(parts, ref):
    if len(parts) == 1:
        tiles = [piece.reshape(PARTS_R, SUBS, LANES) for piece in parts[0]]
    else:
        sub = lax.broadcasted_iota(jnp.int32, (PARTS_R, SUBS, LANES), 1)
        tiles = [None] * (PARTS_C * DOUBLE // SUBS)
        for c in range(PARTS_C):
            for a, pieces in enumerate(parts):
                tile, shift = divmod(c * DOUBLE + a * TILES, SUBS)
                piece = pieces[c].reshape(PARTS_R, SUBS, LANES)
                if shift:
                    piece = pltpu.roll(piece, shift, 1)
                tiles[tile] = piece if tiles[tile] is None else jnp.where(sub >= shift, piece, tiles[tile])
                if shift + TILES > SUBS:
                    tiles[tile + 1] = piece
    values = jnp.concatenate([tile[:, None] for tile in tiles], axis=1)
    ref[...] = values.reshape(-1, LANES).astype(BF16)


def first_to_second():
    index = lax.broadcasted_iota(jnp.int32, (1, WIDE), 1)
    part, s, t = (index % LANES) // SUBS, index % SUBS, index // LANES
    inner = PER * s + t
    residue = jnp.where((s < TILES) & (inner < ROWS), part * ROWS + inner, -1)
    second = lax.broadcasted_iota(jnp.int32, (WIDE, WIDE), 0)
    return jnp.where(second == residue, 1.0, 0.0).astype(BF16)


def second_to_first():
    index = lax.broadcasted_iota(jnp.int32, (WIDE, 1), 0)
    part, s, t = (index % LANES) // SUBS, index % SUBS, index // LANES
    inner = PER * s + t
    residue = jnp.where((s < TILES) & (inner < ROWS), part * ROWS + inner, -1)
    second = lax.broadcasted_iota(jnp.int32, (WIDE, WIDE), 1)
    return jnp.where(second == residue, 1.0, 0.0).astype(BF16)


def edges(normed, proj_mat, kept_ref):
    projected = dot(proj_mat, normed, 0, 0)
    p1, p2, p3, p4 = [projected[q * CHANNELS : (q + 1) * CHANNELS] for q in range(4)]
    s1, s3 = sigmoid(p1), sigmoid(p3)
    left, right = s1 * p2, s3 * p4
    for q, value in enumerate((s1, left, s3, right)):
        kept_ref[q] = value
    return left, right


def back_head(upstream, gating, product, normed_mix, mix_normed, mix_inverse, out_mat):
    through = (upstream * gating).astype(BF16)
    gate_up = (upstream * product * gating * (1.0 - gating)).astype(BF16)
    mix_up = dot(out_mat, through, 1, 0)
    out_part = dot(normed_mix, through, 1, 1)
    return norm_back(mix_normed, mix_inverse, mix_up), out_part, gate_up


def back_tail(upstream, pair_normed, pair_inverse, kept_ref, left_grad, right_grad, gate_up, proj_mat, gate_mat):
    s1, left, s3, right = [kept_ref[q] for q in range(4)]
    proj_up = jnp.concatenate(
        [left_grad * left * (1.0 - s1), left_grad * s1, right_grad * right * (1.0 - s3), right_grad * s3], axis=0
    ).astype(BF16)
    normed_up = dot(proj_mat, proj_up, 1, 0) + dot(gate_mat, gate_up, 1, 0)
    return upstream + norm_back(pair_normed, pair_inverse, normed_up), proj_up


def start_kernel(pair_ref, proj_ref, _, message_ref, flat_ref, normed_ref, inverse_ref, kept_ref, wide):
    pair = block_in(pair_ref)
    flat_ref[...] = pair.astype(BF16)
    pair_normed, inverse = norm_parts(pair)
    normed_ref[...] = pair_normed
    inverse_ref[...] = inverse
    pack(edges(pair_normed.astype(BF16), proj_ref[0], kept_ref), message_ref, wide)


def middle_kernel(
    mix_ref, pair_ref, normed0_ref, proj_ref, gate_ref, out_ref,
    message_ref, mix_normed_ref, mix_inverse_ref, product_ref, gating0_ref, after_ref, normed_ref, inverse_ref, kept_ref,
    gating_ref, narrow, wide,
):
    (mix,) = unpack(mix_ref, narrow, 1)
    mix_normed, mix_inverse = norm_parts(mix)
    mix_normed_ref[...] = mix_normed
    mix_inverse_ref[...] = mix_inverse
    product = dot(out_ref[0], mix_normed.astype(BF16), 0, 0)
    product_ref[...] = product
    gating0 = sigmoid(dot(gate_ref[0], normed0_ref[...].astype(BF16), 0, 0))
    gating0_ref[...] = gating0
    after = (pair_ref[...].astype(F32) + gating0 * product).astype(BF16)
    after_ref[...] = after
    pair_normed, inverse = norm_parts(after.astype(F32))
    normed_ref[...] = pair_normed
    inverse_ref[...] = inverse
    normed = pair_normed.astype(BF16)
    pack(edges(normed, proj_ref[1], kept_ref), message_ref, wide)
    gating_ref[...] = sigmoid(dot(gate_ref[1], normed, 0, 0))


def turn_kernel(mix_ref, mix_up_ref, message_ref, normed_mix_ref, narrow):
    (mix,) = unpack(mix_ref, narrow, 1)
    mix_normed, mix_inverse = norm_parts(mix)
    normed_mix_ref[...] = mix_normed.astype(BF16)
    mix_up = mix_up_ref[...]
    pack([mix_inverse * (mix_up - mix_normed * mean0(mix_up * mix_normed))], message_ref, narrow)


def before_turn(cot_ref, gating_ref, out_ref, cot_flat_ref, through_ref, mix_up_ref):
    cot = block_in(cot_ref)
    cot_flat_ref[...] = cot.astype(BF16)
    through = (cot * gating_ref[...]).astype(BF16)
    through_ref[...] = through
    mix_up = dot(out_ref[1], through, 1, 0)
    mix_up_ref[...] = mix_up - mean0(mix_up)


def after_turn(
    normed_mix_ref, after_ref, gating_ref, cot_ref, through_ref, out_ref, normed_ref,
    pair_out_ref, gate_up_ref, gate_part_ref, out_part_ref,
):
    normed_mix = normed_mix_ref[...]
    product = dot(out_ref[1], normed_mix, 0, 0)
    gating = gating_ref[...]
    pair_out_ref[...] = (after_ref[...].astype(F32) + gating * product).astype(BF16)
    gate_up = (cot_ref[...].astype(F32) * product * gating * (1.0 - gating)).astype(BF16)
    gate_up_ref[...] = gate_up
    gate_part_ref[...] = dot(normed_ref[...].astype(BF16), gate_up, 1, 1)
    out_part_ref[...] = dot(normed_mix, through_ref[...], 1, 1)


def back_kernel(
    grads_ref, cot_ref, normed1_ref, inverse1_ref, kept1_ref, gate_up1_ref, mix_normed_ref, mix_inverse_ref,
    product_ref, gating0_ref, proj_ref, gate_ref, out_ref, pair_out_ref,
    pair_out_hbm, message_ref, upstream_ref, gate_up_ref, proj_part_ref, out_part_ref, narrow, wide, pair_out, sem,
):
    pair_out[...] = block_out_exact(pair_out_ref[...])
    copy = pltpu.make_async_copy(pair_out, pair_out_hbm, sem)
    copy.start()
    left_grad, right_grad = unpack(grads_ref, wide, 2)
    pair_normed = normed1_ref[...]
    upstream, proj_up = back_tail(
        cot_ref[...].astype(F32), pair_normed, inverse1_ref[...], kept1_ref, left_grad, right_grad, gate_up1_ref[...],
        proj_ref[1], gate_ref[1],
    )
    upstream_ref[...] = upstream
    proj_part_ref[...] = dot(pair_normed.astype(BF16), proj_up, 1, 1)
    mix_normed = mix_normed_ref[...]
    mix_grad, out_part, gate_up = back_head(
        upstream, gating0_ref[...], product_ref[...], mix_normed.astype(BF16), mix_normed, mix_inverse_ref[...],
        out_ref[0],
    )
    pack([mix_grad], message_ref, narrow)
    out_part_ref[...] = out_part
    gate_up_ref[...] = gate_up
    copy.wait()


def last_kernel(
    grads_ref, upstream_ref, normed_ref, inverse_ref, kept_ref, gate_up_ref, proj_ref, gate_ref,
    proj1_ref, gate1_ref, out1_ref, out0_ref,
    pair_grad_ref, message_ref, wide,
):
    left_grad, right_grad = unpack(grads_ref, wide, 2)
    pair_normed = normed_ref[...]
    gate_up = gate_up_ref[...]
    total, proj_up = back_tail(
        upstream_ref[...], pair_normed, inverse_ref[...], kept_ref, left_grad, right_grad, gate_up,
        proj_ref[0], gate_ref[0],
    )
    pair_grad_ref[...] = total
    normed = pair_normed.astype(BF16)
    proj_part = dot(normed, proj_up, 1, 1)
    parts = [proj_part[:, q * LANES : (q + 1) * LANES] for q in range(4)]
    parts += [proj1_ref[:, q * LANES : (q + 1) * LANES] for q in range(4)]
    parts += [dot(normed, gate_up, 1, 1), gate1_ref[...], out0_ref[...], out1_ref[...]]
    for q, part in enumerate(parts):
        message_ref[q * CHANNELS : (q + 1) * CHANNELS, :] = part.astype(BF16)


def sum_kernel(parts_ref, total_ref):
    pairs = parts_ref[...].astype(F32).reshape(DEVICES // 2, 2 * WEIGHTS, LANES)
    total = jnp.sum(pairs, axis=0)
    total = (total[:WEIGHTS] + total[WEIGHTS:]) * (1.0 / SIZE)
    total = jnp.concatenate([total, total], axis=0)[None]
    total_ref[...] = jnp.broadcast_to(total, pairs.shape).reshape(DEVICES * WEIGHTS, LANES).astype(BF16)


def spread_kernel(
    sums_ref, pair_grad_ref, proj_hbm, gate_hbm, out_hbm, pair_grad_hbm, proj, gate, out, pair_grad, sems,
):
    copies = []

    def send(source, target):
        copies.append(pltpu.make_async_copy(source, target, sems.at[len(copies)]))
        copies[-1].start()

    parts = [sums_ref[q * CHANNELS : (q + 1) * CHANNELS, :].astype(F32) for q in range(WEIGHTS)]
    for l in range(2):
        proj[l] = jnp.concatenate(parts[4 * l : 4 * l + 4], axis=1)
        send(proj.at[l], proj_hbm.at[l])
    for l in range(2):
        gate[l], out[l] = parts[8 + l], parts[10 + l]
    send(gate, gate_hbm)
    send(out, out_hbm)
    for s in range(TILES):
        low = s * PER * COLS
        count = min(PER * COLS, ROWS * COLS - low)
        pair_grad[low : low + count, :] = pair_grad_ref[:, s * LANES : (s + 1) * LANES].T[:count]
        send(pair_grad.at[pl.ds(low, count)], pair_grad_hbm.at[pl.ds(low, count)])
    for copy in copies:
        copy.wait()


def orders_kernel(forth_ref, back_ref):
    forth_ref[...] = first_to_second()
    back_ref[...] = second_to_first()


def outgoing_kernel(edges_ref, forth_ref, mix_ref, left_ref, right_ref):
    left, right = [matrix_of(pieces) for pieces in pieces_in(edges_ref, 2)]
    right = dot(forth_ref[...], right, 1, 0).astype(BF16)
    left_ref[...], right_ref[...] = left, right
    pieces_out([pieces_of(dot(left, right, 1, 1))], mix_ref)


def incoming_kernel(edges_ref, back_ref, cot_ref, gating_ref, out_ref, mix_ref, left_ref, right_ref, *side):
    left, right = [matrix_of(pieces) for pieces in pieces_in(edges_ref, 2, (0,))]
    turned = dot(back_ref[...], left, 1, 1).astype(BF16)
    left_ref[...], right_ref[...] = turned, right
    pieces_out([pieces_of(dot(turned, right, 1, 0))], mix_ref)
    before_turn(cot_ref, gating_ref, out_ref, *side)


def incoming_back_kernel(grad_ref, back_ref, left_ref, right_ref, *side):
    *side, grads_ref = side
    grad = matrix_of(pieces_in(grad_ref, 1)[0])
    left_grad = dot(right_ref[...], grad, 1, 1).astype(BF16)
    right_grad = dot(left_ref[...], grad, 0, 0)
    pieces_out([pieces_of(dot(left_grad, back_ref[...], 1, 0)), pieces_of(right_grad)], grads_ref)
    after_turn(*side)


def outgoing_back_kernel(grad_ref, back_ref, left_ref, right_ref, grads_ref):
    grad = matrix_of(pieces_in(grad_ref, 1)[0])
    turned = dot(back_ref[...], grad, 1, 1).astype(BF16)
    pieces_out([pieces_of(dot(grad, right_ref[...], 1, 0)), pieces_of(dot(turned, left_ref[...], 1, 0))], grads_ref)


SINGLE_SHAPE = (DEVICES * SINGLE, LANES)
DOUBLE_SHAPE = (DEVICES * DOUBLE, LANES)
WEIGHTS_SHAPE = (DEVICES * WEIGHTS, LANES)
BLOCK = (ROWS * COLS, CHANNELS)
FLAT = (CHANNELS, TILES * LANES)
KEPT = (4, CHANNELS, TILES * LANES)
LINE = (1, TILES * LANES)
SQUARE = (WIDE, WIDE)
WEIGHT = (CHANNELS, CHANNELS)
PROJ = (CHANNELS, 4 * CHANNELS)
DMA = pltpu.SemaphoreType.DMA


def call(kernel, name, outs, scratch, *operands, far_out=(), flops=None):
    def spec(far):
        return pl.BlockSpec(memory_space=pl.ANY if far else pltpu.VMEM)

    return pl.pallas_call(
        kernel,
        out_shape=[jax.ShapeDtypeStruct(shape, kind) for shape, kind in outs],
        in_specs=[spec(False) for _ in operands],
        out_specs=[spec(position in far_out) for position in range(len(outs))],
        scratch_shapes=scratch,
        cost_estimate=flops and pl.CostEstimate(flops=flops, bytes_accessed=0, transcendentals=0),
        compiler_params=pltpu.CompilerParams(vmem_limit_bytes=24 * 1024 * 1024),
        name=name,
    )(*operands)


def exchange(message):
    rows = message.shape[0] // DEVICES
    shape = (DEVICES, rows, LANES)
    for low in (4, 2):
        if rows % 8 and rows % low == 0:
            shape = (DEVICES, rows // low, low, LANES)
            break
    return lax.all_to_all(message.reshape(shape), AXES, 0, 0, tiled=True).reshape(message.shape)


def local(pair_rep, proj_weight, gate_weight, out_weight, pair_cot):
    pair = pair_rep.reshape(BLOCK)
    cot = pair_cot.reshape(BLOCK)
    double = pltpu.VMEM((DEVICES * DOUBLE + 16, LANES), F32)
    spaced = pltpu.VMEM((DEVICES * (SINGLE + 1) + 16, LANES), F32)
    forth, back = call(orders_kernel, "orders", [(SQUARE, BF16), (SQUARE, BF16)], [], flops=4 * 1024**3)
    edges0, pair0, normed0, inverse0, kept0 = call(
        start_kernel, "start", [(DOUBLE_SHAPE, BF16), (FLAT, BF16), (FLAT, F32), (LINE, F32), (KEPT, F32)], [double],
        pair, proj_weight, forth,
    )
    mix0, left0, right0 = call(
        outgoing_kernel, "outgoing", [(SINGLE_SHAPE, BF16), (SQUARE, BF16), (SQUARE, BF16)], [],
        exchange(edges0), forth,
    )
    edges1, mix_normed0, mix_inverse0, product0, gating0, after, normed1, inverse1, kept1, gating1 = call(
        middle_kernel, "middle",
        [
            (DOUBLE_SHAPE, BF16), (FLAT, F32), (LINE, F32), (FLAT, F32), (FLAT, F32), (FLAT, BF16), (FLAT, F32),
            (LINE, F32), (KEPT, F32), (FLAT, F32),
        ],
        [spaced, double], exchange(mix0), pair0, normed0, proj_weight, gate_weight, out_weight,
    )
    mix1, left1, right1, cot1, through1, mix_up1 = call(
        incoming_kernel, "incoming",
        [(SINGLE_SHAPE, BF16), (SQUARE, BF16), (SQUARE, BF16), (FLAT, BF16), (FLAT, BF16), (FLAT, F32)], [],
        exchange(edges1), back, cot, gating1, out_weight,
    )
    grad1, normed_mix1 = call(
        turn_kernel, "turn", [(SINGLE_SHAPE, BF16), (FLAT, BF16)], [spaced], exchange(mix1), mix_up1
    )
    pair_out, gate_up1, gate_part1, out_part1, grads1 = call(
        incoming_back_kernel, "incoming_back",
        [(FLAT, BF16), (FLAT, BF16), (WEIGHT, F32), (WEIGHT, F32), (DOUBLE_SHAPE, BF16)], [],
        exchange(grad1), back, left1, right1, normed_mix1, after, gating1, cot1, through1, out_weight, normed1,
    )
    pair_out, grad0, upstream, gate_up0, proj_part1, out_part0 = call(
        back_kernel, "back",
        [(BLOCK, BF16), (SINGLE_SHAPE, BF16), (FLAT, F32), (FLAT, BF16), (PROJ, F32), (WEIGHT, F32)],
        [spaced, double, pltpu.VMEM(BLOCK, BF16), DMA], exchange(grads1), cot1, normed1, inverse1, kept1, gate_up1, mix_normed0, mix_inverse0,
        product0, gating0, proj_weight, gate_weight, out_weight, pair_out, far_out=(0,),
    )
    (grads0,) = call(
        outgoing_back_kernel, "outgoing_back", [(DOUBLE_SHAPE, BF16)], [], exchange(grad0), back, left0, right0
    )
    pair_grad, parts = call(
        last_kernel, "last", [(FLAT, F32), (WEIGHTS_SHAPE, BF16)], [double],
        exchange(grads0), upstream, normed0, inverse0, kept0, gate_up0, proj_weight, gate_weight,
        proj_part1, gate_part1, out_part1, out_part0,
    )
    (sums,) = call(sum_kernel, "sum", [(WEIGHTS_SHAPE, BF16)], [], exchange(parts))
    outs = [((2,) + PROJ, F32), ((2,) + WEIGHT, F32), ((2,) + WEIGHT, F32), (BLOCK, F32)]
    proj_grad, gate_grad, out_grad, pair_grad = call(
        spread_kernel, "spread", outs, [pltpu.VMEM(shape, kind) for shape, kind in outs] + [DMA((4 + TILES,))],
        exchange(sums), pair_grad, far_out=range(4),
    )
    return (
        pair_out.reshape(ROWS, COLS, CHANNELS),
        pair_grad.reshape(ROWS, COLS, CHANNELS),
        proj_grad,
        gate_grad,
        out_grad,
    )


def solution(mesh):
    in_specs = (P("row", "col", None), P(), P(), P(), P("row", "col", None))
    out_specs = (P("row", "col", None), P("row", "col", None), P(), P(), P())
    return jax.shard_map(local, mesh=mesh, in_specs=in_specs, out_specs=out_specs, check_vma=False)
```

```python
import jax
import jax.numpy as jnp
from jax import lax
from jax.experimental import pallas as pl
from jax.experimental.pallas import tpu as pltpu
from jax.sharding import PartitionSpec as P

EPSILON = 1e-05
F32 = jnp.float32
BF16 = jnp.bfloat16
AXES = ("row", "col")

PARTS_R, PARTS_C = 16, 8
DEVICES = PARTS_R * PARTS_C
ROWS, COLS, CHANNELS = 20, 40, 128
PER = 3
TILES = 7
SUBS = 8
LANES = 128
SIZE = 320
WIDE = 384
SINGLE, DOUBLE, WEIGHTS = 8, 14, 12


def dot(first_op, second_op, first_dim, second_dim):
    return lax.dot_general(
        first_op,
        second_op,
        (((first_dim,), (second_dim,)), ((), ())),
        preferred_element_type=F32,
    )


def mean0(values):
    return jnp.sum(values, axis=0, keepdims=True) * (1.0 / CHANNELS)


def norm_parts(values):
    centered = values - mean0(values)
    inverse = lax.rsqrt(mean0(centered * centered) + EPSILON)
    return centered * inverse, inverse


def norm_back(normed, inverse, upstream):
    return inverse * (upstream - mean0(upstream) - normed * mean0(upstream * normed))


def sigmoid(values):
    return 0.5 * jnp.tanh(0.5 * values) + 0.5


def identity():
    shape = (CHANNELS, CHANNELS)
    same = lax.broadcasted_iota(jnp.int32, shape, 0) == lax.broadcasted_iota(jnp.int32, shape, 1)
    return jnp.where(same, 1.0, 0.0).astype(BF16)


def block_in(ref):
    values = ref[...].astype(F32)
    pieces = []
    for s in range(TILES):
        low = s * PER * COLS
        high = min(low + PER * COLS, ROWS * COLS)
        pieces += [values[low:high], jnp.zeros((LANES - (high - low), CHANNELS), F32)]
    return dot(identity(), jnp.concatenate(pieces, axis=0).astype(BF16), 1, 1)


def block_out_exact(values):
    pieces = []
    for s in range(TILES):
        count = min(PER * COLS, ROWS * COLS - s * PER * COLS)
        pieces.append(dot(identity(), values[:, s * LANES : (s + 1) * LANES], 1, 1)[:count])
    return jnp.concatenate(pieces, axis=0).astype(BF16)


def rows_of(parts):
    return SINGLE if parts == 1 else DOUBLE


def pitch_of(parts):
    return SINGLE + 1 if parts == 1 else DOUBLE


def pack(parts, out_ref, wide):
    pitch = pitch_of(len(parts))
    for a, part in enumerate(parts):
        for s in range(TILES):
            wide[pl.ds(a * TILES + s, CHANNELS, stride=pitch), :] = part[:, s * LANES : (s + 1) * LANES]
    if len(parts) == 1:
        wide[pl.ds(TILES, CHANNELS, stride=pitch), :] = jnp.zeros((CHANNELS, LANES), F32)
        for d in range(0, CHANNELS, 2):
            two = [wide[e * pitch : e * pitch + SINGLE, :] for e in (d, d + 1)]
            out_ref[d * SINGLE : (d + 2) * SINGLE, :] = jnp.concatenate(two, axis=0).astype(BF16)
    else:
        out_ref[...] = wide[: DEVICES * DOUBLE, :].astype(BF16)


def unpack(ref, wide, count):
    pitch = pitch_of(count)
    if count == 1:
        for d in range(0, CHANNELS, 2):
            two = ref[d * SINGLE : (d + 2) * SINGLE, :].astype(F32)
            for e in range(2):
                wide[(d + e) * pitch : (d + e) * pitch + SINGLE, :] = two[e * SINGLE : (e + 1) * SINGLE]
    else:
        wide[: DEVICES * DOUBLE, :] = ref[...].astype(F32)
    return [
        jnp.concatenate([wide[pl.ds(a * TILES + s, CHANNELS, stride=pitch), :] for s in range(TILES)], axis=1)
        for a in range(count)
    ]


def pieces_in(ref, count, clean=()):
    values = ref[...].astype(F32).reshape(PARTS_R, -1, SUBS, LANES)
    if count == 1:
        return [[values[:, c].reshape(LANES, LANES) for c in range(PARTS_C)]]
    sub = lax.broadcasted_iota(jnp.int32, (PARTS_R, SUBS, LANES), 1)
    parts = []
    for a in range(count):
        parts.append([])
        for c in range(PARTS_C):
            tile, shift = divmod(c * DOUBLE + a * TILES, SUBS)
            piece = values[:, tile]
            if shift + TILES > SUBS:
                piece = jnp.where(sub >= shift, piece, values[:, tile + 1])
            if shift:
                piece = pltpu.roll(piece, SUBS - shift, 1)
            if a in clean:
                piece = jnp.where(sub < TILES, piece, 0.0)
            parts[a].append(piece.reshape(LANES, LANES))
    return parts


def matrix_of(pieces):
    lane = lax.broadcasted_iota(jnp.int32, (LANES, LANES), 1)
    pieces = [piece.astype(BF16) for piece in pieces]
    rows = []
    for t in range(PER):
        turned = [
            pltpu.roll(pieces[c], ((c - t) * COLS) % LANES, 1) if (c - t) * COLS % LANES else pieces[c]
            for c in range(PARTS_C)
        ]
        tiles = []
        for q in range(WIDE // LANES):
            low, high = q * LANES, (q + 1) * LANES
            inside = [c for c in range(PARTS_C) if c * COLS < high and (c + 1) * COLS > low]
            tile = turned[inside[0]]
            for c in inside[1:]:
                tile = jnp.where(lane >= c * COLS - low, turned[c], tile)
            if high > SIZE:
                tile = jnp.where(lane < SIZE - low, tile, jnp.zeros_like(tile))
            tiles.append(tile)
        rows.append(jnp.concatenate(tiles, axis=1))
    return jnp.concatenate(rows, axis=0)


def pieces_of(values):
    values = values.astype(BF16)
    lane = lax.broadcasted_iota(jnp.int32, (LANES, LANES), 1)
    pieces = []
    for c in range(PARTS_C):
        low = c * COLS
        first, last = low // LANES, (low + COLS - 1) // LANES
        piece = None
        for t in range(PER):
            band = values[t * LANES : (t + 1) * LANES]
            source = band[:, first * LANES : (first + 1) * LANES]
            if last != first:
                source = jnp.where(lane >= low % LANES, source, band[:, last * LANES : (last + 1) * LANES])
            shift = ((t - c) * COLS) % LANES
            if shift:
                source = pltpu.roll(source, shift, 1)
            piece = source if piece is None else jnp.where(lane >= t * COLS, source, piece)
        pieces.append(jnp.where(lane < PER * COLS, piece, jnp.zeros_like(piece)).astype(F32))
    return pieces


def pieces_out(parts, ref):
    if len(parts) == 1:
        tiles = [piece.reshape(PARTS_R, SUBS, LANES) for piece in parts[0]]
    else:
        sub = lax.broadcasted_iota(jnp.int32, (PARTS_R, SUBS, LANES), 1)
        tiles = [None] * (PARTS_C * DOUBLE // SUBS)
        for c in range(PARTS_C):
            for a, pieces in enumerate(parts):
                tile, shift = divmod(c * DOUBLE + a * TILES, SUBS)
                piece = pieces[c].reshape(PARTS_R, SUBS, LANES)
                if shift:
                    piece = pltpu.roll(piece, shift, 1)
                tiles[tile] = piece if tiles[tile] is None else jnp.where(sub >= shift, piece, tiles[tile])
                if shift + TILES > SUBS:
                    tiles[tile + 1] = piece
    values = jnp.concatenate([tile[:, None] for tile in tiles], axis=1)
    ref[...] = values.reshape(-1, LANES).astype(BF16)


def first_to_second():
    index = lax.broadcasted_iota(jnp.int32, (1, WIDE), 1)
    part, s, t = (index % LANES) // SUBS, index % SUBS, index // LANES
    inner = PER * s + t
    residue = jnp.where((s < TILES) & (inner < ROWS), part * ROWS + inner, -1)
    second = lax.broadcasted_iota(jnp.int32, (WIDE, WIDE), 0)
    return jnp.where(second == residue, 1.0, 0.0).astype(BF16)


def second_to_first():
    index = lax.broadcasted_iota(jnp.int32, (WIDE, 1), 0)
    part, s, t = (index % LANES) // SUBS, index % SUBS, index // LANES
    inner = PER * s + t
    residue = jnp.where((s < TILES) & (inner < ROWS), part * ROWS + inner, -1)
    second = lax.broadcasted_iota(jnp.int32, (WIDE, WIDE), 1)
    return jnp.where(second == residue, 1.0, 0.0).astype(BF16)


def edges(normed, proj_mat, kept_ref):
    projected = dot(proj_mat, normed, 0, 0)
    p1, p2, p3, p4 = [projected[q * CHANNELS : (q + 1) * CHANNELS] for q in range(4)]
    s1, s3 = sigmoid(p1), sigmoid(p3)
    left, right = s1 * p2, s3 * p4
    for q, value in enumerate((s1, left, s3, right)):
        kept_ref[q] = value
    return left, right


def back_head(upstream, gating, product, normed_mix, mix_normed, mix_inverse, out_mat):
    through = (upstream * gating).astype(BF16)
    gate_up = (upstream * product * gating * (1.0 - gating)).astype(BF16)
    mix_up = dot(out_mat, through, 1, 0)
    out_part = dot(normed_mix, through, 1, 1)
    return norm_back(mix_normed, mix_inverse, mix_up), out_part, gate_up


def back_tail(upstream, pair_normed, pair_inverse, kept_ref, left_grad, right_grad, gate_up, proj_mat, gate_mat):
    s1, left, s3, right = [kept_ref[q] for q in range(4)]
    proj_up = jnp.concatenate(
        [left_grad * left * (1.0 - s1), left_grad * s1, right_grad * right * (1.0 - s3), right_grad * s3], axis=0
    ).astype(BF16)
    normed_up = dot(proj_mat, proj_up, 1, 0) + dot(gate_mat, gate_up, 1, 0)
    return upstream + norm_back(pair_normed, pair_inverse, normed_up), proj_up


def start_kernel(pair_ref, proj_ref, _, message_ref, flat_ref, normed_ref, inverse_ref, kept_ref, wide):
    pair = block_in(pair_ref)
    flat_ref[...] = pair.astype(BF16)
    pair_normed, inverse = norm_parts(pair)
    normed_ref[...] = pair_normed
    inverse_ref[...] = inverse
    pack(edges(pair_normed.astype(BF16), proj_ref[0], kept_ref), message_ref, wide)


def middle_kernel(
    mix_ref, pair_ref, gating0_ref, proj_ref, gate_ref, out_ref,
    message_ref, mix_normed_ref, mix_inverse_ref, product_ref, after_ref, normed_ref, inverse_ref, kept_ref,
    gating_ref, narrow, wide,
):
    (mix,) = unpack(mix_ref, narrow, 1)
    mix_normed, mix_inverse = norm_parts(mix)
    mix_normed_ref[...] = mix_normed
    mix_inverse_ref[...] = mix_inverse
    product = dot(out_ref[0], mix_normed.astype(BF16), 0, 0)
    product_ref[...] = product
    after = (pair_ref[...].astype(F32) + gating0_ref[...] * product).astype(BF16)
    after_ref[...] = after
    pair_normed, inverse = norm_parts(after.astype(F32))
    normed_ref[...] = pair_normed
    inverse_ref[...] = inverse
    normed = pair_normed.astype(BF16)
    pack(edges(normed, proj_ref[1], kept_ref), message_ref, wide)
    gating_ref[...] = sigmoid(dot(gate_ref[1], normed, 0, 0))


def turn_kernel(mix_ref, mix_up_ref, message_ref, normed_mix_ref, narrow):
    (mix,) = unpack(mix_ref, narrow, 1)
    mix_normed, mix_inverse = norm_parts(mix)
    normed_mix_ref[...] = mix_normed.astype(BF16)
    mix_up = mix_up_ref[...]
    pack([mix_inverse * (mix_up - mix_normed * mean0(mix_up * mix_normed))], message_ref, narrow)


def before_turn(cot_ref, gating_ref, out_ref, cot_flat_ref, through_ref, mix_up_ref):
    cot = block_in(cot_ref)
    cot_flat_ref[...] = cot.astype(BF16)
    through = (cot * gating_ref[...]).astype(BF16)
    through_ref[...] = through
    mix_up = dot(out_ref[1], through, 1, 0)
    mix_up_ref[...] = mix_up - mean0(mix_up)


def after_turn(
    normed_mix_ref, after_ref, gating_ref, cot_ref, through_ref, out_ref, normed_ref,
    pair_out_ref, gate_up_ref, gate_part_ref, out_part_ref,
):
    normed_mix = normed_mix_ref[...]
    product = dot(out_ref[1], normed_mix, 0, 0)
    gating = gating_ref[...]
    pair_out_ref[...] = (after_ref[...].astype(F32) + gating * product).astype(BF16)
    gate_up = (cot_ref[...].astype(F32) * product * gating * (1.0 - gating)).astype(BF16)
    gate_up_ref[...] = gate_up
    gate_part_ref[...] = dot(normed_ref[...].astype(BF16), gate_up, 1, 1)
    out_part_ref[...] = dot(normed_mix, through_ref[...], 1, 1)


def back_kernel(
    grads_ref, cot_ref, normed1_ref, inverse1_ref, kept1_ref, gate_up1_ref, mix_normed_ref, mix_inverse_ref,
    product_ref, gating0_ref, proj_ref, gate_ref, out_ref, pair_out_ref,
    pair_out_hbm, message_ref, upstream_ref, gate_up_ref, proj_part_ref, out_part_ref, narrow, wide, pair_out, sem,
):
    pair_out[...] = block_out_exact(pair_out_ref[...])
    copy = pltpu.make_async_copy(pair_out, pair_out_hbm, sem)
    copy.start()
    left_grad, right_grad = unpack(grads_ref, wide, 2)
    pair_normed = normed1_ref[...]
    upstream, proj_up = back_tail(
        cot_ref[...].astype(F32), pair_normed, inverse1_ref[...], kept1_ref, left_grad, right_grad, gate_up1_ref[...],
        proj_ref[1], gate_ref[1],
    )
    upstream_ref[...] = upstream
    proj_part_ref[...] = dot(pair_normed.astype(BF16), proj_up, 1, 1)
    mix_normed = mix_normed_ref[...]
    mix_grad, out_part, gate_up = back_head(
        upstream, gating0_ref[...], product_ref[...], mix_normed.astype(BF16), mix_normed, mix_inverse_ref[...],
        out_ref[0],
    )
    pack([mix_grad], message_ref, narrow)
    out_part_ref[...] = out_part
    gate_up_ref[...] = gate_up
    copy.wait()


def last_kernel(
    grads_ref, upstream_ref, normed_ref, inverse_ref, kept_ref, gate_up_ref, proj_ref, gate_ref,
    proj1_ref, gate1_ref, out1_ref, out0_ref,
    pair_grad_ref, message_ref, wide,
):
    left_grad, right_grad = unpack(grads_ref, wide, 2)
    pair_normed = normed_ref[...]
    gate_up = gate_up_ref[...]
    total, proj_up = back_tail(
        upstream_ref[...], pair_normed, inverse_ref[...], kept_ref, left_grad, right_grad, gate_up,
        proj_ref[0], gate_ref[0],
    )
    pair_grad_ref[...] = total
    normed = pair_normed.astype(BF16)
    proj_part = dot(normed, proj_up, 1, 1)
    parts = [proj_part[:, q * LANES : (q + 1) * LANES] for q in range(4)]
    parts += [proj1_ref[:, q * LANES : (q + 1) * LANES] for q in range(4)]
    parts += [dot(normed, gate_up, 1, 1), gate1_ref[...], out0_ref[...], out1_ref[...]]
    for q, part in enumerate(parts):
        message_ref[q * CHANNELS : (q + 1) * CHANNELS, :] = part.astype(BF16)


def sum_kernel(parts_ref, total_ref):
    pairs = parts_ref[...].astype(F32).reshape(DEVICES // 2, 2 * WEIGHTS, LANES)
    total = jnp.sum(pairs, axis=0)
    total = (total[:WEIGHTS] + total[WEIGHTS:]) * (1.0 / SIZE)
    total = jnp.concatenate([total, total], axis=0)[None]
    total_ref[...] = jnp.broadcast_to(total, pairs.shape).reshape(DEVICES * WEIGHTS, LANES).astype(BF16)


def spread_kernel(
    sums_ref, pair_grad_ref, proj_hbm, gate_hbm, out_hbm, pair_grad_hbm, proj, gate, out, pair_grad, sems,
):
    copies = []

    def send(source, target):
        copies.append(pltpu.make_async_copy(source, target, sems.at[len(copies)]))
        copies[-1].start()

    parts = [sums_ref[q * CHANNELS : (q + 1) * CHANNELS, :].astype(F32) for q in range(WEIGHTS)]
    for l in range(2):
        proj[l] = jnp.concatenate(parts[4 * l : 4 * l + 4], axis=1)
        send(proj.at[l], proj_hbm.at[l])
    for l in range(2):
        gate[l], out[l] = parts[8 + l], parts[10 + l]
    send(gate, gate_hbm)
    send(out, out_hbm)
    for s in range(TILES):
        low = s * PER * COLS
        count = min(PER * COLS, ROWS * COLS - low)
        pair_grad[low : low + count, :] = pair_grad_ref[:, s * LANES : (s + 1) * LANES].T[:count]
        send(pair_grad.at[pl.ds(low, count)], pair_grad_hbm.at[pl.ds(low, count)])
    for copy in copies:
        copy.wait()


def orders_kernel(forth_ref, back_ref):
    forth_ref[...] = first_to_second()
    back_ref[...] = second_to_first()


def outgoing_kernel(edges_ref, forth_ref, normed_ref, gate_ref, mix_ref, left_ref, right_ref, gating_ref):
    left, right = [matrix_of(pieces) for pieces in pieces_in(edges_ref, 2)]
    right = dot(forth_ref[...], right, 1, 0).astype(BF16)
    left_ref[...], right_ref[...] = left, right
    pieces_out([pieces_of(dot(left, right, 1, 1))], mix_ref)
    gating_ref[...] = sigmoid(dot(gate_ref[0], normed_ref[...].astype(BF16), 0, 0))


def incoming_kernel(edges_ref, back_ref, cot_ref, gating_ref, out_ref, mix_ref, left_ref, right_ref, *side):
    left, right = [matrix_of(pieces) for pieces in pieces_in(edges_ref, 2, (0,))]
    turned = dot(back_ref[...], left, 1, 1).astype(BF16)
    left_ref[...], right_ref[...] = turned, right
    pieces_out([pieces_of(dot(turned, right, 1, 0))], mix_ref)
    before_turn(cot_ref, gating_ref, out_ref, *side)


def incoming_back_kernel(grad_ref, back_ref, left_ref, right_ref, *side):
    *side, grads_ref = side
    grad = matrix_of(pieces_in(grad_ref, 1)[0])
    left_grad = dot(right_ref[...], grad, 1, 1).astype(BF16)
    right_grad = dot(left_ref[...], grad, 0, 0)
    pieces_out([pieces_of(dot(left_grad, back_ref[...], 1, 0)), pieces_of(right_grad)], grads_ref)
    after_turn(*side)


def outgoing_back_kernel(grad_ref, back_ref, left_ref, right_ref, grads_ref):
    grad = matrix_of(pieces_in(grad_ref, 1)[0])
    turned = dot(back_ref[...], grad, 1, 1).astype(BF16)
    pieces_out([pieces_of(dot(grad, right_ref[...], 1, 0)), pieces_of(dot(turned, left_ref[...], 1, 0))], grads_ref)


SINGLE_SHAPE = (DEVICES * SINGLE, LANES)
DOUBLE_SHAPE = (DEVICES * DOUBLE, LANES)
WEIGHTS_SHAPE = (DEVICES * WEIGHTS, LANES)
BLOCK = (ROWS * COLS, CHANNELS)
FLAT = (CHANNELS, TILES * LANES)
KEPT = (4, CHANNELS, TILES * LANES)
LINE = (1, TILES * LANES)
SQUARE = (WIDE, WIDE)
WEIGHT = (CHANNELS, CHANNELS)
PROJ = (CHANNELS, 4 * CHANNELS)
DMA = pltpu.SemaphoreType.DMA


def call(kernel, name, outs, scratch, *operands, far_out=(), flops=None):
    def spec(far):
        return pl.BlockSpec(memory_space=pl.ANY if far else pltpu.VMEM)

    return pl.pallas_call(
        kernel,
        out_shape=[jax.ShapeDtypeStruct(shape, kind) for shape, kind in outs],
        in_specs=[spec(False) for _ in operands],
        out_specs=[spec(position in far_out) for position in range(len(outs))],
        scratch_shapes=scratch,
        cost_estimate=flops and pl.CostEstimate(flops=flops, bytes_accessed=0, transcendentals=0),
        compiler_params=pltpu.CompilerParams(vmem_limit_bytes=24 * 1024 * 1024),
        name=name,
    )(*operands)


def exchange(message):
    rows = message.shape[0] // DEVICES
    shape = (DEVICES, rows, LANES)
    for low in (4, 2):
        if rows % 8 and rows % low == 0:
            shape = (DEVICES, rows // low, low, LANES)
            break
    return lax.all_to_all(message.reshape(shape), AXES, 0, 0, tiled=True).reshape(message.shape)


def local(pair_rep, proj_weight, gate_weight, out_weight, pair_cot):
    pair = pair_rep.reshape(BLOCK)
    cot = pair_cot.reshape(BLOCK)
    double = pltpu.VMEM((DEVICES * DOUBLE + 16, LANES), F32)
    spaced = pltpu.VMEM((DEVICES * (SINGLE + 1) + 16, LANES), F32)
    forth, back = call(orders_kernel, "orders", [(SQUARE, BF16), (SQUARE, BF16)], [], flops=4 * 1024**3)
    edges0, pair0, normed0, inverse0, kept0 = call(
        start_kernel, "start", [(DOUBLE_SHAPE, BF16), (FLAT, BF16), (FLAT, F32), (LINE, F32), (KEPT, F32)], [double],
        pair, proj_weight, forth,
    )
    mix0, left0, right0, gating0 = call(
        outgoing_kernel, "outgoing", [(SINGLE_SHAPE, BF16), (SQUARE, BF16), (SQUARE, BF16), (FLAT, F32)], [],
        exchange(edges0), forth, normed0, gate_weight,
    )
    edges1, mix_normed0, mix_inverse0, product0, after, normed1, inverse1, kept1, gating1 = call(
        middle_kernel, "middle",
        [
            (DOUBLE_SHAPE, BF16), (FLAT, F32), (LINE, F32), (FLAT, F32), (FLAT, BF16), (FLAT, F32),
            (LINE, F32), (KEPT, F32), (FLAT, F32),
        ],
        [spaced, double], exchange(mix0), pair0, gating0, proj_weight, gate_weight, out_weight,
    )
    mix1, left1, right1, cot1, through1, mix_up1 = call(
        incoming_kernel, "incoming",
        [(SINGLE_SHAPE, BF16), (SQUARE, BF16), (SQUARE, BF16), (FLAT, BF16), (FLAT, BF16), (FLAT, F32)], [],
        exchange(edges1), back, cot, gating1, out_weight,
    )
    grad1, normed_mix1 = call(
        turn_kernel, "turn", [(SINGLE_SHAPE, BF16), (FLAT, BF16)], [spaced], exchange(mix1), mix_up1
    )
    pair_out, gate_up1, gate_part1, out_part1, grads1 = call(
        incoming_back_kernel, "incoming_back",
        [(FLAT, BF16), (FLAT, BF16), (WEIGHT, F32), (WEIGHT, F32), (DOUBLE_SHAPE, BF16)], [],
        exchange(grad1), back, left1, right1, normed_mix1, after, gating1, cot1, through1, out_weight, normed1,
    )
    pair_out, grad0, upstream, gate_up0, proj_part1, out_part0 = call(
        back_kernel, "back",
        [(BLOCK, BF16), (SINGLE_SHAPE, BF16), (FLAT, F32), (FLAT, BF16), (PROJ, F32), (WEIGHT, F32)],
        [spaced, double, pltpu.VMEM(BLOCK, BF16), DMA], exchange(grads1), cot1, normed1, inverse1, kept1, gate_up1, mix_normed0, mix_inverse0,
        product0, gating0, proj_weight, gate_weight, out_weight, pair_out, far_out=(0,),
    )
    (grads0,) = call(
        outgoing_back_kernel, "outgoing_back", [(DOUBLE_SHAPE, BF16)], [], exchange(grad0), back, left0, right0
    )
    pair_grad, parts = call(
        last_kernel, "last", [(FLAT, F32), (WEIGHTS_SHAPE, BF16)], [double],
        exchange(grads0), upstream, normed0, inverse0, kept0, gate_up0, proj_weight, gate_weight,
        proj_part1, gate_part1, out_part1, out_part0,
    )
    (sums,) = call(sum_kernel, "sum", [(WEIGHTS_SHAPE, BF16)], [], exchange(parts))
    outs = [((2,) + PROJ, F32), ((2,) + WEIGHT, F32), ((2,) + WEIGHT, F32), (BLOCK, F32)]
    proj_grad, gate_grad, out_grad, pair_grad = call(
        spread_kernel, "spread", outs, [pltpu.VMEM(shape, kind) for shape, kind in outs] + [DMA((4 + TILES,))],
        exchange(sums), pair_grad, far_out=range(4),
    )
    return (
        pair_out.reshape(ROWS, COLS, CHANNELS),
        pair_grad.reshape(ROWS, COLS, CHANNELS),
        proj_grad,
        gate_grad,
        out_grad,
    )


def solution(mesh):
    in_specs = (P("row", "col", None), P(), P(), P(), P("row", "col", None))
    out_specs = (P("row", "col", None), P("row", "col", None), P(), P(), P())
    return jax.shard_map(local, mesh=mesh, in_specs=in_specs, out_specs=out_specs, check_vma=False)
```

```python
import jax
import jax.numpy as jnp
from jax import lax
from jax.experimental import pallas as pl
from jax.experimental.pallas import tpu as pltpu
from jax.sharding import PartitionSpec as P

EPSILON = 1e-05
F32 = jnp.float32
BF16 = jnp.bfloat16
AXES = ("row", "col")

PARTS_R, PARTS_C = 16, 8
DEVICES = PARTS_R * PARTS_C
ROWS, COLS, CHANNELS = 20, 40, 128
PER = 3
TILES = 7
SUBS = 8
LANES = 128
SIZE = 320
WIDE = 384
SINGLE, DOUBLE, WEIGHTS = 8, 14, 12


def dot(first_op, second_op, first_dim, second_dim):
    return lax.dot_general(
        first_op,
        second_op,
        (((first_dim,), (second_dim,)), ((), ())),
        preferred_element_type=F32,
    )


def mean0(values):
    return jnp.sum(values, axis=0, keepdims=True) * (1.0 / CHANNELS)


def norm_parts(values):
    centered = values - mean0(values)
    inverse = lax.rsqrt(mean0(centered * centered) + EPSILON)
    return centered * inverse, inverse


def norm_back(normed, inverse, upstream):
    return inverse * (upstream - mean0(upstream) - normed * mean0(upstream * normed))


def sigmoid(values):
    return 0.5 * jnp.tanh(0.5 * values) + 0.5


def identity():
    shape = (CHANNELS, CHANNELS)
    same = lax.broadcasted_iota(jnp.int32, shape, 0) == lax.broadcasted_iota(jnp.int32, shape, 1)
    return jnp.where(same, 1.0, 0.0).astype(BF16)


def block_in(ref):
    values = ref[...].astype(F32)
    pieces = []
    for s in range(TILES):
        low = s * PER * COLS
        high = min(low + PER * COLS, ROWS * COLS)
        pieces += [values[low:high], jnp.zeros((LANES - (high - low), CHANNELS), F32)]
    return dot(identity(), jnp.concatenate(pieces, axis=0).astype(BF16), 1, 1)


def block_out_exact(values):
    pieces = []
    for s in range(TILES):
        count = min(PER * COLS, ROWS * COLS - s * PER * COLS)
        pieces.append(dot(identity(), values[:, s * LANES : (s + 1) * LANES], 1, 1)[:count])
    return jnp.concatenate(pieces, axis=0).astype(BF16)


def rows_of(parts):
    return SINGLE if parts == 1 else DOUBLE


def pitch_of(parts):
    return SINGLE + 1 if parts == 1 else DOUBLE


def pack(parts, out_ref, wide):
    pitch = pitch_of(len(parts))
    for a, part in enumerate(parts):
        for s in range(TILES):
            wide[pl.ds(a * TILES + s, CHANNELS, stride=pitch), :] = part[:, s * LANES : (s + 1) * LANES]
    if len(parts) == 1:
        wide[pl.ds(TILES, CHANNELS, stride=pitch), :] = jnp.zeros((CHANNELS, LANES), F32)
        for d in range(0, CHANNELS, 2):
            two = [wide[e * pitch : e * pitch + SINGLE, :] for e in (d, d + 1)]
            out_ref[d * SINGLE : (d + 2) * SINGLE, :] = jnp.concatenate(two, axis=0).astype(BF16)
    else:
        out_ref[...] = wide[: DEVICES * DOUBLE, :].astype(BF16)


def unpack(ref, wide, count):
    pitch = pitch_of(count)
    if count == 1:
        for d in range(0, CHANNELS, 2):
            two = ref[d * SINGLE : (d + 2) * SINGLE, :].astype(F32)
            for e in range(2):
                wide[(d + e) * pitch : (d + e) * pitch + SINGLE, :] = two[e * SINGLE : (e + 1) * SINGLE]
    else:
        wide[: DEVICES * DOUBLE, :] = ref[...].astype(F32)
    return [
        jnp.concatenate([wide[pl.ds(a * TILES + s, CHANNELS, stride=pitch), :] for s in range(TILES)], axis=1)
        for a in range(count)
    ]


def pieces_in(ref, count, clean=()):
    values = ref[...].astype(F32).reshape(PARTS_R, -1, SUBS, LANES)
    if count == 1:
        return [[values[:, c].reshape(LANES, LANES) for c in range(PARTS_C)]]
    sub = lax.broadcasted_iota(jnp.int32, (PARTS_R, SUBS, LANES), 1)
    parts = []
    for a in range(count):
        parts.append([])
        for c in range(PARTS_C):
            tile, shift = divmod(c * DOUBLE + a * TILES, SUBS)
            piece = values[:, tile]
            if shift + TILES > SUBS:
                piece = jnp.where(sub >= shift, piece, values[:, tile + 1])
            if shift:
                piece = pltpu.roll(piece, SUBS - shift, 1)
            if a in clean:
                piece = jnp.where(sub < TILES, piece, 0.0)
            parts[a].append(piece.reshape(LANES, LANES))
    return parts


def matrix_of(pieces):
    lane = lax.broadcasted_iota(jnp.int32, (LANES, LANES), 1)
    pieces = [piece.astype(BF16) for piece in pieces]
    rows = []
    for t in range(PER):
        turned = [
            pltpu.roll(pieces[c], ((c - t) * COLS) % LANES, 1) if (c - t) * COLS % LANES else pieces[c]
            for c in range(PARTS_C)
        ]
        tiles = []
        for q in range(WIDE // LANES):
            low, high = q * LANES, (q + 1) * LANES
            inside = [c for c in range(PARTS_C) if c * COLS < high and (c + 1) * COLS > low]
            tile = turned[inside[0]]
            for c in inside[1:]:
                tile = jnp.where(lane >= c * COLS - low, turned[c], tile)
            if high > SIZE:
                tile = jnp.where(lane < SIZE - low, tile, jnp.zeros_like(tile))
            tiles.append(tile)
        rows.append(jnp.concatenate(tiles, axis=1))
    return jnp.concatenate(rows, axis=0)


def pieces_of(values):
    values = values.astype(BF16)
    lane = lax.broadcasted_iota(jnp.int32, (LANES, LANES), 1)
    pieces = []
    for c in range(PARTS_C):
        low = c * COLS
        first, last = low // LANES, (low + COLS - 1) // LANES
        piece = None
        for t in range(PER):
            band = values[t * LANES : (t + 1) * LANES]
            source = band[:, first * LANES : (first + 1) * LANES]
            if last != first:
                source = jnp.where(lane >= low % LANES, source, band[:, last * LANES : (last + 1) * LANES])
            shift = ((t - c) * COLS) % LANES
            if shift:
                source = pltpu.roll(source, shift, 1)
            piece = source if piece is None else jnp.where(lane >= t * COLS, source, piece)
        pieces.append(jnp.where(lane < PER * COLS, piece, jnp.zeros_like(piece)).astype(F32))
    return pieces


def pieces_out(parts, ref):
    if len(parts) == 1:
        tiles = [piece.reshape(PARTS_R, SUBS, LANES) for piece in parts[0]]
    else:
        sub = lax.broadcasted_iota(jnp.int32, (PARTS_R, SUBS, LANES), 1)
        tiles = [None] * (PARTS_C * DOUBLE // SUBS)
        for c in range(PARTS_C):
            for a, pieces in enumerate(parts):
                tile, shift = divmod(c * DOUBLE + a * TILES, SUBS)
                piece = pieces[c].reshape(PARTS_R, SUBS, LANES)
                if shift:
                    piece = pltpu.roll(piece, shift, 1)
                tiles[tile] = piece if tiles[tile] is None else jnp.where(sub >= shift, piece, tiles[tile])
                if shift + TILES > SUBS:
                    tiles[tile + 1] = piece
    values = jnp.concatenate([tile[:, None] for tile in tiles], axis=1)
    ref[...] = values.reshape(-1, LANES).astype(BF16)


def first_to_second():
    index = lax.broadcasted_iota(jnp.int32, (1, WIDE), 1)
    part, s, t = (index % LANES) // SUBS, index % SUBS, index // LANES
    inner = PER * s + t
    residue = jnp.where((s < TILES) & (inner < ROWS), part * ROWS + inner, -1)
    second = lax.broadcasted_iota(jnp.int32, (WIDE, WIDE), 0)
    return jnp.where(second == residue, 1.0, 0.0).astype(BF16)


def second_to_first():
    index = lax.broadcasted_iota(jnp.int32, (WIDE, 1), 0)
    part, s, t = (index % LANES) // SUBS, index % SUBS, index // LANES
    inner = PER * s + t
    residue = jnp.where((s < TILES) & (inner < ROWS), part * ROWS + inner, -1)
    second = lax.broadcasted_iota(jnp.int32, (WIDE, WIDE), 1)
    return jnp.where(second == residue, 1.0, 0.0).astype(BF16)


def edges(normed, proj_mat, kept_ref):
    projected = dot(proj_mat, normed, 0, 0)
    p1, p2, p3, p4 = [projected[q * CHANNELS : (q + 1) * CHANNELS] for q in range(4)]
    s1, s3 = sigmoid(p1), sigmoid(p3)
    left, right = s1 * p2, s3 * p4
    for q, value in enumerate((s1, left, s3, right)):
        kept_ref[q] = value
    return left, right


def back_head(upstream, gating, product, normed_mix, mix_normed, mix_inverse, out_mat):
    through = (upstream * gating).astype(BF16)
    gate_up = (upstream * product * gating * (1.0 - gating)).astype(BF16)
    mix_up = dot(out_mat, through, 1, 0)
    out_part = dot(normed_mix, through, 1, 1)
    return norm_back(mix_normed, mix_inverse, mix_up), out_part, gate_up


def back_tail(upstream, pair_normed, pair_inverse, kept_ref, left_grad, right_grad, gate_up, proj_mat, gate_mat):
    s1, left, s3, right = [kept_ref[q] for q in range(4)]
    proj_up = jnp.concatenate(
        [left_grad * left * (1.0 - s1), left_grad * s1, right_grad * right * (1.0 - s3), right_grad * s3], axis=0
    ).astype(BF16)
    normed_up = dot(proj_mat, proj_up, 1, 0) + dot(gate_mat, gate_up, 1, 0)
    return upstream + norm_back(pair_normed, pair_inverse, normed_up), proj_up


def start_kernel(pair_ref, proj_ref, _, message_ref, normed_ref, inverse_ref, kept_ref, wide):
    pair = block_in(pair_ref)
    pair_normed, inverse = norm_parts(pair)
    normed_ref[...] = pair_normed
    inverse_ref[...] = inverse
    pack(edges(pair_normed.astype(BF16), proj_ref[0], kept_ref), message_ref, wide)


def middle_kernel(
    mix_ref, pair_ref, gating0_ref, proj_ref, gate_ref, out_ref,
    message_ref, mix_normed_ref, mix_inverse_ref, product_ref, after_ref, normed_ref, inverse_ref, kept_ref,
    gating_ref, narrow, wide,
):
    (mix,) = unpack(mix_ref, narrow, 1)
    mix_normed, mix_inverse = norm_parts(mix)
    mix_normed_ref[...] = mix_normed
    mix_inverse_ref[...] = mix_inverse
    product = dot(out_ref[0], mix_normed.astype(BF16), 0, 0)
    product_ref[...] = product
    after = (pair_ref[...].astype(F32) + gating0_ref[...] * product).astype(BF16)
    after_ref[...] = after
    pair_normed, inverse = norm_parts(after.astype(F32))
    normed_ref[...] = pair_normed
    inverse_ref[...] = inverse
    normed = pair_normed.astype(BF16)
    pack(edges(normed, proj_ref[1], kept_ref), message_ref, wide)
    gating_ref[...] = sigmoid(dot(gate_ref[1], normed, 0, 0))


def turn_kernel(mix_ref, mix_up_ref, message_ref, normed_mix_ref, narrow):
    (mix,) = unpack(mix_ref, narrow, 1)
    mix_normed, mix_inverse = norm_parts(mix)
    normed_mix_ref[...] = mix_normed.astype(BF16)
    mix_up = mix_up_ref[...]
    pack([mix_inverse * (mix_up - mix_normed * mean0(mix_up * mix_normed))], message_ref, narrow)


def before_turn(cot_ref, gating_ref, out_ref, cot_flat_ref, through_ref, mix_up_ref):
    cot = block_in(cot_ref)
    cot_flat_ref[...] = cot.astype(BF16)
    through = (cot * gating_ref[...]).astype(BF16)
    through_ref[...] = through
    mix_up = dot(out_ref[1], through, 1, 0)
    mix_up_ref[...] = mix_up - mean0(mix_up)


def after_turn(
    normed_mix_ref, after_ref, gating_ref, cot_ref, through_ref, out_ref, normed_ref,
    pair_out_ref, gate_up_ref, gate_part_ref, out_part_ref,
):
    normed_mix = normed_mix_ref[...]
    product = dot(out_ref[1], normed_mix, 0, 0)
    gating = gating_ref[...]
    pair_out_ref[...] = (after_ref[...].astype(F32) + gating * product).astype(BF16)
    gate_up = (cot_ref[...].astype(F32) * product * gating * (1.0 - gating)).astype(BF16)
    gate_up_ref[...] = gate_up
    gate_part_ref[...] = dot(normed_ref[...].astype(BF16), gate_up, 1, 1)
    out_part_ref[...] = dot(normed_mix, through_ref[...], 1, 1)


def back_kernel(
    grads_ref, cot_ref, normed1_ref, inverse1_ref, kept1_ref, gate_up1_ref, mix_normed_ref, mix_inverse_ref,
    product_ref, gating0_ref, proj_ref, gate_ref, out_ref, pair_out_ref,
    pair_out_hbm, message_ref, upstream_ref, gate_up_ref, proj_part_ref, out_part_ref, narrow, wide, pair_out, sem,
):
    pair_out[...] = block_out_exact(pair_out_ref[...])
    copy = pltpu.make_async_copy(pair_out, pair_out_hbm, sem)
    copy.start()
    left_grad, right_grad = unpack(grads_ref, wide, 2)
    pair_normed = normed1_ref[...]
    upstream, proj_up = back_tail(
        cot_ref[...].astype(F32), pair_normed, inverse1_ref[...], kept1_ref, left_grad, right_grad, gate_up1_ref[...],
        proj_ref[1], gate_ref[1],
    )
    upstream_ref[...] = upstream
    proj_part_ref[...] = dot(pair_normed.astype(BF16), proj_up, 1, 1)
    mix_normed = mix_normed_ref[...]
    mix_grad, out_part, gate_up = back_head(
        upstream, gating0_ref[...], product_ref[...], mix_normed.astype(BF16), mix_normed, mix_inverse_ref[...],
        out_ref[0],
    )
    pack([mix_grad], message_ref, narrow)
    out_part_ref[...] = out_part
    gate_up_ref[...] = gate_up
    copy.wait()


def last_kernel(
    grads_ref, upstream_ref, normed_ref, inverse_ref, kept_ref, gate_up_ref, proj_ref, gate_ref,
    proj1_ref, gate1_ref, out1_ref, out0_ref,
    pair_grad_ref, message_ref, wide,
):
    left_grad, right_grad = unpack(grads_ref, wide, 2)
    pair_normed = normed_ref[...]
    gate_up = gate_up_ref[...]
    total, proj_up = back_tail(
        upstream_ref[...], pair_normed, inverse_ref[...], kept_ref, left_grad, right_grad, gate_up,
        proj_ref[0], gate_ref[0],
    )
    pair_grad_ref[...] = total
    normed = pair_normed.astype(BF16)
    proj_part = dot(normed, proj_up, 1, 1)
    parts = [proj_part[:, q * LANES : (q + 1) * LANES] for q in range(4)]
    parts += [proj1_ref[:, q * LANES : (q + 1) * LANES] for q in range(4)]
    parts += [dot(normed, gate_up, 1, 1), gate1_ref[...], out0_ref[...], out1_ref[...]]
    for q, part in enumerate(parts):
        message_ref[q * CHANNELS : (q + 1) * CHANNELS, :] = part.astype(BF16)


def sum_kernel(parts_ref, total_ref):
    pairs = parts_ref[...].astype(F32).reshape(DEVICES // 2, 2 * WEIGHTS, LANES)
    total = jnp.sum(pairs, axis=0)
    total = (total[:WEIGHTS] + total[WEIGHTS:]) * (1.0 / SIZE)
    total = jnp.concatenate([total, total], axis=0)[None]
    total_ref[...] = jnp.broadcast_to(total, pairs.shape).reshape(DEVICES * WEIGHTS, LANES).astype(BF16)


def spread_kernel(
    sums_ref, pair_grad_ref, proj_hbm, gate_hbm, out_hbm, pair_grad_hbm, proj, gate, out, pair_grad, sems,
):
    copies = []

    def send(source, target):
        copies.append(pltpu.make_async_copy(source, target, sems.at[len(copies)]))
        copies[-1].start()

    parts = [sums_ref[q * CHANNELS : (q + 1) * CHANNELS, :].astype(F32) for q in range(WEIGHTS)]
    for l in range(2):
        proj[l] = jnp.concatenate(parts[4 * l : 4 * l + 4], axis=1)
        send(proj.at[l], proj_hbm.at[l])
    for l in range(2):
        gate[l], out[l] = parts[8 + l], parts[10 + l]
    send(gate, gate_hbm)
    send(out, out_hbm)
    for s in range(TILES):
        low = s * PER * COLS
        count = min(PER * COLS, ROWS * COLS - low)
        pair_grad[low : low + count, :] = pair_grad_ref[:, s * LANES : (s + 1) * LANES].T[:count]
        send(pair_grad.at[pl.ds(low, count)], pair_grad_hbm.at[pl.ds(low, count)])
    for copy in copies:
        copy.wait()


def orders_kernel(forth_ref, back_ref):
    forth_ref[...] = first_to_second()
    back_ref[...] = second_to_first()


def outgoing_kernel(edges_ref, forth_ref, normed_ref, gate_ref, pair_ref, mix_ref, left_ref, right_ref, gating_ref, flat_ref):
    left, right = [matrix_of(pieces) for pieces in pieces_in(edges_ref, 2)]
    right = dot(forth_ref[...], right, 1, 0).astype(BF16)
    left_ref[...], right_ref[...] = left, right
    pieces_out([pieces_of(dot(left, right, 1, 1))], mix_ref)
    gating_ref[...] = sigmoid(dot(gate_ref[0], normed_ref[...].astype(BF16), 0, 0))
    flat_ref[...] = block_in(pair_ref).astype(BF16)


def incoming_kernel(edges_ref, back_ref, cot_ref, gating_ref, out_ref, mix_ref, left_ref, right_ref, *side):
    left, right = [matrix_of(pieces) for pieces in pieces_in(edges_ref, 2, (0,))]
    turned = dot(back_ref[...], left, 1, 1).astype(BF16)
    left_ref[...], right_ref[...] = turned, right
    pieces_out([pieces_of(dot(turned, right, 1, 0))], mix_ref)
    before_turn(cot_ref, gating_ref, out_ref, *side)


def incoming_back_kernel(grad_ref, back_ref, left_ref, right_ref, *side):
    *side, grads_ref = side
    grad = matrix_of(pieces_in(grad_ref, 1)[0])
    left_grad = dot(right_ref[...], grad, 1, 1).astype(BF16)
    right_grad = dot(left_ref[...], grad, 0, 0)
    pieces_out([pieces_of(dot(left_grad, back_ref[...], 1, 0)), pieces_of(right_grad)], grads_ref)
    after_turn(*side)


def outgoing_back_kernel(grad_ref, back_ref, left_ref, right_ref, grads_ref):
    grad = matrix_of(pieces_in(grad_ref, 1)[0])
    turned = dot(back_ref[...], grad, 1, 1).astype(BF16)
    pieces_out([pieces_of(dot(grad, right_ref[...], 1, 0)), pieces_of(dot(turned, left_ref[...], 1, 0))], grads_ref)


SINGLE_SHAPE = (DEVICES * SINGLE, LANES)
DOUBLE_SHAPE = (DEVICES * DOUBLE, LANES)
WEIGHTS_SHAPE = (DEVICES * WEIGHTS, LANES)
BLOCK = (ROWS * COLS, CHANNELS)
FLAT = (CHANNELS, TILES * LANES)
KEPT = (4, CHANNELS, TILES * LANES)
LINE = (1, TILES * LANES)
SQUARE = (WIDE, WIDE)
WEIGHT = (CHANNELS, CHANNELS)
PROJ = (CHANNELS, 4 * CHANNELS)
DMA = pltpu.SemaphoreType.DMA


def call(kernel, name, outs, scratch, *operands, far_out=(), flops=None):
    def spec(far):
        return pl.BlockSpec(memory_space=pl.ANY if far else pltpu.VMEM)

    return pl.pallas_call(
        kernel,
        out_shape=[jax.ShapeDtypeStruct(shape, kind) for shape, kind in outs],
        in_specs=[spec(False) for _ in operands],
        out_specs=[spec(position in far_out) for position in range(len(outs))],
        scratch_shapes=scratch,
        cost_estimate=flops and pl.CostEstimate(flops=flops, bytes_accessed=0, transcendentals=0),
        compiler_params=pltpu.CompilerParams(vmem_limit_bytes=24 * 1024 * 1024),
        name=name,
    )(*operands)


def exchange(message):
    rows = message.shape[0] // DEVICES
    shape = (DEVICES, rows, LANES)
    for low in (4, 2):
        if rows % 8 and rows % low == 0:
            shape = (DEVICES, rows // low, low, LANES)
            break
    return lax.all_to_all(message.reshape(shape), AXES, 0, 0, tiled=True).reshape(message.shape)


def local(pair_rep, proj_weight, gate_weight, out_weight, pair_cot):
    pair = pair_rep.reshape(BLOCK)
    cot = pair_cot.reshape(BLOCK)
    double = pltpu.VMEM((DEVICES * DOUBLE + 16, LANES), F32)
    spaced = pltpu.VMEM((DEVICES * (SINGLE + 1) + 16, LANES), F32)
    forth, back = call(orders_kernel, "orders", [(SQUARE, BF16), (SQUARE, BF16)], [], flops=4 * 1024**3)
    edges0, normed0, inverse0, kept0 = call(
        start_kernel, "start", [(DOUBLE_SHAPE, BF16), (FLAT, F32), (LINE, F32), (KEPT, F32)], [double],
        pair, proj_weight, forth,
    )
    mix0, left0, right0, gating0, pair0 = call(
        outgoing_kernel, "outgoing", [(SINGLE_SHAPE, BF16), (SQUARE, BF16), (SQUARE, BF16), (FLAT, F32), (FLAT, BF16)], [],
        exchange(edges0), forth, normed0, gate_weight, pair,
    )
    edges1, mix_normed0, mix_inverse0, product0, after, normed1, inverse1, kept1, gating1 = call(
        middle_kernel, "middle",
        [
            (DOUBLE_SHAPE, BF16), (FLAT, F32), (LINE, F32), (FLAT, F32), (FLAT, BF16), (FLAT, F32),
            (LINE, F32), (KEPT, F32), (FLAT, F32),
        ],
        [spaced, double], exchange(mix0), pair0, gating0, proj_weight, gate_weight, out_weight,
    )
    mix1, left1, right1, cot1, through1, mix_up1 = call(
        incoming_kernel, "incoming",
        [(SINGLE_SHAPE, BF16), (SQUARE, BF16), (SQUARE, BF16), (FLAT, BF16), (FLAT, BF16), (FLAT, F32)], [],
        exchange(edges1), back, cot, gating1, out_weight,
    )
    grad1, normed_mix1 = call(
        turn_kernel, "turn", [(SINGLE_SHAPE, BF16), (FLAT, BF16)], [spaced], exchange(mix1), mix_up1
    )
    pair_out, gate_up1, gate_part1, out_part1, grads1 = call(
        incoming_back_kernel, "incoming_back",
        [(FLAT, BF16), (FLAT, BF16), (WEIGHT, F32), (WEIGHT, F32), (DOUBLE_SHAPE, BF16)], [],
        exchange(grad1), back, left1, right1, normed_mix1, after, gating1, cot1, through1, out_weight, normed1,
    )
    pair_out, grad0, upstream, gate_up0, proj_part1, out_part0 = call(
        back_kernel, "back",
        [(BLOCK, BF16), (SINGLE_SHAPE, BF16), (FLAT, F32), (FLAT, BF16), (PROJ, F32), (WEIGHT, F32)],
        [spaced, double, pltpu.VMEM(BLOCK, BF16), DMA], exchange(grads1), cot1, normed1, inverse1, kept1, gate_up1, mix_normed0, mix_inverse0,
        product0, gating0, proj_weight, gate_weight, out_weight, pair_out, far_out=(0,),
    )
    (grads0,) = call(
        outgoing_back_kernel, "outgoing_back", [(DOUBLE_SHAPE, BF16)], [], exchange(grad0), back, left0, right0
    )
    pair_grad, parts = call(
        last_kernel, "last", [(FLAT, F32), (WEIGHTS_SHAPE, BF16)], [double],
        exchange(grads0), upstream, normed0, inverse0, kept0, gate_up0, proj_weight, gate_weight,
        proj_part1, gate_part1, out_part1, out_part0,
    )
    (sums,) = call(sum_kernel, "sum", [(WEIGHTS_SHAPE, BF16)], [], exchange(parts))
    outs = [((2,) + PROJ, F32), ((2,) + WEIGHT, F32), ((2,) + WEIGHT, F32), (BLOCK, F32)]
    proj_grad, gate_grad, out_grad, pair_grad = call(
        spread_kernel, "spread", outs, [pltpu.VMEM(shape, kind) for shape, kind in outs] + [DMA((4 + TILES,))],
        exchange(sums), pair_grad, far_out=range(4),
    )
    return (
        pair_out.reshape(ROWS, COLS, CHANNELS),
        pair_grad.reshape(ROWS, COLS, CHANNELS),
        proj_grad,
        gate_grad,
        out_grad,
    )


def solution(mesh):
    in_specs = (P("row", "col", None), P(), P(), P(), P("row", "col", None))
    out_specs = (P("row", "col", None), P("row", "col", None), P(), P(), P())
    return jax.shard_map(local, mesh=mesh, in_specs=in_specs, out_specs=out_specs, check_vma=False)
```
